32 devices in a mesh: groups: 2 (over x), docs: 16 (over z, y, core).
Axes of the slice: x: 2, y: 2, z: 4, core: 2. Of those that a mesh axis runs over, the one named last changes fastest.
Arguments:
- sentences: bfloat16 [65536, 1280], P(('groups', 'docs')), parts along dimension 0, may hold values from -10 to 10
- sent_doc: int32 [65536], P('groups'), parts along dimension 0, may hold values from 0 to 2047, never falling along the last dimension, each value on 1 to 32 neighbouring positions
- images: bfloat16 [8192, 1280], P(('groups', 'docs')), parts along dimension 0, may hold values from -30 to 30
- image_owner: int32 [8192, 1], P(('groups', 'docs')), parts along dimension 0, may hold values from 0 to 15, as said below
- anchor: int32 [8192], P(('groups', 'docs')), parts along dimension 0, may hold values from 0 to 2047, as said below
- loader_shard: int32 [8192, 1], P(('groups', 'docs')), parts along dimension 0, may hold values from 0 to 15, as said below
Outputs:
- loaded_images: bfloat16 [16384, 1280], P(('groups', 'docs')), parts along dimension 0
- loaded_text: bfloat16 [16384, 1280], P(('groups', 'docs')), parts along dimension 0
The draws below stay inside these ranges and needn't reach their ends.
There are 2 independent parts, one for each index of `groups`. The reference program is written for one: setup_inputs(seed, part) draws one part's arguments, and reference() takes and returns one part's arrays. A program takes and returns all parts, laid end to end along the dimension named above; each array names one. Nothing has to cross between parts.
Inputs may be any that keep to these rules, and one draw needn't show every extreme that they name: `sent_doc`: documents are runs of 1 to 32 consecutive sentences, ids never falling. `image_owner`: the 256 images of one device name one owner at most 32 times, and some owner exactly 32 times. loader_shard = (a[source device] + b[image_owner]) mod 16 for two permutations a and b of the devices, drawn with the data. So the images of one device name one shard at most 32 times (some exactly 32), and the images that one owner receives from all devices name one shard at most 32 times, all from one source device. `anchor`: the image's document is the document of this sentence of its owner.
All inputs are finite; a program needn't handle non-finite values.
Results may differ from the reference program's by a relative error of at most 0.0048.
Values may be sent and summed in bfloat16 or wider, within the bound.
No kernel may reach another device: no remote copies, remote signals or barrier semaphores. Data moves between devices by JAX's collectives and lax.ppermute only.
A program may use at most 64 MiB of HBM per device.

```python
import math
import jax
import jax.numpy as jnp
import numpy as np
from jax import lax

E = 1280
S_DEV = 2048
I_DEV = 256
MOST_SENT = 32
CAP = 32
SENTS = 32768
IMAGES = 4096
DOCS = 2048
SLOTS = 8192
N_DOCS = 16


def draw_sentences(key, part):
    base = jnp.clip(jax.random.normal(jax.random.fold_in(key, 11), (SENTS, E), jnp.float32), -6.0, 6.0)
    return base.astype(jnp.bfloat16)


def draw_images(key, part):
    base = jnp.clip(jax.random.normal(jax.random.fold_in(key, 13), (IMAGES, E), jnp.float32), -6.0, 6.0)
    return base.astype(jnp.bfloat16)


def draw_anchor(key, part):
    chooser = jax.random.randint(jax.random.fold_in(key, 21), (IMAGES,), 0, 4)
    nearby = jax.random.randint(jax.random.fold_in(key, 23), (IMAGES,), 0, 2 * MOST_SENT)
    edges = jnp.where(nearby < MOST_SENT, nearby, S_DEV - 2 * MOST_SENT + nearby)
    spread = jax.random.randint(jax.random.fold_in(key, 29), (IMAGES,), 0, S_DEV)
    return jnp.where(chooser == 0, edges, spread).astype(jnp.int32)


def route_pair(key):
    base = jax.random.fold_in(key, 31)
    listing = jnp.repeat(jnp.arange(N_DOCS, dtype=jnp.int32), CAP)
    total = N_DOCS * CAP
    leaning = jax.random.randint(jax.random.fold_in(base, 1), (N_DOCS,), 0, 3)
    chosen = jax.random.randint(jax.random.fold_in(base, 2), (N_DOCS,), 0, N_DOCS)
    noise = jax.random.randint(jax.random.fold_in(base, 3), (N_DOCS, total), 0, 4096)
    score = noise + leaning[listing][None, :] * 4096 + 1
    score = jnp.where(listing[None, :] == chosen[:, None], 0, score)
    score = score * total + jnp.arange(total, dtype=jnp.int32)[None, :]
    order = jnp.argsort(score, axis=1)
    owners = listing[order[:, :I_DEV]]
    spot_score = jax.random.randint(jax.random.fold_in(base, 4), (N_DOCS, I_DEV), 0, 4096) * I_DEV + jnp.arange(I_DEV, dtype=jnp.int32)[None, :]
    owners = jnp.take_along_axis(owners, jnp.argsort(spot_score, axis=1), axis=1)
    first_perm = jax.random.permutation(jax.random.fold_in(base, 5), N_DOCS).astype(jnp.int32)
    second_perm = jax.random.permutation(jax.random.fold_in(base, 6), N_DOCS).astype(jnp.int32)
    shards = (first_perm[:, None] + second_perm[owners]) % N_DOCS
    return (owners.reshape(IMAGES, 1).astype(jnp.int32), shards.reshape(IMAGES, 1).astype(jnp.int32))


def draw_image_owner(key, part):
    return route_pair(key)[0]


def draw_loader_shard(key, part):
    return route_pair(key)[1]


def profile(count, total, limit, skew):
    portions = [(1 << 20) // math.isqrt(rank ** skew) + 1 for rank in range(2, count + 1)]
    spare, holding = total - limit - (count - 1), [1] * (count - 1)
    while spare > 0:
        candidates = [i for i in range(count - 1) if holding[i] < limit]
        mass, budget = sum([portions[i] for i in candidates]), spare
        for i in candidates:
            more = min(limit - holding[i], max(1, budget * portions[i] // mass), spare)
            holding[i] = holding[i] + more
            spare = spare - more
    return np.array([limit] + holding)


def ragged(key, number_of, total, most, lean):
    if number_of == 2:
        one = jax.random.randint(key, (), max(1, total - most), min(most, total - 1) + 1)
        return jnp.stack([one, total - one])
    sizes = jnp.asarray(profile(number_of, total, most, lean), jnp.int32)
    pairs = (number_of - 1) // 2
    donor, receiver = sizes[1:1 + 2 * pairs:2], sizes[2:2 + 2 * pairs:2]
    room = jnp.minimum(donor - 1, most - receiver)
    shifted = jax.random.randint(jax.random.fold_in(key, 1), (pairs,), 0, 1 << 20) % (room + 1)
    sizes = sizes.at[1:1 + 2 * pairs:2].set(donor - shifted).at[2:2 + 2 * pairs:2].set(receiver + shifted)
    return sizes[jax.random.permutation(jax.random.fold_in(key, 2), number_of)]


def setup_inputs(seed: int = 0, part: int = 0) -> dict:
    streams_of = jax.random.split(jax.random.key(seed), 7)
    part_splits = jax.random.split(jax.random.fold_in(streams_of[6], part), 7)
    return {
        "sentences": draw_sentences(jax.random.fold_in(jax.random.fold_in(streams_of[6], part), 71), part),
        "sent_doc": jnp.searchsorted(jnp.cumsum(ragged(part_splits[1], DOCS, SENTS, MOST_SENT, 1)), jnp.arange(SENTS), side="right").astype(jnp.int32),
        "images": draw_images(jax.random.fold_in(jax.random.fold_in(streams_of[6], part), 71), part),
        "image_owner": draw_image_owner(jax.random.fold_in(jax.random.fold_in(streams_of[6], part), 71), part),
        "anchor": draw_anchor(jax.random.fold_in(jax.random.fold_in(streams_of[6], part), 71), part),
        "loader_shard": draw_loader_shard(jax.random.fold_in(jax.random.fold_in(streams_of[6], part), 71), part),
    }


def reference(sentences, sent_doc, images, image_owner, anchor, loader_shard):
    temper = E ** -0.5
    reach = MOST_SENT
    padded = jnp.pad(sentences, ((reach, reach), (0, 0)))
    padded_ids = jnp.pad(sent_doc, (reach, reach), constant_values=-1)
    centre = (image_owner[:, 0] * S_DEV + anchor).astype(jnp.int32)
    doc_ids = sent_doc[centre]
    offsets = jnp.arange(2 * reach + 1, dtype=jnp.int32)

    def align_block(pieces):
        queries, middle, owned = pieces
        indices = middle[:, None] + offsets[None, :]
        window = padded[indices].astype(jnp.float32)
        window_ids = padded_ids[indices]
        scores = jnp.einsum("be,bwe->bw", queries.astype(jnp.float32), window) * temper
        member = window_ids == owned[:, None]
        peak = jnp.max(jnp.where(member, scores, -1e30), axis=1, keepdims=True)
        raised = jnp.where(member, jnp.exp(scores - peak), 0.0)
        denominator = jnp.sum(raised, axis=1, keepdims=True)
        weights = (raised / denominator).astype(jnp.bfloat16)
        return jnp.einsum("bw,bwe->be", weights.astype(jnp.float32), window).astype(jnp.bfloat16)

    aligned = lax.map(align_block, (images.reshape(N_DOCS, I_DEV, E), centre.reshape(N_DOCS, I_DEV), doc_ids.reshape(N_DOCS, I_DEV)))
    aligned = aligned.reshape(IMAGES, E)
    targets = loader_shard[:, 0]
    sources = jnp.arange(IMAGES, dtype=jnp.int32) // I_DEV
    labels = jnp.arange(N_DOCS, dtype=jnp.int32)
    onehot = (targets[:, None] == labels[None, :]).astype(jnp.int32).reshape(N_DOCS, I_DEV, N_DOCS)
    ranking = jnp.sum((jnp.cumsum(onehot, axis=1) - 1) * onehot, axis=2).reshape(IMAGES)
    places = (targets * (N_DOCS * CAP) + sources * CAP + ranking).astype(jnp.int32)
    loaded_images = jnp.zeros((SLOTS, E), jnp.bfloat16).at[places].set(images)
    loaded_text = jnp.zeros((SLOTS, E), jnp.bfloat16).at[places].set(aligned)
    return loaded_images, loaded_text
```

```python
import functools

import jax
import jax.numpy as jnp
from jax import lax
from jax.experimental import pallas as pl
from jax.experimental.pallas import tpu as pltpu
from jax.sharding import PartitionSpec as P

MOST_SENT = 32


def halo_of(sentences):
    peers = lax.axis_size("docs")
    up = [(i, i + 1) for i in range(peers - 1)]
    down = [(j, i) for i, j in up]
    before = lax.ppermute(sentences[-MOST_SENT:], "docs", up)
    after = lax.ppermute(sentences[:MOST_SENT], "docs", down)
    return before, after


def attend_kernel(temper, q_ref, doc_ref, k_ref, before_ref, after_ref, id_ref, id_before_ref, id_after_ref, o_ref):
    q = q_ref[...]
    doc = doc_ref[...]
    parts = ((k_ref, id_ref), (before_ref, id_before_ref), (after_ref, id_after_ref))
    scores = []
    for rows, ids in parts:
        s = lax.dot_general(q, rows[...], (((1,), (1,)), ((), ())), preferred_element_type=jnp.float32) * temper
        scores.append(jnp.where(doc == ids[...], s, -1e30))
    peak = functools.reduce(jnp.maximum, [jnp.max(s, axis=1, keepdims=True) for s in scores])
    raised = [jnp.where(doc == ids[...], jnp.exp(s - peak), 0.0) for s, (_, ids) in zip(scores, parts)]
    total = sum(jnp.sum(r, axis=1, keepdims=True) for r in raised)
    total = jnp.where(total > 0.0, total, 1.0)
    o_ref[...] = sum(
        jnp.dot((r / total).astype(jnp.bfloat16), rows[...], preferred_element_type=jnp.float32)
        for r, (rows, _) in zip(raised, parts)
    ).astype(jnp.bfloat16)


def attend(queries, docs, sentences, before, after, ids, id_before, id_after):
    rows, feature = queries.shape
    own = sentences.shape[0]
    block = min(128, rows)
    whole = lambda a: pl.BlockSpec(a.shape, lambda i: (0, 0))
    fixed = (sentences, before, after, ids, id_before, id_after)
    return pl.pallas_call(
        functools.partial(attend_kernel, feature**-0.5),
        grid=(rows // block,),
        in_specs=[
            pl.BlockSpec((block, feature), lambda i: (i, 0)),
            pl.BlockSpec((block, 1), lambda i: (i, 0)),
            *[whole(a) for a in fixed],
        ],
        out_specs=pl.BlockSpec((block, feature), lambda i: (i, 0)),
        out_shape=jax.ShapeDtypeStruct((rows, feature), jnp.bfloat16),
        compiler_params=pltpu.CompilerParams(vmem_limit_bytes=40 * 1024 * 1024),
        cost_estimate=pl.CostEstimate(
            flops=4 * rows * own * feature, bytes_accessed=2 * (own + 2 * rows) * feature, transcendentals=rows * own
        ),
        name="attend",
    )(queries, docs, *fixed)


def exchange(x):
    return lax.all_to_all(x, "docs", split_axis=0, concat_axis=0, tiled=True)


def shards(sentences, sent_doc, images, image_owner, anchor, loader_shard):
    members = lax.axis_size("docs")
    me = lax.axis_index("docs")
    own, feature = sentences.shape
    n = images.shape[0]
    cap = max(4, 2 * n // members)
    owner, shard = image_owner[:, 0], loader_shard[:, 0]

    packed = (owner * members + shard) * own + anchor
    every = lax.all_gather(packed, "docs", axis=0, tiled=False)

    spot = jnp.arange(n, dtype=jnp.int32)
    earlier = (owner[:, None] == owner[None, :]) & (spot[None, :] < spot[:, None])
    rank = jnp.sum(earlier.astype(jnp.int32), axis=1)
    slot = jnp.arange(members * cap, dtype=jnp.int32)[:, None]

    def buckets(targets):
        table = (slot == (targets * cap + rank)[None, :]).astype(jnp.bfloat16)
        out = jnp.dot(table, images, preferred_element_type=jnp.float32).astype(jnp.bfloat16)
        return out.reshape(members, cap, feature)

    queries = exchange(buckets(owner)).reshape(members * cap, feature)
    loaded_images = exchange(buckets(shard)).reshape(members * cap, feature)
    before, after = halo_of(sentences)

    spot_of = every % own
    shard_of = every // own % members
    owner_of = every // (own * members)
    mine = owner_of == me
    sooner = (spot[:, None] < spot[None, :]).astype(jnp.bfloat16)
    place = jnp.dot(mine.astype(jnp.bfloat16), sooner, preferred_element_type=jnp.float32).astype(jnp.int32)
    slots = jnp.arange(cap, dtype=jnp.int32)
    hit = mine[:, None, :] & (place[:, None, :] == slots[None, :, None])
    spots = jnp.sum(jnp.where(hit, spot_of[:, None, :] + 1, 0), axis=2).reshape(members * cap) - 1
    docs = jnp.where(spots >= 0, sent_doc[me * own + jnp.maximum(spots, 0)], -2)
    ids = lax.dynamic_slice_in_dim(sent_doc, me * own, own)
    padded = jnp.pad(sent_doc, (MOST_SENT, MOST_SENT), constant_values=-1)
    id_before = lax.dynamic_slice_in_dim(padded, me * own, MOST_SENT)
    id_after = lax.dynamic_slice_in_dim(padded, me * own + own + MOST_SENT, MOST_SENT)
    aligned = attend(queries, docs[:, None], sentences, before, after, ids[None], id_before[None], id_after[None])

    goes = jnp.max(jnp.where(mine, shard_of + 1, 0), axis=1) - 1
    comes = jnp.max(jnp.where(shard_of == me, owner_of + 1, 0), axis=1) - 1

    def move(target, source, rows):
        to, frm = target[:, None], source[None, :]
        table = ((to // cap == frm[..., 0]) & (to % cap == frm[..., 1])).astype(jnp.bfloat16)
        return jnp.dot(table, rows, preferred_element_type=jnp.float32).astype(jnp.bfloat16)

    row = jnp.arange(members * cap, dtype=jnp.int32)
    from_block = jnp.stack([jnp.repeat(goes, cap), row % cap], axis=-1)
    sent = move(row, from_block, aligned).reshape(members, cap, feature)
    got = exchange(sent).reshape(members * cap, feature)
    takes = (jnp.repeat(comes, cap) * cap + row % cap)[:, None] == row[None, :]
    takes = (takes & (jnp.repeat(comes, cap) >= 0)[:, None]).astype(jnp.bfloat16)
    loaded_text = jnp.dot(takes, got, preferred_element_type=jnp.float32).astype(jnp.bfloat16)
    return loaded_images, loaded_text


def solution(mesh):
    split = P(("groups", "docs"))
    rows = P(("groups", "docs"), None)
    return jax.shard_map(
        shards,
        mesh=mesh,
        in_specs=(rows, P("groups"), rows, rows, split, rows),
        out_specs=(rows, rows),
        check_vma=False,
    )
```

```python
import functools

import jax
import jax.numpy as jnp
from jax import lax
from jax.experimental import pallas as pl
from jax.experimental.pallas import tpu as pltpu
from jax.sharding import PartitionSpec as P

MOST_SENT = 32


def halo_of(sentences):
    peers = lax.axis_size("docs")
    up = [(i, i + 1) for i in range(peers - 1)]
    down = [(j, i) for i, j in up]
    before = lax.ppermute(sentences[-MOST_SENT:], "docs", up)
    after = lax.ppermute(sentences[:MOST_SENT], "docs", down)
    return before, after


def attend_kernel(temper, q_ref, doc_ref, k_ref, before_ref, after_ref, id_ref, id_before_ref, id_after_ref, o_ref):
    q = q_ref[...]
    doc = doc_ref[...]
    parts = ((k_ref, id_ref), (before_ref, id_before_ref), (after_ref, id_after_ref))
    scores = []
    for rows, ids in parts:
        s = lax.dot_general(q, rows[...], (((1,), (1,)), ((), ())), preferred_element_type=jnp.float32) * temper
        scores.append(jnp.where(doc == ids[...], s, -1e30))
    peak = functools.reduce(jnp.maximum, [jnp.max(s, axis=1, keepdims=True) for s in scores])
    raised = [jnp.where(doc == ids[...], jnp.exp(s - peak), 0.0) for s, (_, ids) in zip(scores, parts)]
    total = sum(jnp.sum(r, axis=1, keepdims=True) for r in raised)
    total = jnp.where(total > 0.0, total, 1.0)
    o_ref[...] = sum(
        jnp.dot((r / total).astype(jnp.bfloat16), rows[...], preferred_element_type=jnp.float32)
        for r, (rows, _) in zip(raised, parts)
    ).astype(jnp.bfloat16)


def attend(queries, docs, sentences, before, after, ids, id_before, id_after):
    rows, feature = queries.shape
    own = sentences.shape[0]
    block = min(128, rows)
    whole = lambda a: pl.BlockSpec(a.shape, lambda i: (0, 0))
    fixed = (sentences, before, after, ids, id_before, id_after)
    return pl.pallas_call(
        functools.partial(attend_kernel, feature**-0.5),
        grid=(rows // block,),
        in_specs=[
            pl.BlockSpec((block, feature), lambda i: (i, 0)),
            pl.BlockSpec((block, 1), lambda i: (i, 0)),
            *[whole(a) for a in fixed],
        ],
        out_specs=pl.BlockSpec((block, feature), lambda i: (i, 0)),
        out_shape=jax.ShapeDtypeStruct((rows, feature), jnp.bfloat16),
        compiler_params=pltpu.CompilerParams(vmem_limit_bytes=40 * 1024 * 1024),
        cost_estimate=pl.CostEstimate(
            flops=4 * rows * own * feature, bytes_accessed=2 * (own + 2 * rows) * feature, transcendentals=rows * own
        ),
        name="attend",
    )(queries, docs, *fixed)


def every_device(row):
    peers, me = lax.axis_size("docs"), lax.axis_index("docs")
    if peers & (peers - 1):
        return lax.all_gather(row, "docs", axis=0, tiled=False)
    held, step = row[None], 1
    while step < peers:
        held = jnp.concatenate([held, lax.ppermute(held, "docs", [(i, i ^ step) for i in range(peers)])], axis=0)
        step *= 2
    label = jnp.arange(peers, dtype=jnp.int32)
    pick = (label ^ me)[:, None] == label[None, :]
    return jnp.sum(jnp.where(pick[:, :, None], held[None], 0), axis=1)


def copy_kernel(x_ref, o_ref):
    o_ref[...] = x_ref[...]


def write_out(x):
    rows, feature = x.shape
    block = min(128, rows)
    spec = pl.BlockSpec((block, feature), lambda i: (i, 0))
    return pl.pallas_call(
        copy_kernel,
        grid=(rows // block,),
        in_specs=[spec],
        out_specs=spec,
        out_shape=jax.ShapeDtypeStruct(x.shape, x.dtype),
        cost_estimate=pl.CostEstimate(flops=0, bytes_accessed=4 * rows * feature, transcendentals=0),
        name="write_out",
    )(x)


def exchange(x):
    return lax.all_to_all(x, "docs", split_axis=0, concat_axis=0, tiled=True)


def shards(sentences, sent_doc, images, image_owner, anchor, loader_shard):
    members = lax.axis_size("docs")
    me = lax.axis_index("docs")
    own, feature = sentences.shape
    n = images.shape[0]
    cap = max(4, 2 * n // members)
    owner, shard = image_owner[:, 0], loader_shard[:, 0]

    packed = (owner * members + shard) * own + anchor
    every = every_device(packed)

    spot = jnp.arange(n, dtype=jnp.int32)
    earlier = (owner[:, None] == owner[None, :]) & (spot[None, :] < spot[:, None])
    rank = jnp.sum(earlier.astype(jnp.int32), axis=1)
    slot = jnp.arange(members * cap, dtype=jnp.int32)[:, None]

    def buckets(targets):
        table = (slot == (targets * cap + rank)[None, :]).astype(jnp.bfloat16)
        out = jnp.dot(table, images, preferred_element_type=jnp.float32).astype(jnp.bfloat16)
        return out.reshape(members, cap, feature)

    queries = exchange(buckets(owner)).reshape(members * cap, feature)
    loaded_images = write_out(exchange(buckets(shard)).reshape(members * cap, feature))
    before, after = halo_of(sentences)

    spot_of = every % own
    shard_of = every // own % members
    owner_of = every // (own * members)
    mine = owner_of == me
    sooner = (spot[:, None] < spot[None, :]).astype(jnp.bfloat16)
    place = jnp.dot(mine.astype(jnp.bfloat16), sooner, preferred_element_type=jnp.float32).astype(jnp.int32)
    slots = jnp.arange(cap, dtype=jnp.int32)
    hit = mine[:, None, :] & (place[:, None, :] == slots[None, :, None])
    spots = jnp.sum(jnp.where(hit, spot_of[:, None, :] + 1, 0), axis=2).reshape(members * cap) - 1
    docs = jnp.where(spots >= 0, sent_doc[me * own + jnp.maximum(spots, 0)], -2)
    ids = lax.dynamic_slice_in_dim(sent_doc, me * own, own)
    padded = jnp.pad(sent_doc, (MOST_SENT, MOST_SENT), constant_values=-1)
    id_before = lax.dynamic_slice_in_dim(padded, me * own, MOST_SENT)
    id_after = lax.dynamic_slice_in_dim(padded, me * own + own + MOST_SENT, MOST_SENT)
    aligned = attend(queries, docs[:, None], sentences, before, after, ids[None], id_before[None], id_after[None])

    goes = jnp.max(jnp.where(mine, shard_of + 1, 0), axis=1) - 1
    comes = jnp.max(jnp.where(shard_of == me, owner_of + 1, 0), axis=1) - 1

    row = jnp.arange(members * cap, dtype=jnp.int32)
    puts = row[:, None] == (jnp.repeat(goes, cap) * cap + row % cap)[None, :]
    puts = (puts & (jnp.repeat(goes, cap) >= 0)[None, :]).astype(jnp.bfloat16)
    sent = jnp.dot(puts, aligned, preferred_element_type=jnp.float32).astype(jnp.bfloat16).reshape(members, cap, feature)
    got = exchange(sent).reshape(members * cap, feature)
    takes = (jnp.repeat(comes, cap) * cap + row % cap)[:, None] == row[None, :]
    takes = (takes & (jnp.repeat(comes, cap) >= 0)[:, None]).astype(jnp.bfloat16)
    loaded_text = jnp.dot(takes, got, preferred_element_type=jnp.float32).astype(jnp.bfloat16)
    return loaded_images, loaded_text


def solution(mesh):
    split = P(("groups", "docs"))
    rows = P(("groups", "docs"), None)
    return jax.shard_map(
        shards,
        mesh=mesh,
        in_specs=(rows, P("groups"), rows, rows, split, rows),
        out_specs=(rows, rows),
        check_vma=False,
    )
```

```python
import functools

import jax
import jax.numpy as jnp
from jax import lax
from jax.experimental import pallas as pl
from jax.experimental.pallas import tpu as pltpu
from jax.sharding import PartitionSpec as P

MOST_SENT = 32
TILE = 16


def halo_of(sentences):
    peers = lax.axis_size("docs")
    up = [(i, i + 1) for i in range(peers - 1)]
    down = [(j, i) for i, j in up]
    before = lax.ppermute(sentences[-MOST_SENT:], "docs", up)
    after = lax.ppermute(sentences[:MOST_SENT], "docs", down)
    return before, after


def every_device(row, order):
    peers, me = lax.axis_size("docs"), lax.axis_index("docs")
    half = peers // 2
    if peers & (peers - 1):
        held = lax.all_gather(row, "docs", axis=0, tiled=False)
        mirror = lax.ppermute(row, "docs", [(i, (i + half) % peers) for i in range(peers)])
        source = jnp.arange(peers, dtype=jnp.int32)
    else:
        held, apart, step = row[None], [0], half
        while step:
            held = jnp.concatenate([held, lax.ppermute(held, "docs", [(i, i ^ step) for i in range(peers)])], axis=0)
            apart += [a ^ step for a in apart]
            mirror = held[1] if step == half else mirror
            step //= 2
        source = jnp.array(apart, jnp.int32) ^ me
    pick = order[:, None] == source[None, :]
    return jnp.sum(jnp.where(pick[:, :, None], held[None], 0), axis=1), mirror


def one_hot_dot(table, rows):
    return jnp.dot(table.astype(jnp.bfloat16), rows, preferred_element_type=jnp.float32).astype(jnp.bfloat16)


class Arriving:
    def __init__(self, source, held, sems):
        length = source.shape[0] // sems.shape[0]
        self.spans = [pl.ds(i * length, length) for i in range(sems.shape[0])]
        self.held = held
        self.copies = [pltpu.make_async_copy(source.at[s], held.at[s], sems.at[i]) for i, s in enumerate(self.spans)]
        for c in self.copies:
            c.start()

    def parts(self, ids):
        return [(self.held.at[s], ids.at[:, s], c.wait) for s, c in zip(self.spans, self.copies)]


def softmax_rows(temper, q, doc, parts):
    scores = []
    for rows, ids, ready in parts:
        ready()
        s = lax.dot_general(q, rows[...], (((1,), (1,)), ((), ())), preferred_element_type=jnp.float32) * temper
        scores.append(jnp.where(doc == ids[...], s, -1e30))
    peak = functools.reduce(jnp.maximum, [jnp.max(s, axis=1, keepdims=True) for s in scores])
    raised = [jnp.where(doc == ids[...], jnp.exp(s - peak), 0.0) for s, (_, ids, _) in zip(scores, parts)]
    total = sum(jnp.sum(r, axis=1, keepdims=True) for r in raised)
    total = jnp.where(total > 0.0, total, 1.0)
    return sum(
        jnp.dot((r / total).astype(jnp.bfloat16), rows[...], preferred_element_type=jnp.float32)
        for r, (rows, _, _) in zip(raised, parts)
    ).astype(jnp.bfloat16)


def attended(temper, count, q_ref, doc_ref, k, before_ref, after_ref, id_ref, id_before_ref, id_after_ref):
    q = q_ref[:, :count].reshape(doc_ref.shape[0], -1)
    here = lambda: None
    parts = [*k.parts(id_ref), (before_ref, id_before_ref, here), (after_ref, id_after_ref, here)]
    return softmax_rows(temper, q, doc_ref[...], parts)


def attend_kernel(temper, count, q_ref, doc_ref, k_ref, *rest):
    *known, o_ref, held, k_sem = rest
    k = Arriving(k_ref, held, k_sem)
    o_ref[...] = attended(temper, count, q_ref, doc_ref, k, *known)


def attend_route_kernel(temper, count, goes_ref, taken_ref, q_ref, doc_ref, k_ref, *rest):
    *known, own_ref, o_ref, held, out, zero, k_sem, own_sem, out_sem, zero_sem = rest
    half, members = q_ref.shape[0], o_ref.shape[0]
    k = Arriving(k_ref, held, k_sem)
    zero[...] = jnp.zeros_like(zero)
    block = lambda j: pl.ds(j * count, count)
    place = lambda j: jnp.maximum(goes_ref[j], 0)
    owns = [pltpu.make_async_copy(own_ref.at[block(j)], o_ref.at[place(j)], own_sem.at[j]) for j in range(half)]
    outs = [pltpu.make_async_copy(out.at[block(j)], o_ref.at[place(half + j)], out_sem.at[j]) for j in range(half)]
    zeros = [pltpu.make_async_copy(zero, o_ref.at[d], zero_sem.at[d]) for d in range(members)]
    for j in range(half):
        pl.when(goes_ref[j] >= 0)(owns[j].start)
    for d in range(members):
        pl.when(taken_ref[d] < 0)(zeros[d].start)
    out[...] = attended(temper, count, q_ref, doc_ref, k, *known)
    for j in range(half):
        pl.when(goes_ref[half + j] >= 0)(outs[j].start)
    for j in range(half):
        pl.when(goes_ref[j] >= 0)(owns[j].wait)
    for d in range(members):
        pl.when(taken_ref[d] < 0)(zeros[d].wait)
    for j in range(half):
        pl.when(goes_ref[half + j] >= 0)(outs[j].wait)


VMEM, SMEM, ANY, HBM = (pl.BlockSpec(memory_space=m) for m in (pltpu.VMEM, pltpu.SMEM, pl.ANY, pltpu.HBM))


def attend(queries, cap, docs, known, own=None, goes=None):
    blocks, _, feature = queries.shape
    rows = blocks * cap
    if cap % TILE:
        queries = queries[:, :cap].reshape(1, rows, feature)
    routed = own is not None and cap % TILE == 0
    count = queries.shape[1] if cap % TILE else cap
    length = known[0].shape[0]
    chunks = 4
    args = (queries, docs[:, None], *known)
    specs = [VMEM, VMEM, HBM] + [VMEM] * (len(known) - 1)
    held, dma = pltpu.VMEM((length, feature), jnp.bfloat16), pltpu.SemaphoreType.DMA
    if routed:
        taken = jnp.max(jnp.where(goes[None, :] == jnp.arange(2 * blocks)[:, None], 1, -1), axis=1)
        args, specs = (goes, taken, *args, own), [SMEM, SMEM, *specs, ANY]
        shape = (2 * blocks, cap, feature)
        scratch = [
            held,
            pltpu.VMEM((rows, feature), jnp.bfloat16),
            pltpu.VMEM((cap, feature), jnp.bfloat16),
            dma((chunks,)),
            dma((blocks,)),
            dma((blocks,)),
            dma((2 * blocks,)),
        ]
    else:
        shape = (rows, feature)
        scratch = [held, dma((chunks,))]
    out = pl.pallas_call(
        functools.partial(attend_route_kernel if routed else attend_kernel, feature**-0.5, count),
        in_specs=specs,
        out_specs=HBM if routed else pl.BlockSpec(),
        out_shape=jax.ShapeDtypeStruct(shape, jnp.bfloat16),
        scratch_shapes=scratch,
        compiler_params=pltpu.CompilerParams(vmem_limit_bytes=59 * 1024 * 1024),
        cost_estimate=pl.CostEstimate(
            flops=4 * rows * length * feature, bytes_accessed=2 * (length + 2 * rows) * feature, transcendentals=rows * length
        ),
        name="attend_route" if routed else "attend",
    )(*args)
    if own is None or routed:
        return out
    both = jnp.concatenate([own, out])
    row = jnp.arange(2 * rows, dtype=jnp.int32)
    block = jnp.repeat(goes, cap)
    puts = (row[:, None] == (block * cap + row % cap)[None, :]) & (block >= 0)[None, :]
    return one_hot_dot(puts, both).reshape(2 * blocks, cap, feature)


def place_kernel(comes_ref, x_ref, o_ref, zero, sem):
    zero[...] = jnp.zeros_like(zero)
    members = x_ref.shape[0]
    moves = [pltpu.make_async_copy(x_ref.at[jnp.maximum(comes_ref[d], 0)], o_ref.at[d], sem.at[d]) for d in range(members)]
    clears = [pltpu.make_async_copy(zero, o_ref.at[d], sem.at[d]) for d in range(members)]
    for d in range(members):
        pl.when(comes_ref[d] >= 0)(moves[d].start)
        pl.when(comes_ref[d] < 0)(clears[d].start)
    for d in range(members):
        pl.when(comes_ref[d] >= 0)(moves[d].wait)
        pl.when(comes_ref[d] < 0)(clears[d].wait)


def place(x, comes):
    members, cap, feature = x.shape
    if cap % TILE:
        row = jnp.arange(members * cap, dtype=jnp.int32)
        block = jnp.repeat(comes, cap)
        takes = ((block * cap + row % cap)[:, None] == row[None, :]) & (block >= 0)[:, None]
        return one_hot_dot(takes, x.reshape(members * cap, feature))
    return pl.pallas_call(
        place_kernel,
        in_specs=[SMEM, ANY],
        out_specs=ANY,
        out_shape=jax.ShapeDtypeStruct(x.shape, x.dtype),
        scratch_shapes=[pltpu.VMEM((cap, feature), x.dtype), pltpu.SemaphoreType.DMA((members,))],
        cost_estimate=pl.CostEstimate(flops=0, bytes_accessed=4 * x.size, transcendentals=0),
        name="place",
    )(comes, x).reshape(members * cap, feature)


def shards(sentences, sent_doc, images, image_owner, anchor, loader_shard):
    members = lax.axis_size("docs")
    me = lax.axis_index("docs")
    own, feature = sentences.shape
    n = images.shape[0]
    cap = max(4, 2 * n // members)
    half = members // 2
    first = me // half * half
    halves = [list(range(half)), list(range(half, members))]

    mirrored = lax.ppermute(images, "docs", [(i, (i + half) % members) for i in range(members)])
    packed = (image_owner[:, 0] * members + loader_shard[:, 0]) * own + anchor
    order = (first + jnp.arange(members, dtype=jnp.int32)) % members
    every, packed_mirror = every_device(packed, order)
    before, after = halo_of(sentences)

    spot = jnp.arange(n, dtype=jnp.int32)

    def deal(rows, codes):
        owner, shard = codes // (own * members), codes // own % members
        earlier = (owner[:, None] == owner[None, :]) & (spot[None, :] < spot[:, None])
        rank = jnp.sum(earlier.astype(jnp.int32), axis=1)
        slot = jnp.arange(half * 2 * cap, dtype=jnp.int32)[:, None]
        owned = (owner - first) * (2 * cap) + rank
        loads = (shard - first) * (2 * cap) + cap + rank
        table = (slot == owned[None, :]) & (owner // half * half == first)[None, :]
        table |= (slot == loads[None, :]) & (shard // half * half == first)[None, :]
        out = one_hot_dot(table, rows).reshape(half, 2 * cap, feature)
        return lax.all_to_all(out, "docs", split_axis=0, concat_axis=0, tiled=True, axis_index_groups=halves)

    near = deal(images, packed)
    far = deal(mirrored, packed_mirror)

    spot_of, shard_of, owner_of = every % own, every // own % members, every // (own * members)
    mine = owner_of == me
    sooner = (spot[:, None] < spot[None, :]).astype(jnp.bfloat16)
    ranks = jnp.dot(mine.astype(jnp.bfloat16), sooner, preferred_element_type=jnp.float32).astype(jnp.int32)
    slots = jnp.arange(cap, dtype=jnp.int32)
    hit = mine[:, None, :] & (ranks[:, None, :] == slots[None, :, None])
    spots = jnp.sum(jnp.where(hit, spot_of[:, None, :] + 1, 0), axis=2).reshape(members * cap) - 1
    docs = jnp.where(spots >= 0, sent_doc[me * own + jnp.maximum(spots, 0)], -2)
    ids = lax.dynamic_slice_in_dim(sent_doc, me * own, own)
    padded = jnp.pad(sent_doc, (MOST_SENT, MOST_SENT), constant_values=-1)
    id_before = lax.dynamic_slice_in_dim(padded, me * own, MOST_SENT)
    id_after = lax.dynamic_slice_in_dim(padded, me * own + own + MOST_SENT, MOST_SENT)
    known = (sentences, before, after, ids[None], id_before[None], id_after[None])

    goes = jnp.max(jnp.where(mine, shard_of + 1, 0), axis=1) - 1
    comes = jnp.roll(jnp.max(jnp.where(shard_of == me, owner_of + 1, 0), axis=1) - 1, first)

    aligned_near = attend(near, cap, docs[: half * cap], known)
    sent = attend(far, cap, docs[half * cap :], known, aligned_near, goes)
    got = lax.all_to_all(sent, "docs", split_axis=0, concat_axis=0, tiled=True)

    low = first == 0
    near_images, far_images = near[:, cap:], far[:, cap:]
    loaded_images = jnp.concatenate(
        [jnp.where(low, near_images, far_images), jnp.where(low, far_images, near_images)]
    ).reshape(members * cap, feature)
    loaded_text = place(got, comes)
    return loaded_images, loaded_text


def solution(mesh):
    split = P(("groups", "docs"))
    rows = P(("groups", "docs"), None)
    return jax.shard_map(
        shards,
        mesh=mesh,
        in_specs=(rows, P("groups"), rows, rows, split, rows),
        out_specs=(rows, rows),
        check_vma=False,
    )
```

```python
import functools

import jax
import jax.numpy as jnp
from jax import lax
from jax.experimental import pallas as pl
from jax.experimental.pallas import tpu as pltpu
from jax.sharding import PartitionSpec as P

MOST_SENT = 32
TILE = 16
VMEM, SMEM, HBM = (pl.BlockSpec(memory_space=m) for m in (pltpu.VMEM, pltpu.SMEM, pltpu.HBM))


def halo_of(sentences):
    peers = lax.axis_size("docs")
    up = [(i, i + 1) for i in range(peers - 1)]
    down = [(j, i) for i, j in up]
    before = lax.ppermute(sentences[-MOST_SENT:], "docs", up)
    after = lax.ppermute(sentences[:MOST_SENT], "docs", down)
    return before, after


def attend_kernel(temper, q_ref, doc_ref, k_ref, before_ref, after_ref, id_ref, id_before_ref, id_after_ref, o_ref):
    q = q_ref[...]
    doc = doc_ref[...]
    parts = ((k_ref, id_ref), (before_ref, id_before_ref), (after_ref, id_after_ref))
    scores = []
    for rows, ids in parts:
        s = lax.dot_general(q, rows[...], (((1,), (1,)), ((), ())), preferred_element_type=jnp.float32) * temper
        scores.append(jnp.where(doc == ids[...], s, -1e30))
    peak = functools.reduce(jnp.maximum, [jnp.max(s, axis=1, keepdims=True) for s in scores])
    raised = [jnp.where(doc == ids[...], jnp.exp(s - peak), 0.0) for s, (_, ids) in zip(scores, parts)]
    total = sum(jnp.sum(r, axis=1, keepdims=True) for r in raised)
    total = jnp.where(total > 0.0, total, 1.0)
    o_ref[...] = sum(
        jnp.dot((r / total).astype(jnp.bfloat16), rows[...], preferred_element_type=jnp.float32)
        for r, (rows, _) in zip(raised, parts)
    ).astype(jnp.bfloat16)


def attend(queries, docs, sentences, before, after, ids, id_before, id_after):
    rows, feature = queries.shape
    own = sentences.shape[0]
    block = min(256, rows)
    whole = lambda a: pl.BlockSpec(a.shape, lambda i: (0, 0))
    fixed = (sentences, before, after, ids, id_before, id_after)
    return pl.pallas_call(
        functools.partial(attend_kernel, feature**-0.5),
        grid=(rows // block,),
        in_specs=[
            pl.BlockSpec((block, feature), lambda i: (i, 0)),
            pl.BlockSpec((block, 1), lambda i: (i, 0)),
            *[whole(a) for a in fixed],
        ],
        out_specs=pl.BlockSpec((block, feature), lambda i: (i, 0)),
        out_shape=jax.ShapeDtypeStruct((rows, feature), jnp.bfloat16),
        compiler_params=pltpu.CompilerParams(vmem_limit_bytes=40 * 1024 * 1024),
        cost_estimate=pl.CostEstimate(
            flops=4 * rows * own * feature, bytes_accessed=2 * (own + 2 * rows) * feature, transcendentals=rows * own
        ),
        name="attend",
    )(queries, docs, *fixed)


def every_device(row, late):
    peers, me = lax.axis_size("docs"), lax.axis_index("docs")
    if peers & (peers - 1):
        return lax.all_gather(row, "docs", axis=0, tiled=False), late
    held, step = row[None], 1
    while step < peers:
        if 2 * step == peers:
            held, late = lax.optimization_barrier((held, late))
        held = jnp.concatenate([held, lax.ppermute(held, "docs", [(i, i ^ step) for i in range(peers)])], axis=0)
        step *= 2
    label = jnp.arange(peers, dtype=jnp.int32)
    pick = (label ^ me)[:, None] == label[None, :]
    return jnp.sum(jnp.where(pick[:, :, None], held[None], 0), axis=1), late


def copy_kernel(x_ref, o_ref):
    o_ref[...] = x_ref[...]


def write_out(x):
    rows, feature = x.shape
    block = min(128, rows)
    spec = pl.BlockSpec((block, feature), lambda i: (i, 0))
    return pl.pallas_call(
        copy_kernel,
        grid=(rows // block,),
        in_specs=[spec],
        out_specs=spec,
        out_shape=jax.ShapeDtypeStruct(x.shape, x.dtype),
        compiler_params=pltpu.CompilerParams(vmem_limit_bytes=8 * 1024 * 1024),
        cost_estimate=pl.CostEstimate(flops=0, bytes_accessed=4 * rows * feature, transcendentals=0),
        name="write_out",
    )(x)


def exchange(x):
    return lax.all_to_all(x, "docs", split_axis=0, concat_axis=0, tiled=True)


def place_kernel(comes_ref, x_ref, o_ref, zero, sem):
    zero[...] = jnp.zeros_like(zero)
    members = x_ref.shape[0]
    moves = [pltpu.make_async_copy(x_ref.at[jnp.maximum(comes_ref[d], 0)], o_ref.at[d], sem.at[d]) for d in range(members)]
    clears = [pltpu.make_async_copy(zero, o_ref.at[d], sem.at[d]) for d in range(members)]
    for d in range(members):
        pl.when(comes_ref[d] >= 0)(moves[d].start)
        pl.when(comes_ref[d] < 0)(clears[d].start)
    for d in range(members):
        pl.when(comes_ref[d] >= 0)(moves[d].wait)
        pl.when(comes_ref[d] < 0)(clears[d].wait)


def place(x, comes):
    members, cap, feature = x.shape
    if cap % TILE:
        row = jnp.arange(members * cap, dtype=jnp.int32)
        block = jnp.repeat(comes, cap)
        takes = ((block * cap + row % cap)[:, None] == row[None, :]) & (block >= 0)[:, None]
        table = takes.astype(jnp.bfloat16)
        rows = x.reshape(members * cap, feature)
        return jnp.dot(table, rows, preferred_element_type=jnp.float32).astype(jnp.bfloat16)
    return pl.pallas_call(
        place_kernel,
        in_specs=[SMEM, VMEM],
        out_specs=HBM,
        out_shape=jax.ShapeDtypeStruct(x.shape, x.dtype),
        scratch_shapes=[pltpu.VMEM((cap, feature), x.dtype), pltpu.SemaphoreType.DMA((members,))],
        compiler_params=pltpu.CompilerParams(vmem_limit_bytes=8 * 1024 * 1024),
        cost_estimate=pl.CostEstimate(flops=0, bytes_accessed=4 * x.size, transcendentals=0),
        name="place",
    )(comes, x).reshape(members * cap, feature)


def shards(sentences, sent_doc, images, image_owner, anchor, loader_shard):
    members = lax.axis_size("docs")
    me = lax.axis_index("docs")
    own, feature = sentences.shape
    n = images.shape[0]
    cap = max(4, 2 * n // members)
    owner, shard = image_owner[:, 0], loader_shard[:, 0]

    packed = (owner * members + shard) * own + anchor

    spot = jnp.arange(n, dtype=jnp.int32)
    earlier = (owner[:, None] == owner[None, :]) & (spot[None, :] < spot[:, None])
    rank = jnp.sum(earlier.astype(jnp.int32), axis=1)
    slot = jnp.arange(members * cap, dtype=jnp.int32)[:, None]

    def buckets(targets):
        table = (slot == (targets * cap + rank)[None, :]).astype(jnp.bfloat16)
        out = jnp.dot(table, images, preferred_element_type=jnp.float32).astype(jnp.bfloat16)
        return out.reshape(members, cap, feature)

    every, arrived = every_device(packed, exchange(buckets(owner)))
    queries = arrived.reshape(members * cap, feature)
    loaded_images = write_out(exchange(buckets(shard)).reshape(members * cap, feature))
    before, after = halo_of(sentences)

    spot_of = every % own
    shard_of = every // own % members
    owner_of = every // (own * members)
    mine = owner_of == me
    sooner = (spot[:, None] < spot[None, :]).astype(jnp.bfloat16)
    ranks = jnp.dot(mine.astype(jnp.bfloat16), sooner, preferred_element_type=jnp.float32).astype(jnp.int32)
    slots = jnp.arange(cap, dtype=jnp.int32)
    hit = mine[:, None, :] & (ranks[:, None, :] == slots[None, :, None])
    spots = jnp.sum(jnp.where(hit, spot_of[:, None, :] + 1, 0), axis=2).reshape(members * cap) - 1
    ids = lax.dynamic_slice_in_dim(sent_doc, me * own, own)
    here = spots[:, None] == jnp.arange(own, dtype=jnp.int32)[None, :]
    docs = jnp.max(jnp.where(here, ids[None, :], -2), axis=1)
    padded = jnp.pad(sent_doc, (MOST_SENT, MOST_SENT), constant_values=-1)
    id_before = lax.dynamic_slice_in_dim(padded, me * own, MOST_SENT)
    id_after = lax.dynamic_slice_in_dim(padded, me * own + own + MOST_SENT, MOST_SENT)
    aligned = attend(queries, docs[:, None], sentences, before, after, ids[None], id_before[None], id_after[None])

    goes = jnp.max(jnp.where(mine, shard_of + 1, 0), axis=1) - 1
    comes = jnp.max(jnp.where(shard_of == me, owner_of + 1, 0), axis=1) - 1

    row = jnp.arange(members * cap, dtype=jnp.int32)
    puts = row[:, None] == (jnp.repeat(goes, cap) * cap + row % cap)[None, :]
    puts = (puts & (jnp.repeat(goes, cap) >= 0)[None, :]).astype(jnp.bfloat16)
    sent = jnp.dot(puts, aligned, preferred_element_type=jnp.float32).astype(jnp.bfloat16).reshape(members, cap, feature)
    loaded_text = place(exchange(sent), comes)
    return loaded_images, loaded_text


def solution(mesh):
    split = P(("groups", "docs"))
    rows = P(("groups", "docs"), None)
    return jax.shard_map(
        shards,
        mesh=mesh,
        in_specs=(rows, P("groups"), rows, rows, split, rows),
        out_specs=(rows, rows),
        check_vma=False,
    )
```

```python
import functools

import jax
import jax.numpy as jnp
from jax import lax
from jax.experimental import pallas as pl
from jax.experimental.pallas import tpu as pltpu
from jax.sharding import PartitionSpec as P

MOST_SENT = 32
TILE = 16
VMEM, SMEM, HBM = (pl.BlockSpec(memory_space=m) for m in (pltpu.VMEM, pltpu.SMEM, pltpu.HBM))


def halo_of(sentences):
    peers = lax.axis_size("docs")
    up = [(i, i + 1) for i in range(peers - 1)]
    down = [(j, i) for i, j in up]
    before = lax.ppermute(sentences[-MOST_SENT:], "docs", up)
    after = lax.ppermute(sentences[:MOST_SENT], "docs", down)
    return before, after


def attend_kernel(temper, q_ref, doc_ref, k_ref, before_ref, after_ref, id_ref, id_before_ref, id_after_ref, o_ref):
    q = q_ref[...]
    doc = doc_ref[...]
    parts = ((k_ref, id_ref), (before_ref, id_before_ref), (after_ref, id_after_ref))
    scores = []
    for rows, ids in parts:
        s = lax.dot_general(q, rows[...], (((1,), (1,)), ((), ())), preferred_element_type=jnp.float32) * temper
        scores.append(jnp.where(doc == ids[...], s, -1e30))
    peak = functools.reduce(jnp.maximum, [jnp.max(s, axis=1, keepdims=True) for s in scores])
    raised = [jnp.where(doc == ids[...], jnp.exp(s - peak), 0.0) for s, (_, ids) in zip(scores, parts)]
    total = sum(jnp.sum(r, axis=1, keepdims=True) for r in raised)
    total = jnp.where(total > 0.0, total, 1.0)
    o_ref[...] = sum(
        jnp.dot((r / total).astype(jnp.bfloat16), rows[...], preferred_element_type=jnp.float32)
        for r, (rows, _) in zip(raised, parts)
    ).astype(jnp.bfloat16)


def attend(queries, docs, sentences, before, after, ids, id_before, id_after):
    rows, feature = queries.shape
    own = sentences.shape[0]
    block = min(256, rows)
    whole = lambda a: pl.BlockSpec(a.shape, lambda i: (0, 0))
    fixed = (sentences, before, after, ids, id_before, id_after)
    return pl.pallas_call(
        functools.partial(attend_kernel, feature**-0.5),
        grid=(rows // block,),
        in_specs=[
            pl.BlockSpec((block, feature), lambda i: (i, 0)),
            pl.BlockSpec((block, 1), lambda i: (i, 0)),
            *[whole(a) for a in fixed],
        ],
        out_specs=pl.BlockSpec((block, feature), lambda i: (i, 0)),
        out_shape=jax.ShapeDtypeStruct((rows, feature), jnp.bfloat16),
        compiler_params=pltpu.CompilerParams(vmem_limit_bytes=40 * 1024 * 1024),
        cost_estimate=pl.CostEstimate(
            flops=4 * rows * own * feature, bytes_accessed=2 * (own + 2 * rows) * feature, transcendentals=rows * own
        ),
        name="attend",
    )(queries, docs, *fixed)


def every_device(row, after):
    peers, me = lax.axis_size("docs"), lax.axis_index("docs")
    if peers & (peers - 1):
        return lax.all_gather(row, "docs", axis=0, tiled=False), after
    step = max(1, peers // 4)
    apart = list(range(0, peers, step))
    rows = [lax.ppermute(row, "docs", [(i, i ^ a) for i in range(peers)]) if a else row for a in apart]
    held, after = lax.optimization_barrier((jnp.stack(rows), after))
    while step > 1:
        step //= 2
        held = jnp.concatenate([held, lax.ppermute(held, "docs", [(i, i ^ step) for i in range(peers)])], axis=0)
        apart = apart + [a ^ step for a in apart]
    source = jnp.array(apart, dtype=jnp.int32) ^ me
    pick = jnp.arange(peers, dtype=jnp.int32)[:, None] == source[None, :]
    return jnp.sum(jnp.where(pick[:, :, None], held[None], 0), axis=1), after


def copy_kernel(x_ref, o_ref):
    o_ref[...] = x_ref[...]


def write_out(x):
    rows, feature = x.shape
    block = min(128, rows)
    spec = pl.BlockSpec((block, feature), lambda i: (i, 0))
    return pl.pallas_call(
        copy_kernel,
        grid=(rows // block,),
        in_specs=[spec],
        out_specs=spec,
        out_shape=jax.ShapeDtypeStruct(x.shape, x.dtype),
        compiler_params=pltpu.CompilerParams(vmem_limit_bytes=8 * 1024 * 1024),
        cost_estimate=pl.CostEstimate(flops=0, bytes_accessed=4 * rows * feature, transcendentals=0),
        name="write_out",
    )(x)


def exchange(x):
    return lax.all_to_all(x, "docs", split_axis=0, concat_axis=0, tiled=True)


def place_kernel(comes_ref, x_ref, o_ref, zero, sem):
    zero[...] = jnp.zeros_like(zero)
    members = x_ref.shape[0]
    moves = [pltpu.make_async_copy(x_ref.at[jnp.maximum(comes_ref[d], 0)], o_ref.at[d], sem.at[d]) for d in range(members)]
    clears = [pltpu.make_async_copy(zero, o_ref.at[d], sem.at[d]) for d in range(members)]
    for d in range(members):
        pl.when(comes_ref[d] >= 0)(moves[d].start)
        pl.when(comes_ref[d] < 0)(clears[d].start)
    for d in range(members):
        pl.when(comes_ref[d] >= 0)(moves[d].wait)
        pl.when(comes_ref[d] < 0)(clears[d].wait)


def place(x, comes):
    members, cap, feature = x.shape
    if cap % TILE:
        row = jnp.arange(members * cap, dtype=jnp.int32)
        block = jnp.repeat(comes, cap)
        takes = ((block * cap + row % cap)[:, None] == row[None, :]) & (block >= 0)[:, None]
        table = takes.astype(jnp.bfloat16)
        rows = x.reshape(members * cap, feature)
        return jnp.dot(table, rows, preferred_element_type=jnp.float32).astype(jnp.bfloat16)
    return pl.pallas_call(
        place_kernel,
        in_specs=[SMEM, VMEM],
        out_specs=HBM,
        out_shape=jax.ShapeDtypeStruct(x.shape, x.dtype),
        scratch_shapes=[pltpu.VMEM((cap, feature), x.dtype), pltpu.SemaphoreType.DMA((members,))],
        compiler_params=pltpu.CompilerParams(vmem_limit_bytes=8 * 1024 * 1024),
        cost_estimate=pl.CostEstimate(flops=0, bytes_accessed=4 * x.size, transcendentals=0),
        name="place",
    )(comes, x).reshape(members * cap, feature)


def shards(sentences, sent_doc, images, image_owner, anchor, loader_shard):
    members = lax.axis_size("docs")
    me = lax.axis_index("docs")
    own, feature = sentences.shape
    n = images.shape[0]
    cap = max(4, 2 * n // members)
    owner, shard = image_owner[:, 0], loader_shard[:, 0]

    packed = (owner * members + shard) * own + anchor

    spot = jnp.arange(n, dtype=jnp.int32)
    earlier = (owner[:, None] == owner[None, :]) & (spot[None, :] < spot[:, None])
    rank = jnp.sum(earlier.astype(jnp.int32), axis=1)
    slot = jnp.arange(members * cap, dtype=jnp.int32)[:, None]

    def buckets(targets):
        table = (slot == (targets * cap + rank)[None, :]).astype(jnp.bfloat16)
        out = jnp.dot(table, images, preferred_element_type=jnp.float32).astype(jnp.bfloat16)
        return out.reshape(members, cap, feature)

    every, leaving = every_device(packed, buckets(owner))
    queries = exchange(leaving).reshape(members * cap, feature)
    loaded_images = write_out(exchange(buckets(shard)).reshape(members * cap, feature))
    before, after = halo_of(sentences)

    spot_of = every % own
    shard_of = every // own % members
    owner_of = every // (own * members)
    mine = owner_of == me
    sooner = (spot[:, None] < spot[None, :]).astype(jnp.bfloat16)
    ranks = jnp.dot(mine.astype(jnp.bfloat16), sooner, preferred_element_type=jnp.float32).astype(jnp.int32)
    slots = jnp.arange(cap, dtype=jnp.int32)
    hit = mine[:, None, :] & (ranks[:, None, :] == slots[None, :, None])
    spots = jnp.sum(jnp.where(hit, spot_of[:, None, :] + 1, 0), axis=2).reshape(members * cap) - 1
    ids = lax.dynamic_slice_in_dim(sent_doc, me * own, own)
    here = spots[:, None] == jnp.arange(own, dtype=jnp.int32)[None, :]
    docs = jnp.max(jnp.where(here, ids[None, :], -2), axis=1)
    padded = jnp.pad(sent_doc, (MOST_SENT, MOST_SENT), constant_values=-1)
    id_before = lax.dynamic_slice_in_dim(padded, me * own, MOST_SENT)
    id_after = lax.dynamic_slice_in_dim(padded, me * own + own + MOST_SENT, MOST_SENT)
    aligned = attend(queries, docs[:, None], sentences, before, after, ids[None], id_before[None], id_after[None])

    goes = jnp.max(jnp.where(mine, shard_of + 1, 0), axis=1) - 1
    comes = jnp.max(jnp.where(shard_of == me, owner_of + 1, 0), axis=1) - 1

    row = jnp.arange(members * cap, dtype=jnp.int32)
    puts = row[:, None] == (jnp.repeat(goes, cap) * cap + row % cap)[None, :]
    puts = (puts & (jnp.repeat(goes, cap) >= 0)[None, :]).astype(jnp.bfloat16)
    sent = jnp.dot(puts, aligned, preferred_element_type=jnp.float32).astype(jnp.bfloat16).reshape(members, cap, feature)
    loaded_text = place(exchange(sent), comes)
    return loaded_images, loaded_text


def solution(mesh):
    split = P(("groups", "docs"))
    rows = P(("groups", "docs"), None)
    return jax.shard_map(
        shards,
        mesh=mesh,
        in_specs=(rows, P("groups"), rows, rows, split, rows),
        out_specs=(rows, rows),
        check_vma=False,
    )
```

```python
import functools

import jax
import jax.numpy as jnp
from jax import lax
from jax.experimental import pallas as pl
from jax.experimental.pallas import tpu as pltpu
from jax.sharding import PartitionSpec as P

MOST_SENT = 32
TILE = 16
VMEM, SMEM, HBM = (pl.BlockSpec(memory_space=m) for m in (pltpu.VMEM, pltpu.SMEM, pltpu.HBM))


def halo_of(sentences):
    peers = lax.axis_size("docs")
    up = [(i, i + 1) for i in range(peers - 1)]
    down = [(j, i) for i, j in up]
    before = lax.ppermute(sentences[-MOST_SENT:], "docs", up)
    after = lax.ppermute(sentences[:MOST_SENT], "docs", down)
    return before, after


def attend_kernel(temper, q_ref, doc_ref, k_ref, before_ref, after_ref, id_ref, id_before_ref, id_after_ref, o_ref):
    q = q_ref[...]
    doc = doc_ref[...]
    parts = ((k_ref, id_ref), (before_ref, id_before_ref), (after_ref, id_after_ref))
    scores = []
    for rows, ids in parts:
        s = lax.dot_general(q, rows[...], (((1,), (1,)), ((), ())), preferred_element_type=jnp.float32) * temper
        scores.append(jnp.where(doc == ids[...], s, -1e30))
    peak = functools.reduce(jnp.maximum, [jnp.max(s, axis=1, keepdims=True) for s in scores])
    raised = [jnp.where(doc == ids[...], jnp.exp(s - peak), 0.0) for s, (_, ids) in zip(scores, parts)]
    total = sum(jnp.sum(r, axis=1, keepdims=True) for r in raised)
    total = jnp.where(total > 0.0, total, 1.0)
    o_ref[...] = sum(
        jnp.dot((r / total).astype(jnp.bfloat16), rows[...], preferred_element_type=jnp.float32)
        for r, (rows, _) in zip(raised, parts)
    ).astype(jnp.bfloat16)


def attend(queries, docs, sentences, before, after, ids, id_before, id_after):
    rows, feature = queries.shape
    own = sentences.shape[0]
    block = min(256, rows)
    whole = lambda a: pl.BlockSpec(a.shape, lambda i: (0, 0))
    fixed = (sentences, before, after, ids, id_before, id_after)
    return pl.pallas_call(
        functools.partial(attend_kernel, feature**-0.5),
        grid=(rows // block,),
        in_specs=[
            pl.BlockSpec((block, feature), lambda i: (i, 0)),
            pl.BlockSpec((block, 1), lambda i: (i, 0)),
            *[whole(a) for a in fixed],
        ],
        out_specs=pl.BlockSpec((block, feature), lambda i: (i, 0)),
        out_shape=jax.ShapeDtypeStruct((rows, feature), jnp.bfloat16),
        compiler_params=pltpu.CompilerParams(vmem_limit_bytes=40 * 1024 * 1024),
        cost_estimate=pl.CostEstimate(
            flops=4 * rows * own * feature, bytes_accessed=2 * (own + 2 * rows) * feature, transcendentals=rows * own
        ),
        name="attend",
    )(queries, docs, *fixed)


def every_device(row, after):
    peers, me = lax.axis_size("docs"), lax.axis_index("docs")
    if peers & (peers - 1):
        return lax.all_gather(row, "docs", axis=0, tiled=False), after
    step = peers // 2
    held, after = lax.optimization_barrier((row[None], after))
    apart = [0]
    while step:
        held = jnp.concatenate([held, lax.ppermute(held, "docs", [(i, i ^ step) for i in range(peers)])], axis=0)
        if len(apart) == 1:
            held, after = lax.optimization_barrier((held, after))
        apart = apart + [a ^ step for a in apart]
        step //= 2
    source = jnp.array(apart, dtype=jnp.int32) ^ me
    pick = jnp.arange(peers, dtype=jnp.int32)[:, None] == source[None, :]
    return jnp.sum(jnp.where(pick[:, :, None], held[None], 0), axis=1), after


def copy_kernel(x_ref, o_ref):
    o_ref[...] = x_ref[...]


def write_out(x):
    rows, feature = x.shape
    block = min(128, rows)
    spec = pl.BlockSpec((block, feature), lambda i: (i, 0))
    return pl.pallas_call(
        copy_kernel,
        grid=(rows // block,),
        in_specs=[spec],
        out_specs=spec,
        out_shape=jax.ShapeDtypeStruct(x.shape, x.dtype),
        compiler_params=pltpu.CompilerParams(vmem_limit_bytes=8 * 1024 * 1024),
        cost_estimate=pl.CostEstimate(flops=0, bytes_accessed=4 * rows * feature, transcendentals=0),
        name="write_out",
    )(x)


def exchange(x):
    return lax.all_to_all(x, "docs", split_axis=0, concat_axis=0, tiled=True)


def place_kernel(comes_ref, x_ref, o_ref, zero, sem):
    zero[...] = jnp.zeros_like(zero)
    members = x_ref.shape[0]
    moves = [pltpu.make_async_copy(x_ref.at[jnp.maximum(comes_ref[d], 0)], o_ref.at[d], sem.at[d]) for d in range(members)]
    clears = [pltpu.make_async_copy(zero, o_ref.at[d], sem.at[d]) for d in range(members)]
    for d in range(members):
        pl.when(comes_ref[d] >= 0)(moves[d].start)
        pl.when(comes_ref[d] < 0)(clears[d].start)
    for d in range(members):
        pl.when(comes_ref[d] >= 0)(moves[d].wait)
        pl.when(comes_ref[d] < 0)(clears[d].wait)


def place(x, comes):
    members, cap, feature = x.shape
    if cap % TILE:
        row = jnp.arange(members * cap, dtype=jnp.int32)
        block = jnp.repeat(comes, cap)
        takes = ((block * cap + row % cap)[:, None] == row[None, :]) & (block >= 0)[:, None]
        table = takes.astype(jnp.bfloat16)
        rows = x.reshape(members * cap, feature)
        return jnp.dot(table, rows, preferred_element_type=jnp.float32).astype(jnp.bfloat16)
    return pl.pallas_call(
        place_kernel,
        in_specs=[SMEM, VMEM],
        out_specs=HBM,
        out_shape=jax.ShapeDtypeStruct(x.shape, x.dtype),
        scratch_shapes=[pltpu.VMEM((cap, feature), x.dtype), pltpu.SemaphoreType.DMA((members,))],
        compiler_params=pltpu.CompilerParams(vmem_limit_bytes=8 * 1024 * 1024),
        cost_estimate=pl.CostEstimate(flops=0, bytes_accessed=4 * x.size, transcendentals=0),
        name="place",
    )(comes, x).reshape(members * cap, feature)


def shards(sentences, sent_doc, images, image_owner, anchor, loader_shard):
    members = lax.axis_size("docs")
    me = lax.axis_index("docs")
    own, feature = sentences.shape
    n = images.shape[0]
    cap = max(4, 2 * n // members)
    owner, shard = image_owner[:, 0], loader_shard[:, 0]

    packed = (owner * members + shard) * own + anchor

    spot = jnp.arange(n, dtype=jnp.int32)
    earlier = (owner[:, None] == owner[None, :]) & (spot[None, :] < spot[:, None])
    rank = jnp.sum(earlier.astype(jnp.int32), axis=1)
    slot = jnp.arange(members * cap, dtype=jnp.int32)[:, None]

    def buckets(targets):
        table = (slot == (targets * cap + rank)[None, :]).astype(jnp.bfloat16)
        out = jnp.dot(table, images, preferred_element_type=jnp.float32).astype(jnp.bfloat16)
        return out.reshape(members, cap, feature)

    every, leaving = every_device(packed, buckets(owner))
    queries = exchange(leaving).reshape(members * cap, feature)
    loaded_images = write_out(exchange(buckets(shard)).reshape(members * cap, feature))
    before, after = halo_of(sentences)

    spot_of = every % own
    shard_of = every // own % members
    owner_of = every // (own * members)
    mine = owner_of == me
    sooner = (spot[:, None] < spot[None, :]).astype(jnp.bfloat16)
    ranks = jnp.dot(mine.astype(jnp.bfloat16), sooner, preferred_element_type=jnp.float32).astype(jnp.int32)
    slots = jnp.arange(cap, dtype=jnp.int32)
    hit = mine[:, None, :] & (ranks[:, None, :] == slots[None, :, None])
    spots = jnp.sum(jnp.where(hit, spot_of[:, None, :] + 1, 0), axis=2).reshape(members * cap) - 1
    ids = lax.dynamic_slice_in_dim(sent_doc, me * own, own)
    here = spots[:, None] == jnp.arange(own, dtype=jnp.int32)[None, :]
    docs = jnp.max(jnp.where(here, ids[None, :], -2), axis=1)
    padded = jnp.pad(sent_doc, (MOST_SENT, MOST_SENT), constant_values=-1)
    id_before = lax.dynamic_slice_in_dim(padded, me * own, MOST_SENT)
    id_after = lax.dynamic_slice_in_dim(padded, me * own + own + MOST_SENT, MOST_SENT)
    aligned = attend(queries, docs[:, None], sentences, before, after, ids[None], id_before[None], id_after[None])

    goes = jnp.max(jnp.where(mine, shard_of + 1, 0), axis=1) - 1
    comes = jnp.max(jnp.where(shard_of == me, owner_of + 1, 0), axis=1) - 1

    row = jnp.arange(members * cap, dtype=jnp.int32)
    puts = row[:, None] == (jnp.repeat(goes, cap) * cap + row % cap)[None, :]
    puts = (puts & (jnp.repeat(goes, cap) >= 0)[None, :]).astype(jnp.bfloat16)
    sent = jnp.dot(puts, aligned, preferred_element_type=jnp.float32).astype(jnp.bfloat16).reshape(members, cap, feature)
    loaded_text = place(exchange(sent), comes)
    return loaded_images, loaded_text


def solution(mesh):
    split = P(("groups", "docs"))
    rows = P(("groups", "docs"), None)
    return jax.shard_map(
        shards,
        mesh=mesh,
        in_specs=(rows, P("groups"), rows, rows, split, rows),
        out_specs=(rows, rows),
        check_vma=False,
    )
```

```python
import functools

import jax
import jax.numpy as jnp
from jax import lax
from jax.experimental import pallas as pl
from jax.experimental.pallas import tpu as pltpu
from jax.sharding import PartitionSpec as P

MOST_SENT = 32
TILE = 16
VMEM, SMEM, HBM = (pl.BlockSpec(memory_space=m) for m in (pltpu.VMEM, pltpu.SMEM, pltpu.HBM))


def halo_of(sentences):
    peers = lax.axis_size("docs")
    up = [(i, i + 1) for i in range(peers - 1)]
    down = [(j, i) for i, j in up]
    before = lax.ppermute(sentences[-MOST_SENT:], "docs", up)
    after = lax.ppermute(sentences[:MOST_SENT], "docs", down)
    return before, after


def attend_kernel(temper, q_ref, doc_ref, k_ref, before_ref, after_ref, id_ref, id_before_ref, id_after_ref, o_ref):
    q = q_ref[...]
    doc = doc_ref[...]
    parts = ((k_ref, id_ref), (before_ref, id_before_ref), (after_ref, id_after_ref))
    scores = []
    for rows, ids in parts:
        s = lax.dot_general(q, rows[...], (((1,), (1,)), ((), ())), preferred_element_type=jnp.float32) * temper
        scores.append(jnp.where(doc == ids[...], s, -1e30))
    peak = functools.reduce(jnp.maximum, [jnp.max(s, axis=1, keepdims=True) for s in scores])
    raised = [jnp.where(doc == ids[...], jnp.exp(s - peak), 0.0) for s, (_, ids) in zip(scores, parts)]
    total = sum(jnp.sum(r, axis=1, keepdims=True) for r in raised)
    total = jnp.where(total > 0.0, total, 1.0)
    o_ref[...] = sum(
        jnp.dot((r / total).astype(jnp.bfloat16), rows[...], preferred_element_type=jnp.float32)
        for r, (rows, _) in zip(raised, parts)
    ).astype(jnp.bfloat16)


def attend(queries, docs, sentences, before, after, ids, id_before, id_after):
    rows, feature = queries.shape
    own = sentences.shape[0]
    block = min(256, rows)
    whole = lambda a: pl.BlockSpec(a.shape, lambda i: (0, 0))
    fixed = (sentences, before, after, ids, id_before, id_after)
    return pl.pallas_call(
        functools.partial(attend_kernel, feature**-0.5),
        grid=(rows // block,),
        in_specs=[
            pl.BlockSpec((block, feature), lambda i: (i, 0)),
            pl.BlockSpec((block, 1), lambda i: (i, 0)),
            *[whole(a) for a in fixed],
        ],
        out_specs=pl.BlockSpec((block, feature), lambda i: (i, 0)),
        out_shape=jax.ShapeDtypeStruct((rows, feature), jnp.bfloat16),
        compiler_params=pltpu.CompilerParams(vmem_limit_bytes=40 * 1024 * 1024),
        cost_estimate=pl.CostEstimate(
            flops=4 * rows * own * feature, bytes_accessed=2 * (own + 2 * rows) * feature, transcendentals=rows * own
        ),
        name="attend",
    )(queries, docs, *fixed)


def every_device(row, arrived):
    peers, me = lax.axis_size("docs"), lax.axis_index("docs")
    if peers & (peers - 1):
        return lax.all_gather(row, "docs", axis=0, tiled=False), arrived
    step = max(1, peers // 4)
    apart = list(range(0, peers, step))
    rows = [lax.ppermute(row, "docs", [(i, i ^ a) for i in range(peers)]) if a else row for a in apart]
    held, arrived = lax.optimization_barrier((jnp.stack(rows), arrived))
    while step > 1:
        step //= 2
        held = jnp.concatenate([held, lax.ppermute(held, "docs", [(i, i ^ step) for i in range(peers)])], axis=0)
        apart = apart + [a ^ step for a in apart]
    source = jnp.array(apart, dtype=jnp.int32) ^ me
    pick = jnp.arange(peers, dtype=jnp.int32)[:, None] == source[None, :]
    return jnp.sum(jnp.where(pick[:, :, None], held[None], 0), axis=1), arrived


def copy_kernel(x_ref, o_ref):
    o_ref[...] = x_ref[...]


def write_out(x):
    rows, feature = x.shape
    block = min(128, rows)
    spec = pl.BlockSpec((block, feature), lambda i: (i, 0))
    return pl.pallas_call(
        copy_kernel,
        grid=(rows // block,),
        in_specs=[spec],
        out_specs=spec,
        out_shape=jax.ShapeDtypeStruct(x.shape, x.dtype),
        compiler_params=pltpu.CompilerParams(vmem_limit_bytes=8 * 1024 * 1024),
        cost_estimate=pl.CostEstimate(flops=0, bytes_accessed=4 * rows * feature, transcendentals=0),
        name="write_out",
    )(x)


def exchange(x):
    return lax.all_to_all(x, "docs", split_axis=0, concat_axis=0, tiled=True)


def place_kernel(comes_ref, x_ref, o_ref, zero, sem):
    zero[...] = jnp.zeros_like(zero)
    members = x_ref.shape[0]
    moves = [pltpu.make_async_copy(x_ref.at[jnp.maximum(comes_ref[d], 0)], o_ref.at[d], sem.at[d]) for d in range(members)]
    clears = [pltpu.make_async_copy(zero, o_ref.at[d], sem.at[d]) for d in range(members)]
    for d in range(members):
        pl.when(comes_ref[d] >= 0)(moves[d].start)
        pl.when(comes_ref[d] < 0)(clears[d].start)
    for d in range(members):
        pl.when(comes_ref[d] >= 0)(moves[d].wait)
        pl.when(comes_ref[d] < 0)(clears[d].wait)


def place(x, comes):
    members, cap, feature = x.shape
    if cap % TILE:
        row = jnp.arange(members * cap, dtype=jnp.int32)
        block = jnp.repeat(comes, cap)
        takes = ((block * cap + row % cap)[:, None] == row[None, :]) & (block >= 0)[:, None]
        table = takes.astype(jnp.bfloat16)
        rows = x.reshape(members * cap, feature)
        return jnp.dot(table, rows, preferred_element_type=jnp.float32).astype(jnp.bfloat16)
    return pl.pallas_call(
        place_kernel,
        in_specs=[SMEM, VMEM],
        out_specs=HBM,
        out_shape=jax.ShapeDtypeStruct(x.shape, x.dtype),
        scratch_shapes=[pltpu.VMEM((cap, feature), x.dtype), pltpu.SemaphoreType.DMA((members,))],
        compiler_params=pltpu.CompilerParams(vmem_limit_bytes=8 * 1024 * 1024),
        cost_estimate=pl.CostEstimate(flops=0, bytes_accessed=4 * x.size, transcendentals=0),
        name="place",
    )(comes, x).reshape(members * cap, feature)


def shards(sentences, sent_doc, images, image_owner, anchor, loader_shard):
    members = lax.axis_size("docs")
    me = lax.axis_index("docs")
    own, feature = sentences.shape
    n = images.shape[0]
    cap = max(4, 2 * n // members)
    owner, shard = image_owner[:, 0], loader_shard[:, 0]

    packed = (owner * members + shard) * own + anchor

    spot = jnp.arange(n, dtype=jnp.int32)
    earlier = (owner[:, None] == owner[None, :]) & (spot[None, :] < spot[:, None])
    rank = jnp.sum(earlier.astype(jnp.int32), axis=1)
    slot = jnp.arange(members * cap, dtype=jnp.int32)[:, None]

    def buckets(targets):
        table = (slot == (targets * cap + rank)[None, :]).astype(jnp.bfloat16)
        out = jnp.dot(table, images, preferred_element_type=jnp.float32).astype(jnp.bfloat16)
        return out.reshape(members, cap, feature)

    every, arrived = every_device(packed, exchange(buckets(owner)))
    queries = arrived.reshape(members * cap, feature)
    loaded_images = write_out(exchange(buckets(shard)).reshape(members * cap, feature))
    before, after = halo_of(sentences)

    spot_of = every % own
    shard_of = every // own % members
    owner_of = every // (own * members)
    mine = owner_of == me
    sooner = (spot[:, None] < spot[None, :]).astype(jnp.bfloat16)
    ranks = jnp.dot(mine.astype(jnp.bfloat16), sooner, preferred_element_type=jnp.float32).astype(jnp.int32)
    slots = jnp.arange(cap, dtype=jnp.int32)
    hit = mine[:, None, :] & (ranks[:, None, :] == slots[None, :, None])
    spots = jnp.sum(jnp.where(hit, spot_of[:, None, :] + 1, 0), axis=2).reshape(members * cap) - 1
    ids = lax.dynamic_slice_in_dim(sent_doc, me * own, own)
    here = spots[:, None] == jnp.arange(own, dtype=jnp.int32)[None, :]
    docs = jnp.max(jnp.where(here, ids[None, :], -2), axis=1)
    padded = jnp.pad(sent_doc, (MOST_SENT, MOST_SENT), constant_values=-1)
    id_before = lax.dynamic_slice_in_dim(padded, me * own, MOST_SENT)
    id_after = lax.dynamic_slice_in_dim(padded, me * own + own + MOST_SENT, MOST_SENT)
    aligned = attend(queries, docs[:, None], sentences, before, after, ids[None], id_before[None], id_after[None])

    goes = jnp.max(jnp.where(mine, shard_of + 1, 0), axis=1) - 1
    comes = jnp.max(jnp.where(shard_of == me, owner_of + 1, 0), axis=1) - 1

    row = jnp.arange(members * cap, dtype=jnp.int32)
    puts = row[:, None] == (jnp.repeat(goes, cap) * cap + row % cap)[None, :]
    puts = (puts & (jnp.repeat(goes, cap) >= 0)[None, :]).astype(jnp.bfloat16)
    sent = jnp.dot(puts, aligned, preferred_element_type=jnp.float32).astype(jnp.bfloat16).reshape(members, cap, feature)
    loaded_text = place(exchange(sent), comes)
    return loaded_images, loaded_text


def solution(mesh):
    split = P(("groups", "docs"))
    rows = P(("groups", "docs"), None)
    return jax.shard_map(
        shards,
        mesh=mesh,
        in_specs=(rows, P("groups"), rows, rows, split, rows),
        out_specs=(rows, rows),
        check_vma=False,
    )
```

```python
import functools

import jax
import jax.numpy as jnp
from jax import lax
from jax.experimental import pallas as pl
from jax.experimental.pallas import tpu as pltpu
from jax.sharding import PartitionSpec as P

MOST_SENT = 32
TILE = 16
LANES = 128
VMEM, SMEM, HBM = (pl.BlockSpec(memory_space=m) for m in (pltpu.VMEM, pltpu.SMEM, pltpu.HBM))


def halo_of(sentences):
    peers = lax.axis_size("docs")
    up = [(i, i + 1) for i in range(peers - 1)]
    down = [(j, i) for i, j in up]
    before = lax.ppermute(sentences[-MOST_SENT:], "docs", up)
    after = lax.ppermute(sentences[:MOST_SENT], "docs", down)
    return before, after


def deal_kernel(cap, owner_ref, shard_ref, anchor_ref, rows_ref, o_ref):
    members = o_ref.shape[0]
    lines, n = owner_ref.shape[0], rows_ref.shape[0]
    owner, shard, anchor = owner_ref[...], shard_ref[...], anchor_ref[...]
    told = jnp.concatenate([owner, shard, anchor // LANES, anchor % LANES], axis=0)
    told = jnp.concatenate([told, jnp.zeros((TILE - 4 * lines, LANES), jnp.int32)], axis=0)
    told = told.astype(jnp.float32).astype(jnp.bfloat16)
    owner = jnp.concatenate([owner[i : i + 1] for i in range(lines)], axis=1)
    label = lax.broadcasted_iota(jnp.int32, (members, n), 0)
    theirs = jnp.where(label == owner, 1.0, 0.0)
    sooner = lax.broadcasted_iota(jnp.int32, (n, n), 0) < lax.broadcasted_iota(jnp.int32, (n, n), 1)
    before = jnp.dot(
        theirs.astype(jnp.bfloat16), jnp.where(sooner, 1.0, 0.0).astype(jnp.bfloat16), preferred_element_type=jnp.float32
    )
    rank = jnp.sum(theirs * before, axis=0, keepdims=True).astype(jnp.int32)
    slot = lax.broadcasted_iota(jnp.int32, (members * cap, n), 0)
    table = jnp.where(slot == owner * cap + rank, 1.0, 0.0).astype(jnp.bfloat16)
    out = jnp.dot(table, rows_ref[...], preferred_element_type=jnp.float32).astype(jnp.bfloat16)
    for d in range(members):
        for t, r, c in tiles(cap, out.shape[1]):
            o_ref[d, t : t + TILE] = out[d * cap + r : d * cap + r + TILE, c : c + LANES]
        o_ref[d, cap * out.shape[1] // LANES :] = told


def tiles(rows, columns):
    every = [(r, c) for r in range(0, rows, TILE) for c in range(0, columns, LANES)]
    return [(i * TILE, r, c) for i, (r, c) in enumerate(every)]


def deal(images, owner, shard, anchor, members, cap):
    n, feature = images.shape
    lines = lambda a: a.reshape(n // LANES, LANES)
    shape = (members, cap * feature // LANES + TILE, LANES)
    return pl.pallas_call(
        functools.partial(deal_kernel, cap),
        in_specs=[pl.BlockSpec()] * 4,
        out_specs=pl.BlockSpec(),
        out_shape=jax.ShapeDtypeStruct(shape, jnp.bfloat16),
        compiler_params=pltpu.CompilerParams(vmem_limit_bytes=60 * 1024 * 1024),
        cost_estimate=pl.CostEstimate(
            flops=2 * members * cap * n * feature, bytes_accessed=2 * (n + members * cap) * feature, transcendentals=0
        ),
        name="deal",
    )(lines(owner), lines(shard), lines(anchor), images)


def attend_kernel(temper, q_ref, doc_ref, k_ref, before_ref, after_ref, id_ref, id_before_ref, id_after_ref, o_ref, *scratch):
    if scratch:
        rows, cap = scratch[0], o_ref.shape[0] // q_ref.shape[0]
        for d in range(q_ref.shape[0]):
            for t, r, c in tiles(cap, rows.shape[1]):
                rows[d * cap + r : d * cap + r + TILE, c : c + LANES] = q_ref[d, t : t + TILE]
        q_ref = rows
    q = q_ref[...]
    doc = doc_ref[...]
    parts = ((k_ref, id_ref), (before_ref, id_before_ref), (after_ref, id_after_ref))
    scores = []
    for rows, ids in parts:
        s = lax.dot_general(q, rows[...], (((1,), (1,)), ((), ())), preferred_element_type=jnp.float32) * temper
        scores.append(jnp.where(doc == ids[...], s, -1e30))
    peak = functools.reduce(jnp.maximum, [jnp.max(s, axis=1, keepdims=True) for s in scores])
    raised = [jnp.where(doc == ids[...], jnp.exp(s - peak), 0.0) for s, (_, ids) in zip(scores, parts)]
    total = sum(jnp.sum(r, axis=1, keepdims=True) for r in raised)
    total = jnp.where(total > 0.0, total, 1.0)
    o_ref[...] = sum(
        jnp.dot((r / total).astype(jnp.bfloat16), rows[...], preferred_element_type=jnp.float32)
        for r, (rows, _) in zip(raised, parts)
    ).astype(jnp.bfloat16)


def attend(queries, docs, sentences, before, after, ids, id_before, id_after):
    rows, (own, feature) = docs.shape[0], sentences.shape
    block = min(256, rows)
    whole = lambda a: pl.BlockSpec(a.shape, lambda i: (0, 0))
    fixed = (sentences, before, after, ids, id_before, id_after)
    tiled = queries.ndim == 3
    queries_spec = pl.BlockSpec((block, feature), lambda i: (i, 0))
    if tiled:
        buckets = block * queries.shape[0] // rows
        queries_spec = pl.BlockSpec((buckets, *queries.shape[1:]), lambda i: (i, 0, 0))
    return pl.pallas_call(
        functools.partial(attend_kernel, feature**-0.5),
        grid=(rows // block,),
        in_specs=[
            queries_spec,
            pl.BlockSpec((block, 1), lambda i: (i, 0)),
            *[whole(a) for a in fixed],
        ],
        out_specs=pl.BlockSpec((block, feature), lambda i: (i, 0)),
        out_shape=jax.ShapeDtypeStruct((rows, feature), jnp.bfloat16),
        scratch_shapes=[pltpu.VMEM((block, feature), jnp.bfloat16)] * tiled,
        compiler_params=pltpu.CompilerParams(vmem_limit_bytes=40 * 1024 * 1024),
        cost_estimate=pl.CostEstimate(
            flops=4 * rows * own * feature, bytes_accessed=2 * (own + 2 * rows) * feature, transcendentals=rows * own
        ),
        name="attend",
    )(queries, docs, *fixed)


def every_device(row, arrived):
    peers, me = lax.axis_size("docs"), lax.axis_index("docs")
    if peers & (peers - 1):
        return lax.all_gather(row, "docs", axis=0, tiled=False), arrived
    step = max(1, peers // 4)
    apart = list(range(0, peers, step))
    rows = [lax.ppermute(row, "docs", [(i, i ^ a) for i in range(peers)]) if a else row for a in apart]
    held, arrived = lax.optimization_barrier((jnp.stack(rows), arrived))
    while step > 1:
        step //= 2
        held = jnp.concatenate([held, lax.ppermute(held, "docs", [(i, i ^ step) for i in range(peers)])], axis=0)
        apart = apart + [a ^ step for a in apart]
    source = jnp.array(apart, dtype=jnp.int32) ^ me
    pick = jnp.arange(peers, dtype=jnp.int32)[:, None] == source[None, :]
    return jnp.sum(jnp.where(pick[:, :, None], held[None], 0), axis=1), arrived


def copy_kernel(x_ref, o_ref):
    o_ref[...] = x_ref[...]


def write_out(x):
    rows, feature = x.shape
    block = min(128, rows)
    spec = pl.BlockSpec((block, feature), lambda i: (i, 0))
    return pl.pallas_call(
        copy_kernel,
        grid=(rows // block,),
        in_specs=[spec],
        out_specs=spec,
        out_shape=jax.ShapeDtypeStruct(x.shape, x.dtype),
        compiler_params=pltpu.CompilerParams(vmem_limit_bytes=8 * 1024 * 1024),
        cost_estimate=pl.CostEstimate(flops=0, bytes_accessed=4 * rows * feature, transcendentals=0),
        name="write_out",
    )(x)


def exchange(x):
    return lax.all_to_all(x, "docs", split_axis=0, concat_axis=0, tiled=True)


def place_kernel(comes_ref, x_ref, o_ref, zero, sem):
    zero[...] = jnp.zeros_like(zero)
    members = x_ref.shape[0]
    moves = [pltpu.make_async_copy(x_ref.at[jnp.maximum(comes_ref[d], 0)], o_ref.at[d], sem.at[d]) for d in range(members)]
    clears = [pltpu.make_async_copy(zero, o_ref.at[d], sem.at[d]) for d in range(members)]
    for d in range(members):
        pl.when(comes_ref[d] >= 0)(moves[d].start)
        pl.when(comes_ref[d] < 0)(clears[d].start)
    for d in range(members):
        pl.when(comes_ref[d] >= 0)(moves[d].wait)
        pl.when(comes_ref[d] < 0)(clears[d].wait)


def place(x, comes):
    members, cap, feature = x.shape
    if cap % TILE:
        row = jnp.arange(members * cap, dtype=jnp.int32)
        block = jnp.repeat(comes, cap)
        takes = ((block * cap + row % cap)[:, None] == row[None, :]) & (block >= 0)[:, None]
        table = takes.astype(jnp.bfloat16)
        rows = x.reshape(members * cap, feature)
        return jnp.dot(table, rows, preferred_element_type=jnp.float32).astype(jnp.bfloat16)
    return pl.pallas_call(
        place_kernel,
        in_specs=[SMEM, VMEM],
        out_specs=HBM,
        out_shape=jax.ShapeDtypeStruct(x.shape, x.dtype),
        scratch_shapes=[pltpu.VMEM((cap, feature), x.dtype), pltpu.SemaphoreType.DMA((members,))],
        compiler_params=pltpu.CompilerParams(vmem_limit_bytes=8 * 1024 * 1024),
        cost_estimate=pl.CostEstimate(flops=0, bytes_accessed=4 * x.size, transcendentals=0),
        name="place",
    )(comes, x).reshape(members * cap, feature)


def shards(sentences, sent_doc, images, image_owner, anchor, loader_shard):
    members = lax.axis_size("docs")
    me = lax.axis_index("docs")
    own, feature = sentences.shape
    n = images.shape[0]
    cap = max(4, 2 * n // members)
    owner, shard = image_owner[:, 0], loader_shard[:, 0]

    spot = jnp.arange(n, dtype=jnp.int32)
    earlier = (owner[:, None] == owner[None, :]) & (spot[None, :] < spot[:, None])
    rank = jnp.sum(earlier.astype(jnp.int32), axis=1)
    slot = jnp.arange(members * cap, dtype=jnp.int32)[:, None]

    def buckets(targets):
        table = (slot == (targets * cap + rank)[None, :]).astype(jnp.bfloat16)
        out = jnp.dot(table, images, preferred_element_type=jnp.float32).astype(jnp.bfloat16)
        return out.reshape(members, cap, feature)

    whole_tiles = cap % TILE == 0 and feature % LANES == 0 and n % LANES == 0
    if whole_tiles and 4 * n <= TILE * LANES and members <= 256 and own <= 256 * LANES:
        queries = exchange(deal(images, owner, shard, anchor, members, cap))
        told = queries[:, cap * feature // LANES :][:, : 4 * n // LANES].reshape(members, 4, n).astype(jnp.int32)
        owner_of, shard_of, spot_of = told[:, 0], told[:, 1], told[:, 2] * LANES + told[:, 3]
    else:
        packed = (owner * members + shard) * own + anchor
        every, arrived = every_device(packed, exchange(buckets(owner)))
        queries = arrived.reshape(members * cap, feature)
        owner_of, shard_of, spot_of = every // (own * members), every // own % members, every % own
    loaded_images = write_out(exchange(buckets(shard)).reshape(members * cap, feature))
    before, after = halo_of(sentences)

    mine = owner_of == me
    sooner = (spot[:, None] < spot[None, :]).astype(jnp.bfloat16)
    ranks = jnp.dot(mine.astype(jnp.bfloat16), sooner, preferred_element_type=jnp.float32).astype(jnp.int32)
    slots = jnp.arange(cap, dtype=jnp.int32)
    hit = mine[:, None, :] & (ranks[:, None, :] == slots[None, :, None])
    spots = jnp.sum(jnp.where(hit, spot_of[:, None, :] + 1, 0), axis=2).reshape(members * cap) - 1
    ids = lax.dynamic_slice_in_dim(sent_doc, me * own, own)
    here = spots[:, None] == jnp.arange(own, dtype=jnp.int32)[None, :]
    docs = jnp.max(jnp.where(here, ids[None, :], -2), axis=1)
    padded = jnp.pad(sent_doc, (MOST_SENT, MOST_SENT), constant_values=-1)
    id_before = lax.dynamic_slice_in_dim(padded, me * own, MOST_SENT)
    id_after = lax.dynamic_slice_in_dim(padded, me * own + own + MOST_SENT, MOST_SENT)
    aligned = attend(queries, docs[:, None], sentences, before, after, ids[None], id_before[None], id_after[None])

    goes = jnp.max(jnp.where(mine, shard_of + 1, 0), axis=1) - 1
    comes = jnp.max(jnp.where(shard_of == me, owner_of + 1, 0), axis=1) - 1

    row = jnp.arange(members * cap, dtype=jnp.int32)
    puts = row[:, None] == (jnp.repeat(goes, cap) * cap + row % cap)[None, :]
    puts = (puts & (jnp.repeat(goes, cap) >= 0)[None, :]).astype(jnp.bfloat16)
    sent = jnp.dot(puts, aligned, preferred_element_type=jnp.float32).astype(jnp.bfloat16).reshape(members, cap, feature)
    loaded_text = place(exchange(sent), comes)
    return loaded_images, loaded_text


def solution(mesh):
    split = P(("groups", "docs"))
    rows = P(("groups", "docs"), None)
    return jax.shard_map(
        shards,
        mesh=mesh,
        in_specs=(rows, P("groups"), rows, rows, split, rows),
        out_specs=(rows, rows),
        check_vma=False,
    )
```

```python
import functools

import jax
import jax.numpy as jnp
from jax import lax
from jax.experimental import pallas as pl
from jax.experimental.pallas import tpu as pltpu
from jax.sharding import PartitionSpec as P

MOST_SENT = 32
TILE = 16
LANES = 128
VMEM, SMEM, HBM = (pl.BlockSpec(memory_space=m) for m in (pltpu.VMEM, pltpu.SMEM, pltpu.HBM))


def halo_of(sentences):
    peers = lax.axis_size("docs")
    up = [(i, i + 1) for i in range(peers - 1)]
    down = [(j, i) for i, j in up]
    before = lax.ppermute(sentences[-MOST_SENT:], "docs", up)
    after = lax.ppermute(sentences[:MOST_SENT], "docs", down)
    return before, after


def deal_kernel(cap, members, base_ref, owner_ref, shard_ref, anchor_ref, rows_ref, o_ref):
    half, lines, (n, feature) = o_ref.shape[0], owner_ref.shape[0], rows_ref.shape
    size = cap * feature // LANES
    owner, shard, anchor = owner_ref[...], shard_ref[...], anchor_ref[...]
    told = jnp.concatenate([owner, shard, anchor // LANES, anchor % LANES], axis=0)
    told = jnp.concatenate([told, jnp.zeros((TILE - 4 * lines, LANES), jnp.int32)], axis=0)
    told = told.astype(jnp.float32).astype(jnp.bfloat16)
    owner, shard = (jnp.concatenate([x[i : i + 1] for i in range(lines)], axis=1) for x in (owner, shard))
    label = lax.broadcasted_iota(jnp.int32, (members, n), 0)
    theirs = jnp.where(label == owner, 1.0, 0.0)
    sooner = lax.broadcasted_iota(jnp.int32, (n, n), 0) < lax.broadcasted_iota(jnp.int32, (n, n), 1)
    before = jnp.dot(
        theirs.astype(jnp.bfloat16), jnp.where(sooner, 1.0, 0.0).astype(jnp.bfloat16), preferred_element_type=jnp.float32
    )
    rank = jnp.sum(theirs * before, axis=0, keepdims=True).astype(jnp.int32)
    slot = lax.broadcasted_iota(jnp.int32, (half * cap, n), 0)
    for k, target in enumerate((owner, shard)[: o_ref.shape[1] // size]):
        place = (target - base_ref[0]) * cap + rank
        table = jnp.where(slot == place, 1.0, 0.0).astype(jnp.bfloat16)
        out = jnp.dot(table, rows_ref[...], preferred_element_type=jnp.float32).astype(jnp.bfloat16)
        for d in range(half):
            for t, r, c in tiles(cap, feature):
                o_ref[d, k * size + t : k * size + t + TILE] = out[d * cap + r : d * cap + r + TILE, c : c + LANES]
    for d in range(half):
        o_ref[d, o_ref.shape[1] - TILE :] = told


def tiles(rows, columns):
    every = [(r, c) for r in range(0, rows, TILE) for c in range(0, columns, LANES)]
    return [(i * TILE, r, c) for i, (r, c) in enumerate(every)]


def deal(images, owner, shard, anchor, first, members, cap, regions):
    n, feature = images.shape
    lines = lambda a: a.reshape(n // LANES, LANES)
    half = members // 2
    shape = (half, regions * cap * feature // LANES + TILE, LANES)
    return pl.pallas_call(
        functools.partial(deal_kernel, cap, members),
        in_specs=[SMEM] + [pl.BlockSpec()] * 4,
        out_specs=pl.BlockSpec(),
        out_shape=jax.ShapeDtypeStruct(shape, jnp.bfloat16),
        compiler_params=pltpu.CompilerParams(vmem_limit_bytes=60 * 1024 * 1024),
        cost_estimate=pl.CostEstimate(
            flops=2 * regions * half * cap * n * feature, bytes_accessed=2 * (n + regions * half * cap) * feature, transcendentals=0
        ),
        name="deal",
    )(first[None], lines(owner), lines(shard), lines(anchor), images)


def merge_kernel(low_ref, near_ref, far_ref, o_ref):
    cap, feature = far_ref.shape[1:]
    size = cap * feature // LANES
    s, half = pl.program_id(0), pl.num_programs(0) // 2
    is_near = (s < half) == (low_ref[0] == 1)

    @pl.when(is_near)
    def _():
        for t, r, c in tiles(cap, feature):
            o_ref[0, r : r + TILE, c : c + LANES] = near_ref[0, size + t : size + t + TILE]

    @pl.when(jnp.logical_not(is_near))
    def _():
        o_ref[...] = far_ref[...]


def merge(near, far, low):
    half, cap, feature = far.shape
    return pl.pallas_call(
        merge_kernel,
        grid=(2 * half,),
        in_specs=[
            SMEM,
            pl.BlockSpec((1, *near.shape[1:]), lambda i: (i % half, 0, 0)),
            pl.BlockSpec((1, cap, feature), lambda i: (i % half, 0, 0)),
        ],
        out_specs=pl.BlockSpec((1, cap, feature), lambda i: (i, 0, 0)),
        out_shape=jax.ShapeDtypeStruct((2 * half, cap, feature), far.dtype),
        compiler_params=pltpu.CompilerParams(vmem_limit_bytes=8 * 1024 * 1024),
        cost_estimate=pl.CostEstimate(flops=0, bytes_accessed=8 * half * cap * feature, transcendentals=0),
        name="merge",
    )(low.astype(jnp.int32)[None], near, far)


def attend_kernel(temper, q_ref, doc_ref, k_ref, before_ref, after_ref, id_ref, id_before_ref, id_after_ref, o_ref, *scratch):
    if scratch:
        rows, cap = scratch[0], o_ref.shape[0] // q_ref.shape[0]
        for d in range(q_ref.shape[0]):
            for t, r, c in tiles(cap, rows.shape[1]):
                rows[d * cap + r : d * cap + r + TILE, c : c + LANES] = q_ref[d, t : t + TILE]
        q_ref = rows
    q = q_ref[...]
    doc = doc_ref[...]
    parts = ((k_ref, id_ref), (before_ref, id_before_ref), (after_ref, id_after_ref))
    scores = []
    for rows, ids in parts:
        s = lax.dot_general(q, rows[...], (((1,), (1,)), ((), ())), preferred_element_type=jnp.float32) * temper
        scores.append(jnp.where(doc == ids[...], s, -1e30))
    peak = functools.reduce(jnp.maximum, [jnp.max(s, axis=1, keepdims=True) for s in scores])
    raised = [jnp.where(doc == ids[...], jnp.exp(s - peak), 0.0) for s, (_, ids) in zip(scores, parts)]
    total = sum(jnp.sum(r, axis=1, keepdims=True) for r in raised)
    total = jnp.where(total > 0.0, total, 1.0)
    o_ref[...] = sum(
        jnp.dot((r / total).astype(jnp.bfloat16), rows[...], preferred_element_type=jnp.float32)
        for r, (rows, _) in zip(raised, parts)
    ).astype(jnp.bfloat16)


def attend(queries, cap, docs, known):
    rows, (own, feature) = docs.shape[0], known[0].shape
    block = min(256, rows)
    whole = lambda a: pl.BlockSpec(a.shape, lambda i: (0, 0))
    tiled = queries.ndim == 3
    queries_spec = pl.BlockSpec((block, feature), lambda i: (i, 0))
    if tiled:
        region = cap * feature // LANES
        queries_spec = pl.BlockSpec((block // cap, region, LANES), lambda i: (i, 0, 0))
    return pl.pallas_call(
        functools.partial(attend_kernel, feature**-0.5),
        grid=(rows // block,),
        in_specs=[
            queries_spec,
            pl.BlockSpec((block, 1), lambda i: (i, 0)),
            *[whole(a) for a in known],
        ],
        out_specs=pl.BlockSpec((block, feature), lambda i: (i, 0)),
        out_shape=jax.ShapeDtypeStruct((rows, feature), jnp.bfloat16),
        scratch_shapes=[pltpu.VMEM((block, feature), jnp.bfloat16)] * tiled,
        compiler_params=pltpu.CompilerParams(vmem_limit_bytes=40 * 1024 * 1024),
        cost_estimate=pl.CostEstimate(
            flops=4 * rows * own * feature, bytes_accessed=2 * (own + 2 * rows) * feature, transcendentals=rows * own
        ),
        name="attend",
    )(queries, docs, *known)


def every_device(row, arrived):
    peers, me = lax.axis_size("docs"), lax.axis_index("docs")
    if peers & (peers - 1):
        return lax.all_gather(row, "docs", axis=0, tiled=False), arrived
    step = max(1, peers // 4)
    apart = list(range(0, peers, step))
    rows = [lax.ppermute(row, "docs", [(i, i ^ a) for i in range(peers)]) if a else row for a in apart]
    held, arrived = lax.optimization_barrier((jnp.stack(rows), arrived))
    while step > 1:
        step //= 2
        held = jnp.concatenate([held, lax.ppermute(held, "docs", [(i, i ^ step) for i in range(peers)])], axis=0)
        apart = apart + [a ^ step for a in apart]
    source = jnp.array(apart, dtype=jnp.int32) ^ me
    pick = jnp.arange(peers, dtype=jnp.int32)[:, None] == source[None, :]
    return jnp.sum(jnp.where(pick[:, :, None], held[None], 0), axis=1), arrived


def copy_kernel(x_ref, o_ref):
    o_ref[...] = x_ref[...]


def write_out(x):
    rows, feature = x.shape
    block = min(128, rows)
    spec = pl.BlockSpec((block, feature), lambda i: (i, 0))
    return pl.pallas_call(
        copy_kernel,
        grid=(rows // block,),
        in_specs=[spec],
        out_specs=spec,
        out_shape=jax.ShapeDtypeStruct(x.shape, x.dtype),
        compiler_params=pltpu.CompilerParams(vmem_limit_bytes=8 * 1024 * 1024),
        cost_estimate=pl.CostEstimate(flops=0, bytes_accessed=4 * rows * feature, transcendentals=0),
        name="write_out",
    )(x)


def exchange(x):
    return lax.all_to_all(x, "docs", split_axis=0, concat_axis=0, tiled=True)


def place_kernel(comes_ref, x_ref, o_ref, zero, sem):
    zero[...] = jnp.zeros_like(zero)
    members = x_ref.shape[0]
    moves = [pltpu.make_async_copy(x_ref.at[jnp.maximum(comes_ref[d], 0)], o_ref.at[d], sem.at[d]) for d in range(members)]
    clears = [pltpu.make_async_copy(zero, o_ref.at[d], sem.at[d]) for d in range(members)]
    for d in range(members):
        pl.when(comes_ref[d] >= 0)(moves[d].start)
        pl.when(comes_ref[d] < 0)(clears[d].start)
    for d in range(members):
        pl.when(comes_ref[d] >= 0)(moves[d].wait)
        pl.when(comes_ref[d] < 0)(clears[d].wait)


def place(x, comes):
    members, cap, feature = x.shape
    if cap % TILE:
        row = jnp.arange(members * cap, dtype=jnp.int32)
        block = jnp.repeat(comes, cap)
        takes = ((block * cap + row % cap)[:, None] == row[None, :]) & (block >= 0)[:, None]
        table = takes.astype(jnp.bfloat16)
        rows = x.reshape(members * cap, feature)
        return jnp.dot(table, rows, preferred_element_type=jnp.float32).astype(jnp.bfloat16)
    return pl.pallas_call(
        place_kernel,
        in_specs=[SMEM, VMEM],
        out_specs=HBM,
        out_shape=jax.ShapeDtypeStruct(x.shape, x.dtype),
        scratch_shapes=[pltpu.VMEM((cap, feature), x.dtype), pltpu.SemaphoreType.DMA((members,))],
        compiler_params=pltpu.CompilerParams(vmem_limit_bytes=8 * 1024 * 1024),
        cost_estimate=pl.CostEstimate(flops=0, bytes_accessed=4 * x.size, transcendentals=0),
        name="place",
    )(comes, x).reshape(members * cap, feature)


def one_hot_dot(table, rows):
    return jnp.dot(table.astype(jnp.bfloat16), rows, preferred_element_type=jnp.float32).astype(jnp.bfloat16)


def shards(sentences, sent_doc, images, image_owner, anchor, loader_shard):
    members = lax.axis_size("docs")
    me = lax.axis_index("docs")
    own, feature = sentences.shape
    n = images.shape[0]
    cap = max(4, 2 * n // members)
    owner, shard = image_owner[:, 0], loader_shard[:, 0]
    spot = jnp.arange(n, dtype=jnp.int32)
    slots = jnp.arange(cap, dtype=jnp.int32)

    def by_shard(rows, owner, shard, start, count):
        earlier = (owner[:, None] == owner[None, :]) & (spot[None, :] < spot[:, None])
        rank = jnp.sum(earlier.astype(jnp.int32), axis=1)
        slot = jnp.arange(count * cap, dtype=jnp.int32)[:, None]
        return one_hot_dot(slot == ((shard - start) * cap + rank)[None, :], rows).reshape(count, cap, feature)

    ids = lax.dynamic_slice_in_dim(sent_doc, me * own, own)
    padded = jnp.pad(sent_doc, (MOST_SENT, MOST_SENT), constant_values=-1)
    id_before = lax.dynamic_slice_in_dim(padded, me * own, MOST_SENT)
    id_after = lax.dynamic_slice_in_dim(padded, me * own + own + MOST_SENT, MOST_SENT)
    before, after = halo_of(sentences)
    known = (sentences, before, after, ids[None], id_before[None], id_after[None])

    def slots_of(owner_of, shard_of, spot_of):
        mine = owner_of == me
        sooner = (spot[:, None] < spot[None, :]).astype(jnp.bfloat16)
        ranks = jnp.dot(mine.astype(jnp.bfloat16), sooner, preferred_element_type=jnp.float32).astype(jnp.int32)
        hit = mine[:, None, :] & (ranks[:, None, :] == slots[None, :, None])
        spots = jnp.sum(jnp.where(hit, spot_of[:, None, :] + 1, 0), axis=2).reshape(-1) - 1
        here = spots[:, None] == jnp.arange(own, dtype=jnp.int32)[None, :]
        docs = jnp.max(jnp.where(here, ids[None, :], -2), axis=1)
        goes = jnp.max(jnp.where(mine, shard_of + 1, 0), axis=1) - 1
        comes = jnp.max(jnp.where(shard_of == me, owner_of + 1, 0), axis=1) - 1
        return docs[:, None], goes, comes

    row = jnp.arange(members * cap, dtype=jnp.int32)

    def puts(goes):
        block, slot = jnp.repeat(goes, cap), jnp.arange(goes.shape[0] * cap, dtype=jnp.int32) % cap
        return (row[:, None] == (block * cap + slot)[None, :]) & (block >= 0)[None, :]

    whole_tiles = cap % TILE == 0 and feature % LANES == 0 and n % LANES == 0 and members % 2 == 0
    if whole_tiles and 4 * n <= TILE * LANES and members <= 256 and own <= 256 * LANES:
        half = members // 2
        first = me // half * half
        halves = [list(range(half)), list(range(half, members))]
        across = [(i, (i + half) % members) for i in range(members)]

        def exchange_half(x):
            return lax.all_to_all(x, "docs", split_axis=0, concat_axis=0, tiled=True, axis_index_groups=halves)

        def told_by(x):
            told = x[:, -TILE:][:, : 4 * n // LANES].reshape(half, 4, n).astype(jnp.int32)
            return told[:, 0], told[:, 1], told[:, 2] * LANES + told[:, 3]

        codes = jnp.stack([owner, shard, anchor])
        mirrored, codes_mirror = lax.ppermute(images, "docs", across), lax.ppermute(codes, "docs", across)
        near = exchange_half(deal(images, owner, shard, anchor, first, members, cap, 2))
        docs, goes, comes = slots_of(*told_by(near))
        aligned = attend(near, cap, docs, known)
        sent, mirrored = lax.optimization_barrier((one_hot_dot(puts(goes), aligned), mirrored))

        far = exchange_half(deal(mirrored, *codes_mirror, first, members, cap, 1))
        far_images = exchange_half(by_shard(mirrored, codes_mirror[0], codes_mirror[1], first, half))
        docs, goes, comes_far = slots_of(*told_by(far))
        aligned = attend(far, cap, docs, known)
        sent += jnp.dot(puts(goes).astype(jnp.bfloat16), aligned, preferred_element_type=jnp.float32)
        sent, far_images = lax.optimization_barrier((sent.astype(jnp.bfloat16), far_images))
        low = first == 0
        comes = jnp.where(low, jnp.concatenate([comes, comes_far]), jnp.concatenate([comes_far, comes]))
        loaded_images = merge(near, far_images, low).reshape(members * cap, feature)
    else:
        packed = (owner * members + shard) * own + anchor
        every, queries = every_device(packed, exchange(by_shard(images, owner, owner, 0, members)))
        loaded_images = write_out(exchange(by_shard(images, owner, shard, 0, members)).reshape(members * cap, feature))
        docs, goes, comes = slots_of(every // (own * members), every // own % members, every % own)
        aligned = attend(queries.reshape(members * cap, feature), cap, docs, known)
        sent = one_hot_dot(puts(goes), aligned)
    loaded_text = place(exchange(sent.reshape(members, cap, feature)), comes)
    return loaded_images, loaded_text


def solution(mesh):
    split = P(("groups", "docs"))
    rows = P(("groups", "docs"), None)
    return jax.shard_map(
        shards,
        mesh=mesh,
        in_specs=(rows, P("groups"), rows, rows, split, rows),
        out_specs=(rows, rows),
        check_vma=False,
    )
```

```python
import functools

import jax
import jax.numpy as jnp
from jax import lax
from jax.experimental import pallas as pl
from jax.experimental.pallas import tpu as pltpu
from jax.sharding import PartitionSpec as P

MOST_SENT = 32
TILE = 16
LANES = 128
VMEM, SMEM, HBM = (pl.BlockSpec(memory_space=m) for m in (pltpu.VMEM, pltpu.SMEM, pltpu.HBM))


def halo_of(sentences):
    peers = lax.axis_size("docs")
    up = [(i, i + 1) for i in range(peers - 1)]
    down = [(j, i) for i, j in up]
    before = lax.ppermute(sentences[-MOST_SENT:], "docs", up)
    after = lax.ppermute(sentences[:MOST_SENT], "docs", down)
    return before, after


def deal_kernel(cap, members, base_ref, owner_ref, shard_ref, anchor_ref, rows_ref, o_ref):
    half, lines, (n, feature) = o_ref.shape[0], owner_ref.shape[0], rows_ref.shape
    size = cap * feature // LANES
    owner, shard, anchor = owner_ref[...], shard_ref[...], anchor_ref[...]
    told = jnp.concatenate([owner, shard, anchor // LANES, anchor % LANES], axis=0)
    told = jnp.concatenate([told, jnp.zeros((TILE - 4 * lines, LANES), jnp.int32)], axis=0)
    told = told.astype(jnp.float32).astype(jnp.bfloat16)
    owner, shard = (jnp.concatenate([x[i : i + 1] for i in range(lines)], axis=1) for x in (owner, shard))
    label = lax.broadcasted_iota(jnp.int32, (members, n), 0)
    theirs = jnp.where(label == owner, 1.0, 0.0)
    sooner = lax.broadcasted_iota(jnp.int32, (n, n), 0) < lax.broadcasted_iota(jnp.int32, (n, n), 1)
    before = jnp.dot(
        theirs.astype(jnp.bfloat16), jnp.where(sooner, 1.0, 0.0).astype(jnp.bfloat16), preferred_element_type=jnp.float32
    )
    rank = jnp.sum(theirs * before, axis=0, keepdims=True).astype(jnp.int32)
    slot = lax.broadcasted_iota(jnp.int32, (half * cap, n), 0)
    for k, target in enumerate((owner, shard)[: o_ref.shape[1] // size]):
        place = (target - base_ref[0]) * cap + rank
        table = jnp.where(slot == place, 1.0, 0.0).astype(jnp.bfloat16)
        out = jnp.dot(table, rows_ref[...], preferred_element_type=jnp.float32).astype(jnp.bfloat16)
        for d in range(half):
            for t, r, c in tiles(cap, feature):
                o_ref[d, k * size + t : k * size + t + TILE] = out[d * cap + r : d * cap + r + TILE, c : c + LANES]
    for d in range(half):
        o_ref[d, o_ref.shape[1] - TILE :] = told


def tiles(rows, columns):
    every = [(r, c) for r in range(0, rows, TILE) for c in range(0, columns, LANES)]
    return [(i * TILE, r, c) for i, (r, c) in enumerate(every)]


def deal(images, owner, shard, anchor, first, members, cap, regions):
    n, feature = images.shape
    lines = lambda a: a.reshape(n // LANES, LANES)
    half = members // 2
    shape = (half, regions * cap * feature // LANES + TILE, LANES)
    return pl.pallas_call(
        functools.partial(deal_kernel, cap, members),
        in_specs=[SMEM] + [pl.BlockSpec()] * 4,
        out_specs=pl.BlockSpec(),
        out_shape=jax.ShapeDtypeStruct(shape, jnp.bfloat16),
        compiler_params=pltpu.CompilerParams(vmem_limit_bytes=60 * 1024 * 1024),
        cost_estimate=pl.CostEstimate(
            flops=2 * regions * half * cap * n * feature, bytes_accessed=2 * (n + regions * half * cap) * feature, transcendentals=0
        ),
        name="deal",
    )(first[None], lines(owner), lines(shard), lines(anchor), images)


def merge_kernel(low_ref, near_ref, far_ref, o_ref):
    cap, feature = far_ref.shape[1:]
    size = cap * feature // LANES
    s, half = pl.program_id(0), pl.num_programs(0) // 2
    is_near = (s < half) == (low_ref[0] == 1)

    @pl.when(is_near)
    def _():
        for t, r, c in tiles(cap, feature):
            o_ref[0, r : r + TILE, c : c + LANES] = near_ref[0, size + t : size + t + TILE]

    @pl.when(jnp.logical_not(is_near))
    def _():
        o_ref[...] = far_ref[...]


def merge(near, far, low):
    half, cap, feature = far.shape
    return pl.pallas_call(
        merge_kernel,
        grid=(2 * half,),
        in_specs=[
            SMEM,
            pl.BlockSpec((1, *near.shape[1:]), lambda i: (i % half, 0, 0)),
            pl.BlockSpec((1, cap, feature), lambda i: (i % half, 0, 0)),
        ],
        out_specs=pl.BlockSpec((1, cap, feature), lambda i: (i, 0, 0)),
        out_shape=jax.ShapeDtypeStruct((2 * half, cap, feature), far.dtype),
        compiler_params=pltpu.CompilerParams(vmem_limit_bytes=8 * 1024 * 1024),
        cost_estimate=pl.CostEstimate(flops=0, bytes_accessed=8 * half * cap * feature, transcendentals=0),
        name="merge",
    )(low.astype(jnp.int32)[None], near, far)


def attend_kernel(temper, q_ref, doc_ref, k_ref, before_ref, after_ref, id_ref, id_before_ref, id_after_ref, o_ref, *scratch):
    if scratch:
        rows, cap = scratch[0], o_ref.shape[0] // q_ref.shape[0]
        for d in range(q_ref.shape[0]):
            for t, r, c in tiles(cap, rows.shape[1]):
                rows[d * cap + r : d * cap + r + TILE, c : c + LANES] = q_ref[d, t : t + TILE]
        q_ref = rows
    q = q_ref[...]
    doc = doc_ref[...]
    parts = ((k_ref, id_ref), (before_ref, id_before_ref), (after_ref, id_after_ref))
    scores = []
    for rows, ids in parts:
        s = lax.dot_general(q, rows[...], (((1,), (1,)), ((), ())), preferred_element_type=jnp.float32) * temper
        scores.append(jnp.where(doc == ids[...], s, -1e30))
    peak = functools.reduce(jnp.maximum, [jnp.max(s, axis=1, keepdims=True) for s in scores])
    raised = [jnp.where(doc == ids[...], jnp.exp(s - peak), 0.0) for s, (_, ids) in zip(scores, parts)]
    total = sum(jnp.sum(r, axis=1, keepdims=True) for r in raised)
    total = jnp.where(total > 0.0, total, 1.0)
    o_ref[...] = sum(
        jnp.dot((r / total).astype(jnp.bfloat16), rows[...], preferred_element_type=jnp.float32)
        for r, (rows, _) in zip(raised, parts)
    ).astype(jnp.bfloat16)


def attend(queries, cap, docs, known):
    rows, (own, feature) = docs.shape[0], known[0].shape
    block = min(256, rows)
    whole = lambda a: pl.BlockSpec(a.shape, lambda i: (0, 0))
    tiled = queries.ndim == 3
    queries_spec = pl.BlockSpec((block, feature), lambda i: (i, 0))
    if tiled:
        region = cap * feature // LANES
        queries_spec = pl.BlockSpec((block // cap, region, LANES), lambda i: (i, 0, 0))
    return pl.pallas_call(
        functools.partial(attend_kernel, feature**-0.5),
        grid=(rows // block,),
        in_specs=[
            queries_spec,
            pl.BlockSpec((block, 1), lambda i: (i, 0)),
            *[whole(a) for a in known],
        ],
        out_specs=pl.BlockSpec((block, feature), lambda i: (i, 0)),
        out_shape=jax.ShapeDtypeStruct((rows, feature), jnp.bfloat16),
        scratch_shapes=[pltpu.VMEM((block, feature), jnp.bfloat16)] * tiled,
        compiler_params=pltpu.CompilerParams(vmem_limit_bytes=40 * 1024 * 1024),
        cost_estimate=pl.CostEstimate(
            flops=4 * rows * own * feature, bytes_accessed=2 * (own + 2 * rows) * feature, transcendentals=rows * own
        ),
        name="attend",
    )(queries, docs, *known)


def every_device(row, arrived):
    peers, me = lax.axis_size("docs"), lax.axis_index("docs")
    if peers & (peers - 1):
        return lax.all_gather(row, "docs", axis=0, tiled=False), arrived
    step = max(1, peers // 4)
    apart = list(range(0, peers, step))
    rows = [lax.ppermute(row, "docs", [(i, i ^ a) for i in range(peers)]) if a else row for a in apart]
    held, arrived = lax.optimization_barrier((jnp.stack(rows), arrived))
    while step > 1:
        step //= 2
        held = jnp.concatenate([held, lax.ppermute(held, "docs", [(i, i ^ step) for i in range(peers)])], axis=0)
        apart = apart + [a ^ step for a in apart]
    source = jnp.array(apart, dtype=jnp.int32) ^ me
    pick = jnp.arange(peers, dtype=jnp.int32)[:, None] == source[None, :]
    return jnp.sum(jnp.where(pick[:, :, None], held[None], 0), axis=1), arrived


def copy_kernel(x_ref, o_ref):
    o_ref[...] = x_ref[...]


def write_out(x):
    rows, feature = x.shape
    block = min(128, rows)
    spec = pl.BlockSpec((block, feature), lambda i: (i, 0))
    return pl.pallas_call(
        copy_kernel,
        grid=(rows // block,),
        in_specs=[spec],
        out_specs=spec,
        out_shape=jax.ShapeDtypeStruct(x.shape, x.dtype),
        compiler_params=pltpu.CompilerParams(vmem_limit_bytes=8 * 1024 * 1024),
        cost_estimate=pl.CostEstimate(flops=0, bytes_accessed=4 * rows * feature, transcendentals=0),
        name="write_out",
    )(x)


def exchange(x):
    return lax.all_to_all(x, "docs", split_axis=0, concat_axis=0, tiled=True)


def place_kernel(comes_ref, x_ref, o_ref, zero, sem):
    zero[...] = jnp.zeros_like(zero)
    members = x_ref.shape[0]
    moves = [pltpu.make_async_copy(x_ref.at[jnp.maximum(comes_ref[d], 0)], o_ref.at[d], sem.at[d]) for d in range(members)]
    clears = [pltpu.make_async_copy(zero, o_ref.at[d], sem.at[d]) for d in range(members)]
    for d in range(members):
        pl.when(comes_ref[d] >= 0)(moves[d].start)
        pl.when(comes_ref[d] < 0)(clears[d].start)
    for d in range(members):
        pl.when(comes_ref[d] >= 0)(moves[d].wait)
        pl.when(comes_ref[d] < 0)(clears[d].wait)


def place(x, comes):
    members, cap, feature = x.shape
    if cap % TILE:
        row = jnp.arange(members * cap, dtype=jnp.int32)
        block = jnp.repeat(comes, cap)
        takes = ((block * cap + row % cap)[:, None] == row[None, :]) & (block >= 0)[:, None]
        table = takes.astype(jnp.bfloat16)
        rows = x.reshape(members * cap, feature)
        return jnp.dot(table, rows, preferred_element_type=jnp.float32).astype(jnp.bfloat16)
    return pl.pallas_call(
        place_kernel,
        in_specs=[SMEM, VMEM],
        out_specs=HBM,
        out_shape=jax.ShapeDtypeStruct(x.shape, x.dtype),
        scratch_shapes=[pltpu.VMEM((cap, feature), x.dtype), pltpu.SemaphoreType.DMA((members,))],
        compiler_params=pltpu.CompilerParams(vmem_limit_bytes=8 * 1024 * 1024),
        cost_estimate=pl.CostEstimate(flops=0, bytes_accessed=4 * x.size, transcendentals=0),
        name="place",
    )(comes, x).reshape(members * cap, feature)


def one_hot_dot(table, rows):
    return jnp.dot(table.astype(jnp.bfloat16), rows, preferred_element_type=jnp.float32).astype(jnp.bfloat16)


def shards(sentences, sent_doc, images, image_owner, anchor, loader_shard):
    members = lax.axis_size("docs")
    me = lax.axis_index("docs")
    own, feature = sentences.shape
    n = images.shape[0]
    cap = max(4, 2 * n // members)
    owner, shard = image_owner[:, 0], loader_shard[:, 0]
    spot = jnp.arange(n, dtype=jnp.int32)
    slots = jnp.arange(cap, dtype=jnp.int32)

    def by_shard(rows, owner, shard, start, count):
        earlier = (owner[:, None] == owner[None, :]) & (spot[None, :] < spot[:, None])
        rank = jnp.sum(earlier.astype(jnp.int32), axis=1)
        slot = jnp.arange(count * cap, dtype=jnp.int32)[:, None]
        return one_hot_dot(slot == ((shard - start) * cap + rank)[None, :], rows).reshape(count, cap, feature)

    ids = lax.dynamic_slice_in_dim(sent_doc, me * own, own)
    padded = jnp.pad(sent_doc, (MOST_SENT, MOST_SENT), constant_values=-1)
    id_before = lax.dynamic_slice_in_dim(padded, me * own, MOST_SENT)
    id_after = lax.dynamic_slice_in_dim(padded, me * own + own + MOST_SENT, MOST_SENT)
    before, after = halo_of(sentences)
    known = (sentences, before, after, ids[None], id_before[None], id_after[None])

    def slots_of(owner_of, shard_of, spot_of):
        mine = owner_of == me
        sooner = (spot[:, None] < spot[None, :]).astype(jnp.bfloat16)
        ranks = jnp.dot(mine.astype(jnp.bfloat16), sooner, preferred_element_type=jnp.float32).astype(jnp.int32)
        hit = mine[:, None, :] & (ranks[:, None, :] == slots[None, :, None])
        spots = jnp.sum(jnp.where(hit, spot_of[:, None, :] + 1, 0), axis=2).reshape(-1) - 1
        here = spots[:, None] == jnp.arange(own, dtype=jnp.int32)[None, :]
        docs = jnp.max(jnp.where(here, ids[None, :], -2), axis=1)
        goes = jnp.max(jnp.where(mine, shard_of + 1, 0), axis=1) - 1
        comes = jnp.max(jnp.where(shard_of == me, owner_of + 1, 0), axis=1) - 1
        return docs[:, None], goes, comes

    row = jnp.arange(members * cap, dtype=jnp.int32)

    def puts(goes):
        block, slot = jnp.repeat(goes, cap), jnp.arange(goes.shape[0] * cap, dtype=jnp.int32) % cap
        return (row[:, None] == (block * cap + slot)[None, :]) & (block >= 0)[None, :]

    whole_tiles = cap % TILE == 0 and feature % LANES == 0 and n % LANES == 0 and members % 2 == 0
    if whole_tiles and 4 * n <= TILE * LANES and members <= 256 and own <= 256 * LANES:
        half = members // 2
        first = me // half * half
        halves = [list(range(half)), list(range(half, members))]
        across = [(i, (i + half) % members) for i in range(members)]

        def exchange_half(x):
            return lax.all_to_all(x, "docs", split_axis=0, concat_axis=0, tiled=True, axis_index_groups=halves)

        def told_by(x):
            told = x[:, -TILE:][:, : 4 * n // LANES].reshape(half, 4, n).astype(jnp.int32)
            return told[:, 0], told[:, 1], told[:, 2] * LANES + told[:, 3]

        codes = jnp.stack([owner, shard, anchor])
        mirrored, codes_mirror = lax.ppermute(images, "docs", across), lax.ppermute(codes, "docs", across)
        near = exchange_half(deal(images, owner, shard, anchor, first, members, cap, 2))
        docs, goes, comes = slots_of(*told_by(near))
        aligned = attend(near, cap, docs, known)
        sent = one_hot_dot(puts(goes), aligned)
        sent, mirrored, codes_mirror = lax.optimization_barrier((sent, mirrored, codes_mirror))

        far = exchange_half(deal(mirrored, *codes_mirror, first, members, cap, 1))
        far_images = exchange_half(by_shard(mirrored, codes_mirror[0], codes_mirror[1], first, half))
        docs, goes, comes_far = slots_of(*told_by(far))
        aligned = attend(far, cap, docs, known)
        sent += jnp.dot(puts(goes).astype(jnp.bfloat16), aligned, preferred_element_type=jnp.float32)
        sent, far_images = lax.optimization_barrier((sent.astype(jnp.bfloat16), far_images))
        low = first == 0
        comes = jnp.where(low, jnp.concatenate([comes, comes_far]), jnp.concatenate([comes_far, comes]))
        loaded_images = merge(near, far_images, low).reshape(members * cap, feature)
    else:
        packed = (owner * members + shard) * own + anchor
        every, queries = every_device(packed, exchange(by_shard(images, owner, owner, 0, members)))
        loaded_images = write_out(exchange(by_shard(images, owner, shard, 0, members)).reshape(members * cap, feature))
        docs, goes, comes = slots_of(every // (own * members), every // own % members, every % own)
        aligned = attend(queries.reshape(members * cap, feature), cap, docs, known)
        sent = one_hot_dot(puts(goes), aligned)
    loaded_text = place(exchange(sent.reshape(members, cap, feature)), comes)
    return loaded_images, loaded_text


def solution(mesh):
    split = P(("groups", "docs"))
    rows = P(("groups", "docs"), None)
    return jax.shard_map(
        shards,
        mesh=mesh,
        in_specs=(rows, P("groups"), rows, rows, split, rows),
        out_specs=(rows, rows),
        check_vma=False,
    )
```

```python
import functools

import jax
import jax.numpy as jnp
from jax import lax
from jax.experimental import pallas as pl
from jax.experimental.pallas import tpu as pltpu
from jax.sharding import PartitionSpec as P

MOST_SENT = 32
TILE = 16
LANES = 128
VMEM, SMEM, HBM = (pl.BlockSpec(memory_space=m) for m in (pltpu.VMEM, pltpu.SMEM, pltpu.HBM))


def halo_of(sentences):
    peers = lax.axis_size("docs")
    up = [(i, i + 1) for i in range(peers - 1)]
    down = [(j, i) for i, j in up]
    before = lax.ppermute(sentences[-MOST_SENT:], "docs", up)
    after = lax.ppermute(sentences[:MOST_SENT], "docs", down)
    return before, after


def deal_kernel(cap, members, base_ref, owner_ref, shard_ref, anchor_ref, rows_ref, o_ref):
    half, lines, (n, feature) = o_ref.shape[0], owner_ref.shape[0], rows_ref.shape
    size = cap * feature // LANES
    owner, shard, anchor = owner_ref[...], shard_ref[...], anchor_ref[...]
    told = jnp.concatenate([owner, shard, anchor // LANES, anchor % LANES], axis=0)
    told = jnp.concatenate([told, jnp.zeros((TILE - 4 * lines, LANES), jnp.int32)], axis=0)
    told = told.astype(jnp.float32).astype(jnp.bfloat16)
    owner, shard = (jnp.concatenate([x[i : i + 1] for i in range(lines)], axis=1) for x in (owner, shard))
    label = lax.broadcasted_iota(jnp.int32, (members, n), 0)
    theirs = jnp.where(label == owner, 1.0, 0.0)
    sooner = lax.broadcasted_iota(jnp.int32, (n, n), 0) < lax.broadcasted_iota(jnp.int32, (n, n), 1)
    before = jnp.dot(
        theirs.astype(jnp.bfloat16), jnp.where(sooner, 1.0, 0.0).astype(jnp.bfloat16), preferred_element_type=jnp.float32
    )
    rank = jnp.sum(theirs * before, axis=0, keepdims=True).astype(jnp.int32)
    slot = lax.broadcasted_iota(jnp.int32, (half * cap, n), 0)
    for k, target in enumerate((owner, shard)[: o_ref.shape[1] // size]):
        place = (target - base_ref[0]) * cap + rank
        table = jnp.where(slot == place, 1.0, 0.0).astype(jnp.bfloat16)
        out = jnp.dot(table, rows_ref[...], preferred_element_type=jnp.float32).astype(jnp.bfloat16)
        for d in range(half):
            for t, r, c in tiles(cap, feature):
                o_ref[d, k * size + t : k * size + t + TILE] = out[d * cap + r : d * cap + r + TILE, c : c + LANES]
    for d in range(half):
        o_ref[d, o_ref.shape[1] - TILE :] = told


def tiles(rows, columns):
    every = [(r, c) for r in range(0, rows, TILE) for c in range(0, columns, LANES)]
    return [(i * TILE, r, c) for i, (r, c) in enumerate(every)]


def deal(images, owner, shard, anchor, first, members, cap, regions):
    n, feature = images.shape
    lines = lambda a: a.reshape(n // LANES, LANES)
    half = members // 2
    shape = (half, regions * cap * feature // LANES + TILE, LANES)
    return pl.pallas_call(
        functools.partial(deal_kernel, cap, members),
        in_specs=[SMEM] + [pl.BlockSpec()] * 4,
        out_specs=pl.BlockSpec(),
        out_shape=jax.ShapeDtypeStruct(shape, jnp.bfloat16),
        compiler_params=pltpu.CompilerParams(vmem_limit_bytes=60 * 1024 * 1024),
        cost_estimate=pl.CostEstimate(
            flops=2 * regions * half * cap * n * feature, bytes_accessed=2 * (n + regions * half * cap) * feature, transcendentals=0
        ),
        name="deal",
    )(first[None], lines(owner), lines(shard), lines(anchor), images)


def merge_kernel(low_ref, near_ref, far_ref, o_ref):
    cap, feature = o_ref.shape[1:]
    size = cap * feature // LANES
    s, half = pl.program_id(0), pl.num_programs(0) // 2
    is_near = (s < half) == (low_ref[0] == 1)

    def take(ref):
        for t, r, c in tiles(cap, feature):
            o_ref[0, r : r + TILE, c : c + LANES] = ref[0, size + t : size + t + TILE]

    pl.when(is_near)(lambda: take(near_ref))
    pl.when(jnp.logical_not(is_near))(lambda: take(far_ref))


def merge(near, far, low, cap, feature):
    half = near.shape[0]
    spec = pl.BlockSpec((1, *near.shape[1:]), lambda i: (i % half, 0, 0))
    return pl.pallas_call(
        merge_kernel,
        grid=(2 * half,),
        in_specs=[SMEM, spec, spec],
        out_specs=pl.BlockSpec((1, cap, feature), lambda i: (i, 0, 0)),
        out_shape=jax.ShapeDtypeStruct((2 * half, cap, feature), far.dtype),
        compiler_params=pltpu.CompilerParams(vmem_limit_bytes=8 * 1024 * 1024),
        cost_estimate=pl.CostEstimate(flops=0, bytes_accessed=8 * half * cap * feature, transcendentals=0),
        name="merge",
    )(low.astype(jnp.int32)[None], near, far)


def attend_kernel(temper, q_ref, doc_ref, k_ref, before_ref, after_ref, id_ref, id_before_ref, id_after_ref, o_ref, *scratch):
    doc = doc_ref[...]
    here = lambda: None
    parts = [(before_ref, id_before_ref, here), (after_ref, id_after_ref, here)]
    if scratch:
        rows, held, sems = scratch
        length, cap = held.shape[0] // sems.shape[0], o_ref.shape[0] // q_ref.shape[0]
        spans = [pl.ds(i * length, length) for i in range(sems.shape[0])]
        copies = [pltpu.make_async_copy(k_ref.at[x], held.at[x], sems.at[i]) for i, x in enumerate(spans)]
        for c in copies:
            c.start()
        for d in range(q_ref.shape[0]):
            for t, r, c in tiles(cap, rows.shape[1]):
                rows[d * cap + r : d * cap + r + TILE, c : c + LANES] = q_ref[d, t : t + TILE]
        q_ref = rows
        parts += [(held.at[x], id_ref.at[:, x], c.wait) for x, c in zip(spans, copies)]
    else:
        parts.append((k_ref, id_ref, here))
    q = q_ref[...]
    scores = []
    for rows, ids, ready in parts:
        ready()
        s = lax.dot_general(q, rows[...], (((1,), (1,)), ((), ())), preferred_element_type=jnp.float32) * temper
        scores.append(jnp.where(doc == ids[...], s, -1e30))
    peak = functools.reduce(jnp.maximum, [jnp.max(s, axis=1, keepdims=True) for s in scores])
    raised = [jnp.where(doc == ids[...], jnp.exp(s - peak), 0.0) for s, (_, ids, _) in zip(scores, parts)]
    total = sum(jnp.sum(r, axis=1, keepdims=True) for r in raised)
    total = jnp.where(total > 0.0, total, 1.0)
    o_ref[...] = sum(
        jnp.dot((r / total).astype(jnp.bfloat16), rows[...], preferred_element_type=jnp.float32)
        for r, (rows, _, _) in zip(raised, parts)
    ).astype(jnp.bfloat16)


def attend(queries, cap, docs, known):
    rows, (own, feature) = docs.shape[0], known[0].shape
    block = min(256, rows)
    whole = lambda a: pl.BlockSpec(a.shape, lambda i: (0, 0))
    tiled = queries.ndim == 3
    block, chunks = rows if tiled else block, 4
    queries_spec = pl.BlockSpec((block, feature), lambda i: (i, 0))
    if tiled:
        region = cap * feature // LANES
        queries_spec = pl.BlockSpec((block // cap, region, LANES), lambda i: (i, 0, 0))
    return pl.pallas_call(
        functools.partial(attend_kernel, feature**-0.5),
        grid=(rows // block,),
        in_specs=[
            queries_spec,
            pl.BlockSpec((block, 1), lambda i: (i, 0)),
            HBM if tiled else whole(known[0]),
            *[whole(a) for a in known[1:]],
        ],
        out_specs=pl.BlockSpec((block, feature), lambda i: (i, 0)),
        out_shape=jax.ShapeDtypeStruct((rows, feature), jnp.bfloat16),
        scratch_shapes=[
            pltpu.VMEM((block, feature), jnp.bfloat16),
            pltpu.VMEM((own, feature), jnp.bfloat16),
            pltpu.SemaphoreType.DMA((chunks,)),
        ]
        if tiled
        else [],
        compiler_params=pltpu.CompilerParams(vmem_limit_bytes=(59 if tiled else 40) * 1024 * 1024),
        cost_estimate=pl.CostEstimate(
            flops=4 * rows * own * feature, bytes_accessed=2 * (own + 2 * rows) * feature, transcendentals=rows * own
        ),
        name="attend",
    )(queries, docs, *known)


def every_device(row, arrived):
    peers, me = lax.axis_size("docs"), lax.axis_index("docs")
    if peers & (peers - 1):
        return lax.all_gather(row, "docs", axis=0, tiled=False), arrived
    step = max(1, peers // 4)
    apart = list(range(0, peers, step))
    rows = [lax.ppermute(row, "docs", [(i, i ^ a) for i in range(peers)]) if a else row for a in apart]
    held, arrived = lax.optimization_barrier((jnp.stack(rows), arrived))
    while step > 1:
        step //= 2
        held = jnp.concatenate([held, lax.ppermute(held, "docs", [(i, i ^ step) for i in range(peers)])], axis=0)
        apart = apart + [a ^ step for a in apart]
    source = jnp.array(apart, dtype=jnp.int32) ^ me
    pick = jnp.arange(peers, dtype=jnp.int32)[:, None] == source[None, :]
    return jnp.sum(jnp.where(pick[:, :, None], held[None], 0), axis=1), arrived


def copy_kernel(x_ref, o_ref):
    o_ref[...] = x_ref[...]


def write_out(x):
    rows, feature = x.shape
    block = min(128, rows)
    spec = pl.BlockSpec((block, feature), lambda i: (i, 0))
    return pl.pallas_call(
        copy_kernel,
        grid=(rows // block,),
        in_specs=[spec],
        out_specs=spec,
        out_shape=jax.ShapeDtypeStruct(x.shape, x.dtype),
        compiler_params=pltpu.CompilerParams(vmem_limit_bytes=8 * 1024 * 1024),
        cost_estimate=pl.CostEstimate(flops=0, bytes_accessed=4 * rows * feature, transcendentals=0),
        name="write_out",
    )(x)


def exchange(x):
    return lax.all_to_all(x, "docs", split_axis=0, concat_axis=0, tiled=True)


def place_kernel(comes_ref, x_ref, o_ref, zero, sem):
    zero[...] = jnp.zeros_like(zero)
    members = x_ref.shape[0]
    moves = [pltpu.make_async_copy(x_ref.at[jnp.maximum(comes_ref[d], 0)], o_ref.at[d], sem.at[d]) for d in range(members)]
    clears = [pltpu.make_async_copy(zero, o_ref.at[d], sem.at[d]) for d in range(members)]
    for d in range(members):
        pl.when(comes_ref[d] >= 0)(moves[d].start)
        pl.when(comes_ref[d] < 0)(clears[d].start)
    for d in range(members):
        pl.when(comes_ref[d] >= 0)(moves[d].wait)
        pl.when(comes_ref[d] < 0)(clears[d].wait)


def place(x, comes):
    members, cap, feature = x.shape
    if cap % TILE:
        row = jnp.arange(members * cap, dtype=jnp.int32)
        block = jnp.repeat(comes, cap)
        takes = ((block * cap + row % cap)[:, None] == row[None, :]) & (block >= 0)[:, None]
        table = takes.astype(jnp.bfloat16)
        rows = x.reshape(members * cap, feature)
        return jnp.dot(table, rows, preferred_element_type=jnp.float32).astype(jnp.bfloat16)
    return pl.pallas_call(
        place_kernel,
        in_specs=[SMEM, VMEM],
        out_specs=HBM,
        out_shape=jax.ShapeDtypeStruct(x.shape, x.dtype),
        scratch_shapes=[pltpu.VMEM((cap, feature), x.dtype), pltpu.SemaphoreType.DMA((members,))],
        compiler_params=pltpu.CompilerParams(vmem_limit_bytes=8 * 1024 * 1024),
        cost_estimate=pl.CostEstimate(flops=0, bytes_accessed=4 * x.size, transcendentals=0),
        name="place",
    )(comes, x).reshape(members * cap, feature)


def one_hot_dot(table, rows):
    return jnp.dot(table.astype(jnp.bfloat16), rows, preferred_element_type=jnp.float32).astype(jnp.bfloat16)


def shards(sentences, sent_doc, images, image_owner, anchor, loader_shard):
    members = lax.axis_size("docs")
    me = lax.axis_index("docs")
    own, feature = sentences.shape
    n = images.shape[0]
    cap = max(4, 2 * n // members)
    owner, shard = image_owner[:, 0], loader_shard[:, 0]
    spot = jnp.arange(n, dtype=jnp.int32)
    slots = jnp.arange(cap, dtype=jnp.int32)

    def by_shard(rows, owner, shard, start, count):
        earlier = (owner[:, None] == owner[None, :]) & (spot[None, :] < spot[:, None])
        rank = jnp.sum(earlier.astype(jnp.int32), axis=1)
        slot = jnp.arange(count * cap, dtype=jnp.int32)[:, None]
        return one_hot_dot(slot == ((shard - start) * cap + rank)[None, :], rows).reshape(count, cap, feature)

    ids = lax.dynamic_slice_in_dim(sent_doc, me * own, own)
    padded = jnp.pad(sent_doc, (MOST_SENT, MOST_SENT), constant_values=-1)
    id_before = lax.dynamic_slice_in_dim(padded, me * own, MOST_SENT)
    id_after = lax.dynamic_slice_in_dim(padded, me * own + own + MOST_SENT, MOST_SENT)
    before, after = halo_of(sentences)
    known = (sentences, before, after, ids[None], id_before[None], id_after[None])

    def slots_of(owner_of, shard_of, spot_of):
        mine = owner_of == me
        sooner = (spot[:, None] < spot[None, :]).astype(jnp.bfloat16)
        ranks = jnp.dot(mine.astype(jnp.bfloat16), sooner, preferred_element_type=jnp.float32).astype(jnp.int32)
        hit = mine[:, None, :] & (ranks[:, None, :] == slots[None, :, None])
        spots = jnp.sum(jnp.where(hit, spot_of[:, None, :] + 1, 0), axis=2).reshape(-1) - 1
        here = spots[:, None] == jnp.arange(own, dtype=jnp.int32)[None, :]
        docs = jnp.max(jnp.where(here, ids[None, :], -2), axis=1)
        goes = jnp.max(jnp.where(mine, shard_of + 1, 0), axis=1) - 1
        comes = jnp.max(jnp.where(shard_of == me, owner_of + 1, 0), axis=1) - 1
        return docs[:, None], goes, comes

    row = jnp.arange(members * cap, dtype=jnp.int32)

    def puts(goes):
        block, slot = jnp.repeat(goes, cap), jnp.arange(goes.shape[0] * cap, dtype=jnp.int32) % cap
        return (row[:, None] == (block * cap + slot)[None, :]) & (block >= 0)[None, :]

    whole_tiles = cap % TILE == 0 and feature % LANES == 0 and n % LANES == 0 and members % 2 == 0
    if whole_tiles and 4 * n <= TILE * LANES and members <= 256 and own % (4 * TILE) == 0 and own <= 256 * LANES:
        half = members // 2
        first = me // half * half
        halves = [list(range(half)), list(range(half, members))]
        across = [(i, (i + half) % members) for i in range(members)]

        def exchange_half(x):
            return lax.all_to_all(x, "docs", split_axis=0, concat_axis=0, tiled=True, axis_index_groups=halves)

        def told_by(x):
            told = x[:, -TILE:][:, : 4 * n // LANES].reshape(half, 4, n).astype(jnp.int32)
            return told[:, 0], told[:, 1], told[:, 2] * LANES + told[:, 3]

        codes = jnp.stack([owner, shard, anchor])
        mirrored, codes_mirror = lax.ppermute(images, "docs", across), lax.ppermute(codes, "docs", across)
        near = exchange_half(deal(images, owner, shard, anchor, first, members, cap, 2))
        near, mirrored, codes_mirror = lax.optimization_barrier((near, mirrored, codes_mirror))
        docs, goes, comes = slots_of(*told_by(near))
        aligned = attend(near, cap, docs, known)
        sent = one_hot_dot(puts(goes), aligned)

        far = exchange_half(deal(mirrored, *codes_mirror, first, members, cap, 2))
        sent, far = lax.optimization_barrier((sent, far))
        docs, goes, comes_far = slots_of(*told_by(far))
        aligned = attend(far, cap, docs, known)
        sent += jnp.dot(puts(goes).astype(jnp.bfloat16), aligned, preferred_element_type=jnp.float32)
        sent = sent.astype(jnp.bfloat16)
        low = first == 0
        comes = jnp.where(low, jnp.concatenate([comes, comes_far]), jnp.concatenate([comes_far, comes]))
        loaded_images = merge(near, far, low, cap, feature).reshape(members * cap, feature)
    else:
        packed = (owner * members + shard) * own + anchor
        every, queries = every_device(packed, exchange(by_shard(images, owner, owner, 0, members)))
        loaded_images = write_out(exchange(by_shard(images, owner, shard, 0, members)).reshape(members * cap, feature))
        docs, goes, comes = slots_of(every // (own * members), every // own % members, every % own)
        aligned = attend(queries.reshape(members * cap, feature), cap, docs, known)
        sent = one_hot_dot(puts(goes), aligned)
    loaded_text = place(exchange(sent.reshape(members, cap, feature)), comes)
    return loaded_images, loaded_text


def solution(mesh):
    split = P(("groups", "docs"))
    rows = P(("groups", "docs"), None)
    return jax.shard_map(
        shards,
        mesh=mesh,
        in_specs=(rows, P("groups"), rows, rows, split, rows),
        out_specs=(rows, rows),
        check_vma=False,
    )
```

```python
import functools

import jax
import jax.numpy as jnp
from jax import lax
from jax.experimental import pallas as pl
from jax.experimental.pallas import tpu as pltpu
from jax.sharding import PartitionSpec as P

MOST_SENT = 32
TILE = 16
LANES = 128
VMEM, SMEM, HBM = (pl.BlockSpec(memory_space=m) for m in (pltpu.VMEM, pltpu.SMEM, pltpu.HBM))


def halo_of(sentences):
    peers = lax.axis_size("docs")
    up = [(i, i + 1) for i in range(peers - 1)]
    down = [(j, i) for i, j in up]
    before = lax.ppermute(sentences[-MOST_SENT:], "docs", up)
    after = lax.ppermute(sentences[:MOST_SENT], "docs", down)
    return before, after


def deal_kernel(cap, members, base_ref, owner_ref, shard_ref, anchor_ref, rows_ref, o_ref):
    half, lines, (n, feature) = o_ref.shape[0], owner_ref.shape[0], rows_ref.shape
    size = cap * feature // LANES
    owner, shard, anchor = owner_ref[...], shard_ref[...], anchor_ref[...]
    told = jnp.concatenate([owner, shard, anchor // LANES, anchor % LANES], axis=0)
    told = jnp.concatenate([told, jnp.zeros((TILE - 4 * lines, LANES), jnp.int32)], axis=0)
    told = told.astype(jnp.float32).astype(jnp.bfloat16)
    owner, shard = (jnp.concatenate([x[i : i + 1] for i in range(lines)], axis=1) for x in (owner, shard))
    label = lax.broadcasted_iota(jnp.int32, (members, n), 0)
    theirs = jnp.where(label == owner, 1.0, 0.0)
    sooner = lax.broadcasted_iota(jnp.int32, (n, n), 0) < lax.broadcasted_iota(jnp.int32, (n, n), 1)
    before = jnp.dot(
        theirs.astype(jnp.bfloat16), jnp.where(sooner, 1.0, 0.0).astype(jnp.bfloat16), preferred_element_type=jnp.float32
    )
    rank = jnp.sum(theirs * before, axis=0, keepdims=True).astype(jnp.int32)
    slot = lax.broadcasted_iota(jnp.int32, (half * cap, n), 0)
    for k, target in enumerate((owner, shard)[: o_ref.shape[1] // size]):
        place = (target - base_ref[0]) * cap + rank
        table = jnp.where(slot == place, 1.0, 0.0).astype(jnp.bfloat16)
        out = jnp.dot(table, rows_ref[...], preferred_element_type=jnp.float32).astype(jnp.bfloat16)
        for d in range(half):
            for t, r, c in tiles(cap, feature):
                o_ref[d, k * size + t : k * size + t + TILE] = out[d * cap + r : d * cap + r + TILE, c : c + LANES]
    for d in range(half):
        o_ref[d, o_ref.shape[1] - TILE :] = told


def tiles(rows, columns):
    every = [(r, c) for r in range(0, rows, TILE) for c in range(0, columns, LANES)]
    return [(i * TILE, r, c) for i, (r, c) in enumerate(every)]


def deal(images, owner, shard, anchor, first, members, cap, regions):
    n, feature = images.shape
    lines = lambda a: a.reshape(n // LANES, LANES)
    half = members // 2
    shape = (half, regions * cap * feature // LANES + TILE, LANES)
    return pl.pallas_call(
        functools.partial(deal_kernel, cap, members),
        in_specs=[SMEM] + [pl.BlockSpec()] * 4,
        out_specs=pl.BlockSpec(),
        out_shape=jax.ShapeDtypeStruct(shape, jnp.bfloat16),
        compiler_params=pltpu.CompilerParams(vmem_limit_bytes=60 * 1024 * 1024),
        cost_estimate=pl.CostEstimate(
            flops=2 * regions * half * cap * n * feature, bytes_accessed=2 * (n + regions * half * cap) * feature, transcendentals=0
        ),
        name="deal",
    )(first[None], lines(owner), lines(shard), lines(anchor), images)


def merge_kernel(low_ref, near_ref, far_ref, o_ref):
    cap, feature = o_ref.shape[1:]
    size = cap * feature // LANES
    s, half = pl.program_id(0), pl.num_programs(0) // 2
    is_near = (s < half) == (low_ref[0] == 1)

    def take(ref):
        for t, r, c in tiles(cap, feature):
            o_ref[0, r : r + TILE, c : c + LANES] = ref[0, size + t : size + t + TILE]

    pl.when(is_near)(lambda: take(near_ref))
    pl.when(jnp.logical_not(is_near))(lambda: take(far_ref))


def merge(near, far, low, cap, feature):
    half = near.shape[0]
    spec = pl.BlockSpec((1, *near.shape[1:]), lambda i: (i % half, 0, 0))
    return pl.pallas_call(
        merge_kernel,
        grid=(2 * half,),
        in_specs=[SMEM, spec, spec],
        out_specs=pl.BlockSpec((1, cap, feature), lambda i: (i, 0, 0)),
        out_shape=jax.ShapeDtypeStruct((2 * half, cap, feature), far.dtype),
        compiler_params=pltpu.CompilerParams(vmem_limit_bytes=8 * 1024 * 1024),
        cost_estimate=pl.CostEstimate(flops=0, bytes_accessed=8 * half * cap * feature, transcendentals=0),
        name="merge",
    )(low.astype(jnp.int32)[None], near, far)


def attend_kernel(temper, q_ref, doc_ref, k_ref, before_ref, after_ref, id_ref, id_before_ref, id_after_ref, o_ref, *scratch):
    if scratch:
        rows, cap = scratch[0], o_ref.shape[0] // q_ref.shape[0]
        for d in range(q_ref.shape[0]):
            for t, r, c in tiles(cap, rows.shape[1]):
                rows[d * cap + r : d * cap + r + TILE, c : c + LANES] = q_ref[d, t : t + TILE]
        q_ref = rows
    q = q_ref[...]
    doc = doc_ref[...]
    parts = ((k_ref, id_ref), (before_ref, id_before_ref), (after_ref, id_after_ref))
    scores = []
    for rows, ids in parts:
        s = lax.dot_general(q, rows[...], (((1,), (1,)), ((), ())), preferred_element_type=jnp.float32) * temper
        scores.append(jnp.where(doc == ids[...], s, -1e30))
    peak = functools.reduce(jnp.maximum, [jnp.max(s, axis=1, keepdims=True) for s in scores])
    raised = [jnp.where(doc == ids[...], jnp.exp(s - peak), 0.0) for s, (_, ids) in zip(scores, parts)]
    total = sum(jnp.sum(r, axis=1, keepdims=True) for r in raised)
    total = jnp.where(total > 0.0, total, 1.0)
    o_ref[...] = sum(
        jnp.dot((r / total).astype(jnp.bfloat16), rows[...], preferred_element_type=jnp.float32)
        for r, (rows, _) in zip(raised, parts)
    ).astype(jnp.bfloat16)


def attend(queries, cap, docs, known):
    rows, (own, feature) = docs.shape[0], known[0].shape
    block = min(256, rows)
    whole = lambda a: pl.BlockSpec(a.shape, lambda i: (0, 0))
    tiled = queries.ndim == 3
    queries_spec = pl.BlockSpec((block, feature), lambda i: (i, 0))
    if tiled:
        region = cap * feature // LANES
        queries_spec = pl.BlockSpec((block // cap, region, LANES), lambda i: (i, 0, 0))
    return pl.pallas_call(
        functools.partial(attend_kernel, feature**-0.5),
        grid=(rows // block,),
        in_specs=[
            queries_spec,
            pl.BlockSpec((block, 1), lambda i: (i, 0)),
            *[whole(a) for a in known],
        ],
        out_specs=pl.BlockSpec((block, feature), lambda i: (i, 0)),
        out_shape=jax.ShapeDtypeStruct((rows, feature), jnp.bfloat16),
        scratch_shapes=[pltpu.VMEM((block, feature), jnp.bfloat16)] * tiled,
        compiler_params=pltpu.CompilerParams(vmem_limit_bytes=40 * 1024 * 1024),
        cost_estimate=pl.CostEstimate(
            flops=4 * rows * own * feature, bytes_accessed=2 * (own + 2 * rows) * feature, transcendentals=rows * own
        ),
        name="attend",
    )(queries, docs, *known)


def every_device(row, arrived):
    peers, me = lax.axis_size("docs"), lax.axis_index("docs")
    if peers & (peers - 1):
        return lax.all_gather(row, "docs", axis=0, tiled=False), arrived
    step = max(1, peers // 4)
    apart = list(range(0, peers, step))
    rows = [lax.ppermute(row, "docs", [(i, i ^ a) for i in range(peers)]) if a else row for a in apart]
    held, arrived = lax.optimization_barrier((jnp.stack(rows), arrived))
    while step > 1:
        step //= 2
        held = jnp.concatenate([held, lax.ppermute(held, "docs", [(i, i ^ step) for i in range(peers)])], axis=0)
        apart = apart + [a ^ step for a in apart]
    source = jnp.array(apart, dtype=jnp.int32) ^ me
    pick = jnp.arange(peers, dtype=jnp.int32)[:, None] == source[None, :]
    return jnp.sum(jnp.where(pick[:, :, None], held[None], 0), axis=1), arrived


def copy_kernel(x_ref, o_ref):
    o_ref[...] = x_ref[...]


def write_out(x):
    rows, feature = x.shape
    block = min(128, rows)
    spec = pl.BlockSpec((block, feature), lambda i: (i, 0))
    return pl.pallas_call(
        copy_kernel,
        grid=(rows // block,),
        in_specs=[spec],
        out_specs=spec,
        out_shape=jax.ShapeDtypeStruct(x.shape, x.dtype),
        compiler_params=pltpu.CompilerParams(vmem_limit_bytes=8 * 1024 * 1024),
        cost_estimate=pl.CostEstimate(flops=0, bytes_accessed=4 * rows * feature, transcendentals=0),
        name="write_out",
    )(x)


def exchange(x):
    return lax.all_to_all(x, "docs", split_axis=0, concat_axis=0, tiled=True)


def place_kernel(comes_ref, x_ref, o_ref, zero, sem):
    zero[...] = jnp.zeros_like(zero)
    members = x_ref.shape[0]
    moves = [pltpu.make_async_copy(x_ref.at[jnp.maximum(comes_ref[d], 0)], o_ref.at[d], sem.at[d]) for d in range(members)]
    clears = [pltpu.make_async_copy(zero, o_ref.at[d], sem.at[d]) for d in range(members)]
    for d in range(members):
        pl.when(comes_ref[d] >= 0)(moves[d].start)
        pl.when(comes_ref[d] < 0)(clears[d].start)
    for d in range(members):
        pl.when(comes_ref[d] >= 0)(moves[d].wait)
        pl.when(comes_ref[d] < 0)(clears[d].wait)


def place(x, comes):
    members, cap, feature = x.shape
    if cap % TILE:
        row = jnp.arange(members * cap, dtype=jnp.int32)
        block = jnp.repeat(comes, cap)
        takes = ((block * cap + row % cap)[:, None] == row[None, :]) & (block >= 0)[:, None]
        table = takes.astype(jnp.bfloat16)
        rows = x.reshape(members * cap, feature)
        return jnp.dot(table, rows, preferred_element_type=jnp.float32).astype(jnp.bfloat16)
    return pl.pallas_call(
        place_kernel,
        in_specs=[SMEM, VMEM],
        out_specs=HBM,
        out_shape=jax.ShapeDtypeStruct(x.shape, x.dtype),
        scratch_shapes=[pltpu.VMEM((cap, feature), x.dtype), pltpu.SemaphoreType.DMA((members,))],
        compiler_params=pltpu.CompilerParams(vmem_limit_bytes=8 * 1024 * 1024),
        cost_estimate=pl.CostEstimate(flops=0, bytes_accessed=4 * x.size, transcendentals=0),
        name="place",
    )(comes, x).reshape(members * cap, feature)


def one_hot_dot(table, rows):
    return jnp.dot(table.astype(jnp.bfloat16), rows, preferred_element_type=jnp.float32).astype(jnp.bfloat16)


def shards(sentences, sent_doc, images, image_owner, anchor, loader_shard):
    members = lax.axis_size("docs")
    me = lax.axis_index("docs")
    own, feature = sentences.shape
    n = images.shape[0]
    cap = max(4, 2 * n // members)
    owner, shard = image_owner[:, 0], loader_shard[:, 0]
    spot = jnp.arange(n, dtype=jnp.int32)
    slots = jnp.arange(cap, dtype=jnp.int32)

    def by_shard(rows, owner, shard, start, count):
        earlier = (owner[:, None] == owner[None, :]) & (spot[None, :] < spot[:, None])
        rank = jnp.sum(earlier.astype(jnp.int32), axis=1)
        slot = jnp.arange(count * cap, dtype=jnp.int32)[:, None]
        return one_hot_dot(slot == ((shard - start) * cap + rank)[None, :], rows).reshape(count, cap, feature)

    ids = lax.dynamic_slice_in_dim(sent_doc, me * own, own)
    padded = jnp.pad(sent_doc, (MOST_SENT, MOST_SENT), constant_values=-1)
    id_before = lax.dynamic_slice_in_dim(padded, me * own, MOST_SENT)
    id_after = lax.dynamic_slice_in_dim(padded, me * own + own + MOST_SENT, MOST_SENT)
    before, after = halo_of(sentences)
    known = (sentences, before, after, ids[None], id_before[None], id_after[None])

    def slots_of(owner_of, shard_of, spot_of):
        mine = owner_of == me
        sooner = (spot[:, None] < spot[None, :]).astype(jnp.bfloat16)
        ranks = jnp.dot(mine.astype(jnp.bfloat16), sooner, preferred_element_type=jnp.float32).astype(jnp.int32)
        hit = mine[:, None, :] & (ranks[:, None, :] == slots[None, :, None])
        spots = jnp.sum(jnp.where(hit, spot_of[:, None, :] + 1, 0), axis=2).reshape(-1) - 1
        here = spots[:, None] == jnp.arange(own, dtype=jnp.int32)[None, :]
        docs = jnp.max(jnp.where(here, ids[None, :], -2), axis=1)
        goes = jnp.max(jnp.where(mine, shard_of + 1, 0), axis=1) - 1
        comes = jnp.max(jnp.where(shard_of == me, owner_of + 1, 0), axis=1) - 1
        return docs[:, None], goes, comes

    row = jnp.arange(members * cap, dtype=jnp.int32)

    def puts(goes):
        block, slot = jnp.repeat(goes, cap), jnp.arange(goes.shape[0] * cap, dtype=jnp.int32) % cap
        return (row[:, None] == (block * cap + slot)[None, :]) & (block >= 0)[None, :]

    whole_tiles = cap % TILE == 0 and feature % LANES == 0 and n % LANES == 0 and members % 2 == 0
    if whole_tiles and 4 * n <= TILE * LANES and members <= 256 and own <= 256 * LANES:
        half = members // 2
        first = me // half * half
        halves = [list(range(half)), list(range(half, members))]
        across = [(i, (i + half) % members) for i in range(members)]

        def exchange_half(x):
            return lax.all_to_all(x, "docs", split_axis=0, concat_axis=0, tiled=True, axis_index_groups=halves)

        def told_by(x):
            told = x[:, -TILE:][:, : 4 * n // LANES].reshape(half, 4, n).astype(jnp.int32)
            return told[:, 0], told[:, 1], told[:, 2] * LANES + told[:, 3]

        codes = jnp.stack([owner, shard, anchor])
        mirrored, codes_mirror = lax.ppermute(images, "docs", across), lax.ppermute(codes, "docs", across)
        near = exchange_half(deal(images, owner, shard, anchor, first, members, cap, 2))
        far = deal(mirrored, *codes_mirror, first, members, cap, 2)
        near, far = lax.optimization_barrier((near, far))
        docs, goes, comes = slots_of(*told_by(near))
        aligned = attend(near, cap, docs, known)
        sent = one_hot_dot(puts(goes), aligned)

        far = exchange_half(far)
        sent, far = lax.optimization_barrier((sent, far))
        docs, goes, comes_far = slots_of(*told_by(far))
        aligned = attend(far, cap, docs, known)
        sent += jnp.dot(puts(goes).astype(jnp.bfloat16), aligned, preferred_element_type=jnp.float32)
        sent = sent.astype(jnp.bfloat16)
        low = first == 0
        comes = jnp.where(low, jnp.concatenate([comes, comes_far]), jnp.concatenate([comes_far, comes]))
        loaded_images = merge(near, far, low, cap, feature).reshape(members * cap, feature)
    else:
        packed = (owner * members + shard) * own + anchor
        every, queries = every_device(packed, exchange(by_shard(images, owner, owner, 0, members)))
        loaded_images = write_out(exchange(by_shard(images, owner, shard, 0, members)).reshape(members * cap, feature))
        docs, goes, comes = slots_of(every // (own * members), every // own % members, every % own)
        aligned = attend(queries.reshape(members * cap, feature), cap, docs, known)
        sent = one_hot_dot(puts(goes), aligned)
    loaded_text = place(exchange(sent.reshape(members, cap, feature)), comes)
    return loaded_images, loaded_text


def solution(mesh):
    split = P(("groups", "docs"))
    rows = P(("groups", "docs"), None)
    return jax.shard_map(
        shards,
        mesh=mesh,
        in_specs=(rows, P("groups"), rows, rows, split, rows),
        out_specs=(rows, rows),
        check_vma=False,
    )
```

```python
import functools

import jax
import jax.numpy as jnp
from jax import lax
from jax.experimental import pallas as pl
from jax.experimental.pallas import tpu as pltpu
from jax.sharding import PartitionSpec as P

MOST_SENT = 32
TILE = 16
LANES = 128
VMEM, SMEM, HBM = (pl.BlockSpec(memory_space=m) for m in (pltpu.VMEM, pltpu.SMEM, pltpu.HBM))


def halo_of(sentences):
    peers = lax.axis_size("docs")
    up = [(i, i + 1) for i in range(peers - 1)]
    down = [(j, i) for i, j in up]
    before = lax.ppermute(sentences[-MOST_SENT:], "docs", up)
    after = lax.ppermute(sentences[:MOST_SENT], "docs", down)
    return before, after


def deal_kernel(cap, owner_ref, shard_ref, anchor_ref, rows_ref, o_ref, rows, made, rows_sem, made_sem):
    members, parts = o_ref.shape[0], made_sem.shape[0]
    lines, (n, feature) = owner_ref.shape[0], rows_ref.shape
    coming = pltpu.make_async_copy(rows_ref, rows, rows_sem)
    coming.start()
    owner, shard, anchor = owner_ref[...], shard_ref[...], anchor_ref[...]
    told = jnp.concatenate([owner, shard, anchor // LANES, anchor % LANES], axis=0)
    told = jnp.concatenate([told, jnp.zeros((TILE - 4 * lines, LANES), jnp.int32)], axis=0)
    told = told.astype(jnp.float32).astype(jnp.bfloat16)
    owner = jnp.concatenate([owner[i : i + 1] for i in range(lines)], axis=1)
    label = lax.broadcasted_iota(jnp.int32, (members, n), 0)
    theirs = jnp.where(label == owner, 1.0, 0.0)
    sooner = lax.broadcasted_iota(jnp.int32, (n, n), 0) < lax.broadcasted_iota(jnp.int32, (n, n), 1)
    before = jnp.dot(
        theirs.astype(jnp.bfloat16), jnp.where(sooner, 1.0, 0.0).astype(jnp.bfloat16), preferred_element_type=jnp.float32
    )
    rank = jnp.sum(theirs * before, axis=0, keepdims=True).astype(jnp.int32)
    place = owner * cap + rank
    each = members // parts
    slot = lax.broadcasted_iota(jnp.int32, (each * cap, n), 0)
    coming.wait()
    leaving = []
    for p in range(parts):
        table = jnp.where(slot + p * each * cap == place, 1.0, 0.0).astype(jnp.bfloat16)
        out = jnp.dot(table, rows[...], preferred_element_type=jnp.float32).astype(jnp.bfloat16)
        for d in range(each):
            for t, r, c in tiles(cap, feature):
                made[p * each + d, t : t + TILE] = out[d * cap + r : d * cap + r + TILE, c : c + LANES]
            made[p * each + d, cap * feature // LANES :] = told
        part = pl.ds(p * each, each)
        leaving.append(pltpu.make_async_copy(made.at[part], o_ref.at[part], made_sem.at[p]))
        leaving[p].start()
    for copy in leaving:
        copy.wait()


def tiles(rows, columns):
    every = [(r, c) for r in range(0, rows, TILE) for c in range(0, columns, LANES)]
    return [(i * TILE, r, c) for i, (r, c) in enumerate(every)]


def deal(images, owner, shard, anchor, members, cap):
    n, feature = images.shape
    lines = lambda a: a.reshape(n // LANES, LANES)
    shape = (members, cap * feature // LANES + TILE, LANES)
    return pl.pallas_call(
        functools.partial(deal_kernel, cap),
        in_specs=[VMEM] * 3 + [HBM],
        out_specs=HBM,
        out_shape=jax.ShapeDtypeStruct(shape, jnp.bfloat16),
        scratch_shapes=[
            pltpu.VMEM((n, feature), jnp.bfloat16),
            pltpu.VMEM(shape, jnp.bfloat16),
            pltpu.SemaphoreType.DMA,
            pltpu.SemaphoreType.DMA((4 if members % 4 == 0 else 1,)),
        ],
        compiler_params=pltpu.CompilerParams(vmem_limit_bytes=60 * 1024 * 1024),
        cost_estimate=pl.CostEstimate(
            flops=2 * members * cap * n * feature, bytes_accessed=2 * (n + members * cap) * feature, transcendentals=0
        ),
        name="deal",
    )(lines(owner), lines(shard), lines(anchor), images)


def attend_kernel(temper, q_ref, doc_ref, k_ref, before_ref, after_ref, id_ref, id_before_ref, id_after_ref, o_ref, *scratch):
    if scratch:
        rows, cap = scratch[0], o_ref.shape[0] // q_ref.shape[0]
        for d in range(q_ref.shape[0]):
            for t, r, c in tiles(cap, rows.shape[1]):
                rows[d * cap + r : d * cap + r + TILE, c : c + LANES] = q_ref[d, t : t + TILE]
        q_ref = rows
    q = q_ref[...]
    doc = doc_ref[...]
    parts = ((k_ref, id_ref), (before_ref, id_before_ref), (after_ref, id_after_ref))
    scores = []
    for rows, ids in parts:
        s = lax.dot_general(q, rows[...], (((1,), (1,)), ((), ())), preferred_element_type=jnp.float32) * temper
        scores.append(jnp.where(doc == ids[...], s, -1e30))
    peak = functools.reduce(jnp.maximum, [jnp.max(s, axis=1, keepdims=True) for s in scores])
    raised = [jnp.where(doc == ids[...], jnp.exp(s - peak), 0.0) for s, (_, ids) in zip(scores, parts)]
    total = sum(jnp.sum(r, axis=1, keepdims=True) for r in raised)
    total = jnp.where(total > 0.0, total, 1.0)
    o_ref[...] = sum(
        jnp.dot((r / total).astype(jnp.bfloat16), rows[...], preferred_element_type=jnp.float32)
        for r, (rows, _) in zip(raised, parts)
    ).astype(jnp.bfloat16)


def attend(queries, docs, sentences, before, after, ids, id_before, id_after):
    rows, (own, feature) = docs.shape[0], sentences.shape
    block = min(256, rows)
    whole = lambda a: pl.BlockSpec(a.shape, lambda i: (0, 0))
    fixed = (sentences, before, after, ids, id_before, id_after)
    tiled = queries.ndim == 3
    queries_spec = pl.BlockSpec((block, feature), lambda i: (i, 0))
    if tiled:
        buckets = block * queries.shape[0] // rows
        queries_spec = pl.BlockSpec((buckets, *queries.shape[1:]), lambda i: (i, 0, 0))
    return pl.pallas_call(
        functools.partial(attend_kernel, feature**-0.5),
        grid=(rows // block,),
        in_specs=[
            queries_spec,
            pl.BlockSpec((block, 1), lambda i: (i, 0)),
            *[whole(a) for a in fixed],
        ],
        out_specs=pl.BlockSpec((block, feature), lambda i: (i, 0)),
        out_shape=jax.ShapeDtypeStruct((rows, feature), jnp.bfloat16),
        scratch_shapes=[pltpu.VMEM((block, feature), jnp.bfloat16)] * tiled,
        compiler_params=pltpu.CompilerParams(vmem_limit_bytes=40 * 1024 * 1024),
        cost_estimate=pl.CostEstimate(
            flops=4 * rows * own * feature, bytes_accessed=2 * (own + 2 * rows) * feature, transcendentals=rows * own
        ),
        name="attend",
    )(queries, docs, *fixed)


def every_device(row, arrived):
    peers, me = lax.axis_size("docs"), lax.axis_index("docs")
    if peers & (peers - 1):
        return lax.all_gather(row, "docs", axis=0, tiled=False), arrived
    step = max(1, peers // 4)
    apart = list(range(0, peers, step))
    rows = [lax.ppermute(row, "docs", [(i, i ^ a) for i in range(peers)]) if a else row for a in apart]
    held, arrived = lax.optimization_barrier((jnp.stack(rows), arrived))
    while step > 1:
        step //= 2
        held = jnp.concatenate([held, lax.ppermute(held, "docs", [(i, i ^ step) for i in range(peers)])], axis=0)
        apart = apart + [a ^ step for a in apart]
    source = jnp.array(apart, dtype=jnp.int32) ^ me
    pick = jnp.arange(peers, dtype=jnp.int32)[:, None] == source[None, :]
    return jnp.sum(jnp.where(pick[:, :, None], held[None], 0), axis=1), arrived


def copy_kernel(x_ref, o_ref):
    o_ref[...] = x_ref[...]


def write_out(x):
    rows, feature = x.shape
    block = min(128, rows)
    spec = pl.BlockSpec((block, feature), lambda i: (i, 0))
    return pl.pallas_call(
        copy_kernel,
        grid=(rows // block,),
        in_specs=[spec],
        out_specs=spec,
        out_shape=jax.ShapeDtypeStruct(x.shape, x.dtype),
        compiler_params=pltpu.CompilerParams(vmem_limit_bytes=8 * 1024 * 1024),
        cost_estimate=pl.CostEstimate(flops=0, bytes_accessed=4 * rows * feature, transcendentals=0),
        name="write_out",
    )(x)


def exchange(x):
    return lax.all_to_all(x, "docs", split_axis=0, concat_axis=0, tiled=True)


def place_kernel(comes_ref, x_ref, o_ref, zero, sem):
    zero[...] = jnp.zeros_like(zero)
    members = x_ref.shape[0]
    moves = [pltpu.make_async_copy(x_ref.at[jnp.maximum(comes_ref[d], 0)], o_ref.at[d], sem.at[d]) for d in range(members)]
    clears = [pltpu.make_async_copy(zero, o_ref.at[d], sem.at[d]) for d in range(members)]
    for d in range(members):
        pl.when(comes_ref[d] >= 0)(moves[d].start)
        pl.when(comes_ref[d] < 0)(clears[d].start)
    for d in range(members):
        pl.when(comes_ref[d] >= 0)(moves[d].wait)
        pl.when(comes_ref[d] < 0)(clears[d].wait)


def place(x, comes):
    members, cap, feature = x.shape
    if cap % TILE:
        row = jnp.arange(members * cap, dtype=jnp.int32)
        block = jnp.repeat(comes, cap)
        takes = ((block * cap + row % cap)[:, None] == row[None, :]) & (block >= 0)[:, None]
        table = takes.astype(jnp.bfloat16)
        rows = x.reshape(members * cap, feature)
        return jnp.dot(table, rows, preferred_element_type=jnp.float32).astype(jnp.bfloat16)
    return pl.pallas_call(
        place_kernel,
        in_specs=[SMEM, VMEM],
        out_specs=HBM,
        out_shape=jax.ShapeDtypeStruct(x.shape, x.dtype),
        scratch_shapes=[pltpu.VMEM((cap, feature), x.dtype), pltpu.SemaphoreType.DMA((members,))],
        compiler_params=pltpu.CompilerParams(vmem_limit_bytes=8 * 1024 * 1024),
        cost_estimate=pl.CostEstimate(flops=0, bytes_accessed=4 * x.size, transcendentals=0),
        name="place",
    )(comes, x).reshape(members * cap, feature)


def shards(sentences, sent_doc, images, image_owner, anchor, loader_shard):
    members = lax.axis_size("docs")
    me = lax.axis_index("docs")
    own, feature = sentences.shape
    n = images.shape[0]
    cap = max(4, 2 * n // members)
    owner, shard = image_owner[:, 0], loader_shard[:, 0]

    spot = jnp.arange(n, dtype=jnp.int32)
    earlier = (owner[:, None] == owner[None, :]) & (spot[None, :] < spot[:, None])
    rank = jnp.sum(earlier.astype(jnp.int32), axis=1)
    slot = jnp.arange(members * cap, dtype=jnp.int32)[:, None]

    def buckets(targets):
        table = (slot == (targets * cap + rank)[None, :]).astype(jnp.bfloat16)
        out = jnp.dot(table, images, preferred_element_type=jnp.float32).astype(jnp.bfloat16)
        return out.reshape(members, cap, feature)

    whole_tiles = cap % TILE == 0 and feature % LANES == 0 and n % LANES == 0
    if whole_tiles and 4 * n <= TILE * LANES and members <= 256 and own <= 256 * LANES:
        queries = exchange(deal(images, owner, shard, anchor, members, cap))
        told = queries[:, cap * feature // LANES :][:, : 4 * n // LANES].reshape(members, 4, n).astype(jnp.int32)
        owner_of, shard_of, spot_of = told[:, 0], told[:, 1], told[:, 2] * LANES + told[:, 3]
    else:
        packed = (owner * members + shard) * own + anchor
        every, arrived = every_device(packed, exchange(buckets(owner)))
        queries = arrived.reshape(members * cap, feature)
        owner_of, shard_of, spot_of = every // (own * members), every // own % members, every % own
    loaded_images = write_out(exchange(buckets(shard)).reshape(members * cap, feature))
    before, after = halo_of(sentences)

    mine = owner_of == me
    sooner = (spot[:, None] < spot[None, :]).astype(jnp.bfloat16)
    ranks = jnp.dot(mine.astype(jnp.bfloat16), sooner, preferred_element_type=jnp.float32).astype(jnp.int32)
    slots = jnp.arange(cap, dtype=jnp.int32)
    hit = mine[:, None, :] & (ranks[:, None, :] == slots[None, :, None])
    spots = jnp.sum(jnp.where(hit, spot_of[:, None, :] + 1, 0), axis=2).reshape(members * cap) - 1
    ids = lax.dynamic_slice_in_dim(sent_doc, me * own, own)
    here = spots[:, None] == jnp.arange(own, dtype=jnp.int32)[None, :]
    docs = jnp.max(jnp.where(here, ids[None, :], -2), axis=1)
    padded = jnp.pad(sent_doc, (MOST_SENT, MOST_SENT), constant_values=-1)
    id_before = lax.dynamic_slice_in_dim(padded, me * own, MOST_SENT)
    id_after = lax.dynamic_slice_in_dim(padded, me * own + own + MOST_SENT, MOST_SENT)
    aligned = attend(queries, docs[:, None], sentences, before, after, ids[None], id_before[None], id_after[None])

    goes = jnp.max(jnp.where(mine, shard_of + 1, 0), axis=1) - 1
    comes = jnp.max(jnp.where(shard_of == me, owner_of + 1, 0), axis=1) - 1

    row = jnp.arange(members * cap, dtype=jnp.int32)
    puts = row[:, None] == (jnp.repeat(goes, cap) * cap + row % cap)[None, :]
    puts = (puts & (jnp.repeat(goes, cap) >= 0)[None, :]).astype(jnp.bfloat16)
    sent = jnp.dot(puts, aligned, preferred_element_type=jnp.float32).astype(jnp.bfloat16).reshape(members, cap, feature)
    loaded_text = place(exchange(sent), comes)
    return loaded_images, loaded_text


def solution(mesh):
    split = P(("groups", "docs"))
    rows = P(("groups", "docs"), None)
    return jax.shard_map(
        shards,
        mesh=mesh,
        in_specs=(rows, P("groups"), rows, rows, split, rows),
        out_specs=(rows, rows),
        check_vma=False,
    )
```

```python
import functools

import jax
import jax.numpy as jnp
from jax import lax
from jax.experimental import pallas as pl
from jax.experimental.pallas import tpu as pltpu
from jax.sharding import PartitionSpec as P

MOST_SENT = 32
TILE = 16
LANES = 128
VMEM, SMEM, HBM = (pl.BlockSpec(memory_space=m) for m in (pltpu.VMEM, pltpu.SMEM, pltpu.HBM))


def halo_of(sentences):
    peers = lax.axis_size("docs")
    up = [(i, i + 1) for i in range(peers - 1)]
    down = [(j, i) for i, j in up]
    before = lax.ppermute(sentences[-MOST_SENT:], "docs", up)
    after = lax.ppermute(sentences[:MOST_SENT], "docs", down)
    return before, after


def deal_kernel(cap, owner_ref, shard_ref, anchor_ref, rows_ref, o_ref, rows, made, rows_sem, made_sem):
    members, parts = o_ref.shape[0], made_sem.shape[0]
    lines, (n, feature) = owner_ref.shape[0], rows_ref.shape
    coming = pltpu.make_async_copy(rows_ref, rows, rows_sem)
    coming.start()
    owner, shard, anchor = owner_ref[...], shard_ref[...], anchor_ref[...]
    told = jnp.concatenate([owner, shard, anchor // LANES, anchor % LANES], axis=0)
    told = jnp.concatenate([told, jnp.zeros((TILE - 4 * lines, LANES), jnp.int32)], axis=0)
    told = told.astype(jnp.float32).astype(jnp.bfloat16)
    owner = jnp.concatenate([owner[i : i + 1] for i in range(lines)], axis=1)
    label = lax.broadcasted_iota(jnp.int32, (members, n), 0)
    theirs = jnp.where(label == owner, 1.0, 0.0)
    sooner = lax.broadcasted_iota(jnp.int32, (n, n), 0) < lax.broadcasted_iota(jnp.int32, (n, n), 1)
    before = jnp.dot(
        theirs.astype(jnp.bfloat16), jnp.where(sooner, 1.0, 0.0).astype(jnp.bfloat16), preferred_element_type=jnp.float32
    )
    rank = jnp.sum(theirs * before, axis=0, keepdims=True).astype(jnp.int32)
    place = owner * cap + rank
    each = members // parts
    slot = lax.broadcasted_iota(jnp.int32, (members * cap, n), 0)
    table = jnp.where(slot == place, 1.0, 0.0).astype(jnp.bfloat16)
    coming.wait()
    out = jnp.dot(table, rows[...], preferred_element_type=jnp.float32).astype(jnp.bfloat16)
    leaving = []
    for p in range(parts):
        for d in range(p * each, (p + 1) * each):
            for t, r, c in tiles(cap, feature):
                made[d, t : t + TILE] = out[d * cap + r : d * cap + r + TILE, c : c + LANES]
            made[d, cap * feature // LANES :] = told
        part = pl.ds(p * each, each)
        leaving.append(pltpu.make_async_copy(made.at[part], o_ref.at[part], made_sem.at[p]))
        leaving[p].start()
    for copy in leaving:
        copy.wait()


def tiles(rows, columns):
    every = [(r, c) for r in range(0, rows, TILE) for c in range(0, columns, LANES)]
    return [(i * TILE, r, c) for i, (r, c) in enumerate(every)]


def deal(images, owner, shard, anchor, members, cap):
    n, feature = images.shape
    lines = lambda a: a.reshape(n // LANES, LANES)
    shape = (members, cap * feature // LANES + TILE, LANES)
    return pl.pallas_call(
        functools.partial(deal_kernel, cap),
        in_specs=[VMEM] * 3 + [HBM],
        out_specs=HBM,
        out_shape=jax.ShapeDtypeStruct(shape, jnp.bfloat16),
        scratch_shapes=[
            pltpu.VMEM((n, feature), jnp.bfloat16),
            pltpu.VMEM(shape, jnp.bfloat16),
            pltpu.SemaphoreType.DMA,
            pltpu.SemaphoreType.DMA((4 if members % 4 == 0 else 1,)),
        ],
        compiler_params=pltpu.CompilerParams(vmem_limit_bytes=60 * 1024 * 1024),
        cost_estimate=pl.CostEstimate(
            flops=2 * members * cap * n * feature, bytes_accessed=2 * (n + members * cap) * feature, transcendentals=0
        ),
        name="deal",
    )(lines(owner), lines(shard), lines(anchor), images)


def attend_kernel(temper, q_ref, doc_ref, k_ref, before_ref, after_ref, id_ref, id_before_ref, id_after_ref, o_ref, *scratch):
    if scratch:
        rows, cap = scratch[0], o_ref.shape[0] // q_ref.shape[0]
        for d in range(q_ref.shape[0]):
            for t, r, c in tiles(cap, rows.shape[1]):
                rows[d * cap + r : d * cap + r + TILE, c : c + LANES] = q_ref[d, t : t + TILE]
        q_ref = rows
    q = q_ref[...]
    doc = doc_ref[...]
    parts = ((k_ref, id_ref), (before_ref, id_before_ref), (after_ref, id_after_ref))
    scores = []
    for rows, ids in parts:
        s = lax.dot_general(q, rows[...], (((1,), (1,)), ((), ())), preferred_element_type=jnp.float32) * temper
        scores.append(jnp.where(doc == ids[...], s, -1e30))
    peak = functools.reduce(jnp.maximum, [jnp.max(s, axis=1, keepdims=True) for s in scores])
    raised = [jnp.where(doc == ids[...], jnp.exp(s - peak), 0.0) for s, (_, ids) in zip(scores, parts)]
    total = sum(jnp.sum(r, axis=1, keepdims=True) for r in raised)
    total = jnp.where(total > 0.0, total, 1.0)
    o_ref[...] = sum(
        jnp.dot((r / total).astype(jnp.bfloat16), rows[...], preferred_element_type=jnp.float32)
        for r, (rows, _) in zip(raised, parts)
    ).astype(jnp.bfloat16)


def attend(queries, docs, sentences, before, after, ids, id_before, id_after):
    rows, (own, feature) = docs.shape[0], sentences.shape
    block = min(256, rows)
    whole = lambda a: pl.BlockSpec(a.shape, lambda i: (0, 0))
    fixed = (sentences, before, after, ids, id_before, id_after)
    tiled = queries.ndim == 3
    queries_spec = pl.BlockSpec((block, feature), lambda i: (i, 0))
    if tiled:
        buckets = block * queries.shape[0] // rows
        queries_spec = pl.BlockSpec((buckets, *queries.shape[1:]), lambda i: (i, 0, 0))
    return pl.pallas_call(
        functools.partial(attend_kernel, feature**-0.5),
        grid=(rows // block,),
        in_specs=[
            queries_spec,
            pl.BlockSpec((block, 1), lambda i: (i, 0)),
            *[whole(a) for a in fixed],
        ],
        out_specs=pl.BlockSpec((block, feature), lambda i: (i, 0)),
        out_shape=jax.ShapeDtypeStruct((rows, feature), jnp.bfloat16),
        scratch_shapes=[pltpu.VMEM((block, feature), jnp.bfloat16)] * tiled,
        compiler_params=pltpu.CompilerParams(vmem_limit_bytes=40 * 1024 * 1024),
        cost_estimate=pl.CostEstimate(
            flops=4 * rows * own * feature, bytes_accessed=2 * (own + 2 * rows) * feature, transcendentals=rows * own
        ),
        name="attend",
    )(queries, docs, *fixed)


def every_device(row, arrived):
    peers, me = lax.axis_size("docs"), lax.axis_index("docs")
    if peers & (peers - 1):
        return lax.all_gather(row, "docs", axis=0, tiled=False), arrived
    step = max(1, peers // 4)
    apart = list(range(0, peers, step))
    rows = [lax.ppermute(row, "docs", [(i, i ^ a) for i in range(peers)]) if a else row for a in apart]
    held, arrived = lax.optimization_barrier((jnp.stack(rows), arrived))
    while step > 1:
        step //= 2
        held = jnp.concatenate([held, lax.ppermute(held, "docs", [(i, i ^ step) for i in range(peers)])], axis=0)
        apart = apart + [a ^ step for a in apart]
    source = jnp.array(apart, dtype=jnp.int32) ^ me
    pick = jnp.arange(peers, dtype=jnp.int32)[:, None] == source[None, :]
    return jnp.sum(jnp.where(pick[:, :, None], held[None], 0), axis=1), arrived


def copy_kernel(x_ref, o_ref):
    o_ref[...] = x_ref[...]


def write_out(x):
    rows, feature = x.shape
    block = min(128, rows)
    spec = pl.BlockSpec((block, feature), lambda i: (i, 0))
    return pl.pallas_call(
        copy_kernel,
        grid=(rows // block,),
        in_specs=[spec],
        out_specs=spec,
        out_shape=jax.ShapeDtypeStruct(x.shape, x.dtype),
        compiler_params=pltpu.CompilerParams(vmem_limit_bytes=8 * 1024 * 1024),
        cost_estimate=pl.CostEstimate(flops=0, bytes_accessed=4 * rows * feature, transcendentals=0),
        name="write_out",
    )(x)


def exchange(x):
    return lax.all_to_all(x, "docs", split_axis=0, concat_axis=0, tiled=True)


def place_kernel(comes_ref, x_ref, o_ref, zero, sem):
    zero[...] = jnp.zeros_like(zero)
    members, rows = x_ref.shape[0], zero.shape[0]
    for d in range(members):
        for i in range(x_ref.shape[1] // rows):
            part = pl.ds(i * rows, rows)
            move = pltpu.make_async_copy(x_ref.at[jnp.maximum(comes_ref[d], 0), part], o_ref.at[d, part], sem.at[d, i])
            clear = pltpu.make_async_copy(zero, o_ref.at[d, part], sem.at[d, i])
            pl.when(comes_ref[d] >= 0)(move.start)
            pl.when(comes_ref[d] < 0)(clear.start)
    for d in range(members):
        for i in range(x_ref.shape[1] // rows):
            part = pl.ds(i * rows, rows)
            move = pltpu.make_async_copy(x_ref.at[jnp.maximum(comes_ref[d], 0), part], o_ref.at[d, part], sem.at[d, i])
            clear = pltpu.make_async_copy(zero, o_ref.at[d, part], sem.at[d, i])
            pl.when(comes_ref[d] >= 0)(move.wait)
            pl.when(comes_ref[d] < 0)(clear.wait)


def place(x, comes):
    members, cap, feature = x.shape
    if cap % TILE:
        row = jnp.arange(members * cap, dtype=jnp.int32)
        block = jnp.repeat(comes, cap)
        takes = ((block * cap + row % cap)[:, None] == row[None, :]) & (block >= 0)[:, None]
        table = takes.astype(jnp.bfloat16)
        rows = x.reshape(members * cap, feature)
        return jnp.dot(table, rows, preferred_element_type=jnp.float32).astype(jnp.bfloat16)
    return pl.pallas_call(
        place_kernel,
        in_specs=[SMEM, VMEM],
        out_specs=HBM,
        out_shape=jax.ShapeDtypeStruct(x.shape, x.dtype),
        scratch_shapes=[pltpu.VMEM((TILE, feature), x.dtype), pltpu.SemaphoreType.DMA((members, cap // TILE))],
        compiler_params=pltpu.CompilerParams(vmem_limit_bytes=8 * 1024 * 1024),
        cost_estimate=pl.CostEstimate(flops=0, bytes_accessed=4 * x.size, transcendentals=0),
        name="place",
    )(comes, x).reshape(members * cap, feature)


def shards(sentences, sent_doc, images, image_owner, anchor, loader_shard):
    members = lax.axis_size("docs")
    me = lax.axis_index("docs")
    own, feature = sentences.shape
    n = images.shape[0]
    cap = max(4, 2 * n // members)
    owner, shard = image_owner[:, 0], loader_shard[:, 0]

    spot = jnp.arange(n, dtype=jnp.int32)
    earlier = (owner[:, None] == owner[None, :]) & (spot[None, :] < spot[:, None])
    rank = jnp.sum(earlier.astype(jnp.int32), axis=1)
    slot = jnp.arange(members * cap, dtype=jnp.int32)[:, None]

    def buckets(targets):
        table = (slot == (targets * cap + rank)[None, :]).astype(jnp.bfloat16)
        out = jnp.dot(table, images, preferred_element_type=jnp.float32).astype(jnp.bfloat16)
        return out.reshape(members, cap, feature)

    whole_tiles = cap % TILE == 0 and feature % LANES == 0 and n % LANES == 0
    if whole_tiles and 4 * n <= TILE * LANES and members <= 256 and own <= 256 * LANES:
        queries = exchange(deal(images, owner, shard, anchor, members, cap))
        told = queries[:, cap * feature // LANES :][:, : 4 * n // LANES].reshape(members, 4, n).astype(jnp.int32)
        owner_of, shard_of, spot_of = told[:, 0], told[:, 1], told[:, 2] * LANES + told[:, 3]
    else:
        packed = (owner * members + shard) * own + anchor
        every, arrived = every_device(packed, exchange(buckets(owner)))
        queries = arrived.reshape(members * cap, feature)
        owner_of, shard_of, spot_of = every // (own * members), every // own % members, every % own
    loaded_images = write_out(exchange(buckets(shard)).reshape(members * cap, feature))
    before, after = halo_of(sentences)

    mine = owner_of == me
    sooner = (spot[:, None] < spot[None, :]).astype(jnp.bfloat16)
    ranks = jnp.dot(mine.astype(jnp.bfloat16), sooner, preferred_element_type=jnp.float32).astype(jnp.int32)
    slots = jnp.arange(cap, dtype=jnp.int32)
    hit = mine[:, None, :] & (ranks[:, None, :] == slots[None, :, None])
    spots = jnp.sum(jnp.where(hit, spot_of[:, None, :] + 1, 0), axis=2).reshape(members * cap) - 1
    ids = lax.dynamic_slice_in_dim(sent_doc, me * own, own)
    here = spots[:, None] == jnp.arange(own, dtype=jnp.int32)[None, :]
    docs = jnp.max(jnp.where(here, ids[None, :], -2), axis=1)
    padded = jnp.pad(sent_doc, (MOST_SENT, MOST_SENT), constant_values=-1)
    id_before = lax.dynamic_slice_in_dim(padded, me * own, MOST_SENT)
    id_after = lax.dynamic_slice_in_dim(padded, me * own + own + MOST_SENT, MOST_SENT)
    aligned = attend(queries, docs[:, None], sentences, before, after, ids[None], id_before[None], id_after[None])

    goes = jnp.max(jnp.where(mine, shard_of + 1, 0), axis=1) - 1
    comes = jnp.max(jnp.where(shard_of == me, owner_of + 1, 0), axis=1) - 1

    row = jnp.arange(members * cap, dtype=jnp.int32)
    puts = row[:, None] == (jnp.repeat(goes, cap) * cap + row % cap)[None, :]
    puts = (puts & (jnp.repeat(goes, cap) >= 0)[None, :]).astype(jnp.bfloat16)
    sent = jnp.dot(puts, aligned, preferred_element_type=jnp.float32).astype(jnp.bfloat16).reshape(members, cap, feature)
    loaded_text = place(exchange(sent), comes)
    return loaded_images, loaded_text


def solution(mesh):
    split = P(("groups", "docs"))
    rows = P(("groups", "docs"), None)
    return jax.shard_map(
        shards,
        mesh=mesh,
        in_specs=(rows, P("groups"), rows, rows, split, rows),
        out_specs=(rows, rows),
        check_vma=False,
    )
```

```python
import functools

import jax
import jax.numpy as jnp
from jax import lax
from jax.experimental import pallas as pl
from jax.experimental.pallas import tpu as pltpu
from jax.sharding import PartitionSpec as P

MOST_SENT = 32
TILE = 16
LANES = 128
VMEM, SMEM, HBM = (pl.BlockSpec(memory_space=m) for m in (pltpu.VMEM, pltpu.SMEM, pltpu.HBM))


def halo_of(sentences):
    peers = lax.axis_size("docs")
    up = [(i, i + 1) for i in range(peers - 1)]
    down = [(j, i) for i, j in up]
    before = lax.ppermute(sentences[-MOST_SENT:], "docs", up)
    after = lax.ppermute(sentences[:MOST_SENT], "docs", down)
    return before, after


def deal_kernel(cap, owner_ref, shard_ref, anchor_ref, rows_ref, o_ref):
    members = o_ref.shape[0]
    lines, n = owner_ref.shape[0], rows_ref.shape[0]
    owner, shard, anchor = owner_ref[...], shard_ref[...], anchor_ref[...]
    told = jnp.concatenate([owner, shard, anchor // LANES, anchor % LANES], axis=0)
    told = jnp.concatenate([told, jnp.zeros((TILE - 4 * lines, LANES), jnp.int32)], axis=0)
    told = told.astype(jnp.float32).astype(jnp.bfloat16)
    owner = jnp.concatenate([owner[i : i + 1] for i in range(lines)], axis=1)
    label = lax.broadcasted_iota(jnp.int32, (members, n), 0)
    theirs = jnp.where(label == owner, 1.0, 0.0)
    sooner = lax.broadcasted_iota(jnp.int32, (n, n), 0) < lax.broadcasted_iota(jnp.int32, (n, n), 1)
    before = jnp.dot(
        theirs.astype(jnp.bfloat16), jnp.where(sooner, 1.0, 0.0).astype(jnp.bfloat16), preferred_element_type=jnp.float32
    )
    rank = jnp.sum(theirs * before, axis=0, keepdims=True).astype(jnp.int32)
    slot = lax.broadcasted_iota(jnp.int32, (members * cap, n), 0)
    table = jnp.where(slot == owner * cap + rank, 1.0, 0.0).astype(jnp.bfloat16)
    out = jnp.dot(table, rows_ref[...], preferred_element_type=jnp.float32).astype(jnp.bfloat16)
    for d in range(members):
        for t, r, c in tiles(cap, out.shape[1]):
            o_ref[d, t : t + TILE] = out[d * cap + r : d * cap + r + TILE, c : c + LANES]
        o_ref[d, cap * out.shape[1] // LANES :] = told


def tiles(rows, columns):
    every = [(r, c) for r in range(0, rows, TILE) for c in range(0, columns, LANES)]
    return [(i * TILE, r, c) for i, (r, c) in enumerate(every)]


def deal(images, owner, shard, anchor, members, cap):
    n, feature = images.shape
    lines = lambda a: a.reshape(n // LANES, LANES)
    shape = (members, cap * feature // LANES + TILE, LANES)
    return pl.pallas_call(
        functools.partial(deal_kernel, cap),
        in_specs=[pl.BlockSpec()] * 4,
        out_specs=pl.BlockSpec(),
        out_shape=jax.ShapeDtypeStruct(shape, jnp.bfloat16),
        compiler_params=pltpu.CompilerParams(vmem_limit_bytes=60 * 1024 * 1024),
        cost_estimate=pl.CostEstimate(
            flops=2 * members * cap * n * feature, bytes_accessed=2 * (n + members * cap) * feature, transcendentals=0
        ),
        name="deal",
    )(lines(owner), lines(shard), lines(anchor), images)


def attend_kernel(temper, q_ref, doc_ref, k_ref, before_ref, after_ref, id_ref, id_before_ref, id_after_ref, o_ref, *scratch):
    if scratch:
        rows, cap = scratch[0], o_ref.shape[0] // q_ref.shape[0]
        for d in range(q_ref.shape[0]):
            for t, r, c in tiles(cap, rows.shape[1]):
                rows[d * cap + r : d * cap + r + TILE, c : c + LANES] = q_ref[d, t : t + TILE]
        q_ref = rows
    q = q_ref[...]
    doc = doc_ref[...]
    parts = ((k_ref, id_ref), (before_ref, id_before_ref), (after_ref, id_after_ref))
    scores = []
    for rows, ids in parts:
        s = lax.dot_general(q, rows[...], (((1,), (1,)), ((), ())), preferred_element_type=jnp.float32) * temper
        scores.append(jnp.where(doc == ids[...], s, -1e30))
    peak = functools.reduce(jnp.maximum, [jnp.max(s, axis=1, keepdims=True) for s in scores])
    raised = [jnp.where(doc == ids[...], jnp.exp(s - peak), 0.0) for s, (_, ids) in zip(scores, parts)]
    total = sum(jnp.sum(r, axis=1, keepdims=True) for r in raised)
    total = jnp.where(total > 0.0, total, 1.0)
    o_ref[...] = sum(
        jnp.dot((r / total).astype(jnp.bfloat16), rows[...], preferred_element_type=jnp.float32)
        for r, (rows, _) in zip(raised, parts)
    ).astype(jnp.bfloat16)


def attend(queries, docs, sentences, before, after, ids, id_before, id_after):
    rows, (own, feature) = docs.shape[0], sentences.shape
    block = min(256, rows)
    whole = lambda a: pl.BlockSpec(a.shape, lambda i: (0, 0))
    fixed = (sentences, before, after, ids, id_before, id_after)
    tiled = queries.ndim == 3
    queries_spec = pl.BlockSpec((block, feature), lambda i: (i, 0))
    if tiled:
        buckets = block * queries.shape[0] // rows
        queries_spec = pl.BlockSpec((buckets, *queries.shape[1:]), lambda i: (i, 0, 0))
    return pl.pallas_call(
        functools.partial(attend_kernel, feature**-0.5),
        grid=(rows // block,),
        in_specs=[
            queries_spec,
            pl.BlockSpec((block, 1), lambda i: (i, 0)),
            *[whole(a) for a in fixed],
        ],
        out_specs=pl.BlockSpec((block, feature), lambda i: (i, 0)),
        out_shape=jax.ShapeDtypeStruct((rows, feature), jnp.bfloat16),
        scratch_shapes=[pltpu.VMEM((block, feature), jnp.bfloat16)] * tiled,
        compiler_params=pltpu.CompilerParams(vmem_limit_bytes=40 * 1024 * 1024),
        cost_estimate=pl.CostEstimate(
            flops=4 * rows * own * feature, bytes_accessed=2 * (own + 2 * rows) * feature, transcendentals=rows * own
        ),
        name="attend",
    )(queries, docs, *fixed)


def every_device(row, arrived):
    peers, me = lax.axis_size("docs"), lax.axis_index("docs")
    if peers & (peers - 1):
        return lax.all_gather(row, "docs", axis=0, tiled=False), arrived
    step = max(1, peers // 4)
    apart = list(range(0, peers, step))
    rows = [lax.ppermute(row, "docs", [(i, i ^ a) for i in range(peers)]) if a else row for a in apart]
    held, arrived = lax.optimization_barrier((jnp.stack(rows), arrived))
    while step > 1:
        step //= 2
        held = jnp.concatenate([held, lax.ppermute(held, "docs", [(i, i ^ step) for i in range(peers)])], axis=0)
        apart = apart + [a ^ step for a in apart]
    source = jnp.array(apart, dtype=jnp.int32) ^ me
    pick = jnp.arange(peers, dtype=jnp.int32)[:, None] == source[None, :]
    return jnp.sum(jnp.where(pick[:, :, None], held[None], 0), axis=1), arrived


def copy_kernel(x_ref, o_ref):
    o_ref[...] = x_ref[...]


def write_out(x):
    rows, feature = x.shape
    block = min(128, rows)
    spec = pl.BlockSpec((block, feature), lambda i: (i, 0))
    return pl.pallas_call(
        copy_kernel,
        grid=(rows // block,),
        in_specs=[spec],
        out_specs=spec,
        out_shape=jax.ShapeDtypeStruct(x.shape, x.dtype),
        compiler_params=pltpu.CompilerParams(vmem_limit_bytes=8 * 1024 * 1024),
        cost_estimate=pl.CostEstimate(flops=0, bytes_accessed=4 * rows * feature, transcendentals=0),
        name="write_out",
    )(x)


def exchange(x):
    return lax.all_to_all(x, "docs", split_axis=0, concat_axis=0, tiled=True)


def place_kernel(comes_ref, x_ref, o_ref):
    each = o_ref.shape[0]
    for i in range(each):
        block = comes_ref[pl.program_id(0) * each + i]

        @pl.when(block >= 0)
        def _():
            o_ref[i] = x_ref[jnp.maximum(block, 0)]

        @pl.when(block < 0)
        def _():
            o_ref[i] = jnp.zeros_like(o_ref[i])


def place(x, comes):
    members, cap, feature = x.shape
    if cap % TILE:
        row = jnp.arange(members * cap, dtype=jnp.int32)
        block = jnp.repeat(comes, cap)
        takes = ((block * cap + row % cap)[:, None] == row[None, :]) & (block >= 0)[:, None]
        table = takes.astype(jnp.bfloat16)
        rows = x.reshape(members * cap, feature)
        return jnp.dot(table, rows, preferred_element_type=jnp.float32).astype(jnp.bfloat16)
    steps = 4 if members % 4 == 0 else 1
    return pl.pallas_call(
        place_kernel,
        grid=(steps,),
        in_specs=[SMEM, VMEM],
        out_specs=pl.BlockSpec((members // steps, cap, feature), lambda i: (i, 0, 0)),
        out_shape=jax.ShapeDtypeStruct(x.shape, x.dtype),
        compiler_params=pltpu.CompilerParams(vmem_limit_bytes=8 * 1024 * 1024),
        cost_estimate=pl.CostEstimate(flops=0, bytes_accessed=4 * x.size, transcendentals=0),
        name="place",
    )(comes, x).reshape(members * cap, feature)


def shards(sentences, sent_doc, images, image_owner, anchor, loader_shard):
    members = lax.axis_size("docs")
    me = lax.axis_index("docs")
    own, feature = sentences.shape
    n = images.shape[0]
    cap = max(4, 2 * n // members)
    owner, shard = image_owner[:, 0], loader_shard[:, 0]

    spot = jnp.arange(n, dtype=jnp.int32)
    earlier = (owner[:, None] == owner[None, :]) & (spot[None, :] < spot[:, None])
    rank = jnp.sum(earlier.astype(jnp.int32), axis=1)
    slot = jnp.arange(members * cap, dtype=jnp.int32)[:, None]

    def buckets(targets):
        table = (slot == (targets * cap + rank)[None, :]).astype(jnp.bfloat16)
        out = jnp.dot(table, images, preferred_element_type=jnp.float32).astype(jnp.bfloat16)
        return out.reshape(members, cap, feature)

    whole_tiles = cap % TILE == 0 and feature % LANES == 0 and n % LANES == 0
    if whole_tiles and 4 * n <= TILE * LANES and members <= 256 and own <= 256 * LANES:
        queries = exchange(deal(images, owner, shard, anchor, members, cap))
        told = queries[:, cap * feature // LANES :][:, : 4 * n // LANES].reshape(members, 4, n).astype(jnp.int32)
        owner_of, shard_of, spot_of = told[:, 0], told[:, 1], told[:, 2] * LANES + told[:, 3]
    else:
        packed = (owner * members + shard) * own + anchor
        every, arrived = every_device(packed, exchange(buckets(owner)))
        queries = arrived.reshape(members * cap, feature)
        owner_of, shard_of, spot_of = every // (own * members), every // own % members, every % own
    loaded_images = write_out(exchange(buckets(shard)).reshape(members * cap, feature))
    before, after = halo_of(sentences)

    mine = owner_of == me
    sooner = (spot[:, None] < spot[None, :]).astype(jnp.bfloat16)
    ranks = jnp.dot(mine.astype(jnp.bfloat16), sooner, preferred_element_type=jnp.float32).astype(jnp.int32)
    slots = jnp.arange(cap, dtype=jnp.int32)
    hit = mine[:, None, :] & (ranks[:, None, :] == slots[None, :, None])
    spots = jnp.sum(jnp.where(hit, spot_of[:, None, :] + 1, 0), axis=2).reshape(members * cap) - 1
    ids = lax.dynamic_slice_in_dim(sent_doc, me * own, own)
    here = spots[:, None] == jnp.arange(own, dtype=jnp.int32)[None, :]
    docs = jnp.max(jnp.where(here, ids[None, :], -2), axis=1)
    padded = jnp.pad(sent_doc, (MOST_SENT, MOST_SENT), constant_values=-1)
    id_before = lax.dynamic_slice_in_dim(padded, me * own, MOST_SENT)
    id_after = lax.dynamic_slice_in_dim(padded, me * own + own + MOST_SENT, MOST_SENT)
    aligned = attend(queries, docs[:, None], sentences, before, after, ids[None], id_before[None], id_after[None])

    goes = jnp.max(jnp.where(mine, shard_of + 1, 0), axis=1) - 1
    comes = jnp.max(jnp.where(shard_of == me, owner_of + 1, 0), axis=1) - 1

    row = jnp.arange(members * cap, dtype=jnp.int32)
    puts = row[:, None] == (jnp.repeat(goes, cap) * cap + row % cap)[None, :]
    puts = (puts & (jnp.repeat(goes, cap) >= 0)[None, :]).astype(jnp.bfloat16)
    sent = jnp.dot(puts, aligned, preferred_element_type=jnp.float32).astype(jnp.bfloat16).reshape(members, cap, feature)
    loaded_text = place(exchange(sent), comes)
    return loaded_images, loaded_text


def solution(mesh):
    split = P(("groups", "docs"))
    rows = P(("groups", "docs"), None)
    return jax.shard_map(
        shards,
        mesh=mesh,
        in_specs=(rows, P("groups"), rows, rows, split, rows),
        out_specs=(rows, rows),
        check_vma=False,
    )
```

```python
import functools

import jax
import jax.numpy as jnp
from jax import lax
from jax.experimental import pallas as pl
from jax.experimental.pallas import tpu as pltpu
from jax.sharding import PartitionSpec as P

MOST_SENT = 32
TILE = 16
LANES = 128
VMEM, SMEM, HBM = (pl.BlockSpec(memory_space=m) for m in (pltpu.VMEM, pltpu.SMEM, pltpu.HBM))


def halo_of(sentences):
    peers = lax.axis_size("docs")
    up = [(i, i + 1) for i in range(peers - 1)]
    down = [(j, i) for i, j in up]
    before = lax.ppermute(sentences[-MOST_SENT:], "docs", up)
    after = lax.ppermute(sentences[:MOST_SENT], "docs", down)
    return before, after


def deal_kernel(cap, owner_ref, shard_ref, anchor_ref, rows_ref, o_ref):
    members = o_ref.shape[0]
    lines, n = owner_ref.shape[0], rows_ref.shape[0]
    owner, shard, anchor = owner_ref[...], shard_ref[...], anchor_ref[...]
    told = jnp.concatenate([owner, shard, anchor // LANES, anchor % LANES], axis=0)
    told = jnp.concatenate([told, jnp.zeros((TILE - 4 * lines, LANES), jnp.int32)], axis=0)
    told = told.astype(jnp.float32).astype(jnp.bfloat16)
    owner = jnp.concatenate([owner[i : i + 1] for i in range(lines)], axis=1)
    label = lax.broadcasted_iota(jnp.int32, (members, n), 0)
    theirs = jnp.where(label == owner, 1.0, 0.0)
    sooner = lax.broadcasted_iota(jnp.int32, (n, n), 0) < lax.broadcasted_iota(jnp.int32, (n, n), 1)
    before = jnp.dot(
        theirs.astype(jnp.bfloat16), jnp.where(sooner, 1.0, 0.0).astype(jnp.bfloat16), preferred_element_type=jnp.float32
    )
    rank = jnp.sum(theirs * before, axis=0, keepdims=True).astype(jnp.int32)
    each = members // (4 if members % 4 == 0 else 1)
    slot = lax.broadcasted_iota(jnp.int32, (each * cap, n), 0)
    place = owner * cap + rank
    for start in range(0, members, each):
        table = jnp.where(slot + start * cap == place, 1.0, 0.0).astype(jnp.bfloat16)
        out = jnp.dot(table, rows_ref[...], preferred_element_type=jnp.float32).astype(jnp.bfloat16)
        for d in range(each):
            for t, r, c in tiles(cap, out.shape[1]):
                o_ref[start + d, t : t + TILE] = out[d * cap + r : d * cap + r + TILE, c : c + LANES]
            o_ref[start + d, cap * out.shape[1] // LANES :] = told


def tiles(rows, columns):
    every = [(r, c) for r in range(0, rows, TILE) for c in range(0, columns, LANES)]
    return [(i * TILE, r, c) for i, (r, c) in enumerate(every)]


def deal(images, owner, shard, anchor, members, cap):
    n, feature = images.shape
    lines = lambda a: a.reshape(n // LANES, LANES)
    shape = (members, cap * feature // LANES + TILE, LANES)
    return pl.pallas_call(
        functools.partial(deal_kernel, cap),
        in_specs=[pl.BlockSpec()] * 4,
        out_specs=pl.BlockSpec(),
        out_shape=jax.ShapeDtypeStruct(shape, jnp.bfloat16),
        compiler_params=pltpu.CompilerParams(vmem_limit_bytes=60 * 1024 * 1024),
        cost_estimate=pl.CostEstimate(
            flops=2 * members * cap * n * feature, bytes_accessed=2 * (n + members * cap) * feature, transcendentals=0
        ),
        name="deal",
    )(lines(owner), lines(shard), lines(anchor), images)


def attend_kernel(temper, q_ref, doc_ref, k_ref, before_ref, after_ref, id_ref, id_before_ref, id_after_ref, o_ref, *scratch):
    if scratch:
        rows, cap = scratch[0], o_ref.shape[0] // q_ref.shape[0]
        for d in range(q_ref.shape[0]):
            for t, r, c in tiles(cap, rows.shape[1]):
                rows[d * cap + r : d * cap + r + TILE, c : c + LANES] = q_ref[d, t : t + TILE]
        q_ref = rows
    q = q_ref[...]
    doc = doc_ref[...]
    parts = ((k_ref, id_ref), (before_ref, id_before_ref), (after_ref, id_after_ref))
    scores = []
    for rows, ids in parts:
        s = lax.dot_general(q, rows[...], (((1,), (1,)), ((), ())), preferred_element_type=jnp.float32) * temper
        scores.append(jnp.where(doc == ids[...], s, -1e30))
    peak = functools.reduce(jnp.maximum, [jnp.max(s, axis=1, keepdims=True) for s in scores])
    raised = [jnp.where(doc == ids[...], jnp.exp(s - peak), 0.0) for s, (_, ids) in zip(scores, parts)]
    total = sum(jnp.sum(r, axis=1, keepdims=True) for r in raised)
    total = jnp.where(total > 0.0, total, 1.0)
    o_ref[...] = sum(
        jnp.dot((r / total).astype(jnp.bfloat16), rows[...], preferred_element_type=jnp.float32)
        for r, (rows, _) in zip(raised, parts)
    ).astype(jnp.bfloat16)


def attend(queries, docs, sentences, before, after, ids, id_before, id_after):
    rows, (own, feature) = docs.shape[0], sentences.shape
    block = min(256, rows)
    whole = lambda a: pl.BlockSpec(a.shape, lambda i: (0, 0))
    fixed = (sentences, before, after, ids, id_before, id_after)
    tiled = queries.ndim == 3
    queries_spec = pl.BlockSpec((block, feature), lambda i: (i, 0))
    if tiled:
        buckets = block * queries.shape[0] // rows
        queries_spec = pl.BlockSpec((buckets, *queries.shape[1:]), lambda i: (i, 0, 0))
    return pl.pallas_call(
        functools.partial(attend_kernel, feature**-0.5),
        grid=(rows // block,),
        in_specs=[
            queries_spec,
            pl.BlockSpec((block, 1), lambda i: (i, 0)),
            *[whole(a) for a in fixed],
        ],
        out_specs=pl.BlockSpec((block, feature), lambda i: (i, 0)),
        out_shape=jax.ShapeDtypeStruct((rows, feature), jnp.bfloat16),
        scratch_shapes=[pltpu.VMEM((block, feature), jnp.bfloat16)] * tiled,
        compiler_params=pltpu.CompilerParams(vmem_limit_bytes=40 * 1024 * 1024),
        cost_estimate=pl.CostEstimate(
            flops=4 * rows * own * feature, bytes_accessed=2 * (own + 2 * rows) * feature, transcendentals=rows * own
        ),
        name="attend",
    )(queries, docs, *fixed)


def every_device(row, arrived):
    peers, me = lax.axis_size("docs"), lax.axis_index("docs")
    if peers & (peers - 1):
        return lax.all_gather(row, "docs", axis=0, tiled=False), arrived
    step = max(1, peers // 4)
    apart = list(range(0, peers, step))
    rows = [lax.ppermute(row, "docs", [(i, i ^ a) for i in range(peers)]) if a else row for a in apart]
    held, arrived = lax.optimization_barrier((jnp.stack(rows), arrived))
    while step > 1:
        step //= 2
        held = jnp.concatenate([held, lax.ppermute(held, "docs", [(i, i ^ step) for i in range(peers)])], axis=0)
        apart = apart + [a ^ step for a in apart]
    source = jnp.array(apart, dtype=jnp.int32) ^ me
    pick = jnp.arange(peers, dtype=jnp.int32)[:, None] == source[None, :]
    return jnp.sum(jnp.where(pick[:, :, None], held[None], 0), axis=1), arrived


def copy_kernel(x_ref, o_ref):
    o_ref[...] = x_ref[...]


def write_out(x):
    rows, feature = x.shape
    block = min(128, rows)
    spec = pl.BlockSpec((block, feature), lambda i: (i, 0))
    return pl.pallas_call(
        copy_kernel,
        grid=(rows // block,),
        in_specs=[spec],
        out_specs=spec,
        out_shape=jax.ShapeDtypeStruct(x.shape, x.dtype),
        compiler_params=pltpu.CompilerParams(vmem_limit_bytes=8 * 1024 * 1024),
        cost_estimate=pl.CostEstimate(flops=0, bytes_accessed=4 * rows * feature, transcendentals=0),
        name="write_out",
    )(x)


def exchange(x):
    return lax.all_to_all(x, "docs", split_axis=0, concat_axis=0, tiled=True)


def place_kernel(comes_ref, x_ref, o_ref, zero, sem):
    zero[...] = jnp.zeros_like(zero)
    members = x_ref.shape[0]
    moves = [pltpu.make_async_copy(x_ref.at[jnp.maximum(comes_ref[d], 0)], o_ref.at[d], sem.at[d]) for d in range(members)]
    clears = [pltpu.make_async_copy(zero, o_ref.at[d], sem.at[d]) for d in range(members)]
    for d in range(members):
        pl.when(comes_ref[d] >= 0)(moves[d].start)
        pl.when(comes_ref[d] < 0)(clears[d].start)
    for d in range(members):
        pl.when(comes_ref[d] >= 0)(moves[d].wait)
        pl.when(comes_ref[d] < 0)(clears[d].wait)


def place(x, comes):
    members, cap, feature = x.shape
    if cap % TILE:
        row = jnp.arange(members * cap, dtype=jnp.int32)
        block = jnp.repeat(comes, cap)
        takes = ((block * cap + row % cap)[:, None] == row[None, :]) & (block >= 0)[:, None]
        table = takes.astype(jnp.bfloat16)
        rows = x.reshape(members * cap, feature)
        return jnp.dot(table, rows, preferred_element_type=jnp.float32).astype(jnp.bfloat16)
    return pl.pallas_call(
        place_kernel,
        in_specs=[SMEM, VMEM],
        out_specs=HBM,
        out_shape=jax.ShapeDtypeStruct(x.shape, x.dtype),
        scratch_shapes=[pltpu.VMEM((cap, feature), x.dtype), pltpu.SemaphoreType.DMA((members,))],
        compiler_params=pltpu.CompilerParams(vmem_limit_bytes=8 * 1024 * 1024),
        cost_estimate=pl.CostEstimate(flops=0, bytes_accessed=4 * x.size, transcendentals=0),
        name="place",
    )(comes, x).reshape(members * cap, feature)


def shards(sentences, sent_doc, images, image_owner, anchor, loader_shard):
    members = lax.axis_size("docs")
    me = lax.axis_index("docs")
    own, feature = sentences.shape
    n = images.shape[0]
    cap = max(4, 2 * n // members)
    owner, shard = image_owner[:, 0], loader_shard[:, 0]

    spot = jnp.arange(n, dtype=jnp.int32)
    earlier = (owner[:, None] == owner[None, :]) & (spot[None, :] < spot[:, None])
    rank = jnp.sum(earlier.astype(jnp.int32), axis=1)
    slot = jnp.arange(members * cap, dtype=jnp.int32)[:, None]

    def buckets(targets):
        table = (slot == (targets * cap + rank)[None, :]).astype(jnp.bfloat16)
        out = jnp.dot(table, images, preferred_element_type=jnp.float32).astype(jnp.bfloat16)
        return out.reshape(members, cap, feature)

    whole_tiles = cap % TILE == 0 and feature % LANES == 0 and n % LANES == 0
    if whole_tiles and 4 * n <= TILE * LANES and members <= 256 and own <= 256 * LANES:
        queries = exchange(deal(images, owner, shard, anchor, members, cap))
        told = queries[:, cap * feature // LANES :][:, : 4 * n // LANES].reshape(members, 4, n).astype(jnp.int32)
        owner_of, shard_of, spot_of = told[:, 0], told[:, 1], told[:, 2] * LANES + told[:, 3]
    else:
        packed = (owner * members + shard) * own + anchor
        every, arrived = every_device(packed, exchange(buckets(owner)))
        queries = arrived.reshape(members * cap, feature)
        owner_of, shard_of, spot_of = every // (own * members), every // own % members, every % own
    loaded_images = write_out(exchange(buckets(shard)).reshape(members * cap, feature))
    before, after = halo_of(sentences)

    mine = owner_of == me
    sooner = (spot[:, None] < spot[None, :]).astype(jnp.bfloat16)
    ranks = jnp.dot(mine.astype(jnp.bfloat16), sooner, preferred_element_type=jnp.float32).astype(jnp.int32)
    slots = jnp.arange(cap, dtype=jnp.int32)
    hit = mine[:, None, :] & (ranks[:, None, :] == slots[None, :, None])
    spots = jnp.sum(jnp.where(hit, spot_of[:, None, :] + 1, 0), axis=2).reshape(members * cap) - 1
    ids = lax.dynamic_slice_in_dim(sent_doc, me * own, own)
    here = spots[:, None] == jnp.arange(own, dtype=jnp.int32)[None, :]
    docs = jnp.max(jnp.where(here, ids[None, :], -2), axis=1)
    padded = jnp.pad(sent_doc, (MOST_SENT, MOST_SENT), constant_values=-1)
    id_before = lax.dynamic_slice_in_dim(padded, me * own, MOST_SENT)
    id_after = lax.dynamic_slice_in_dim(padded, me * own + own + MOST_SENT, MOST_SENT)
    aligned = attend(queries, docs[:, None], sentences, before, after, ids[None], id_before[None], id_after[None])

    goes = jnp.max(jnp.where(mine, shard_of + 1, 0), axis=1) - 1
    comes = jnp.max(jnp.where(shard_of == me, owner_of + 1, 0), axis=1) - 1

    row = jnp.arange(members * cap, dtype=jnp.int32)
    puts = row[:, None] == (jnp.repeat(goes, cap) * cap + row % cap)[None, :]
    puts = (puts & (jnp.repeat(goes, cap) >= 0)[None, :]).astype(jnp.bfloat16)
    sent = jnp.dot(puts, aligned, preferred_element_type=jnp.float32).astype(jnp.bfloat16).reshape(members, cap, feature)
    loaded_text = place(exchange(sent), comes)
    return loaded_images, loaded_text


def solution(mesh):
    split = P(("groups", "docs"))
    rows = P(("groups", "docs"), None)
    return jax.shard_map(
        shards,
        mesh=mesh,
        in_specs=(rows, P("groups"), rows, rows, split, rows),
        out_specs=(rows, rows),
        check_vma=False,
    )
```
